32 devices in a mesh: dp: 2 (over x), ctx: 16 (over z, y, core).
Axes of the slice: x: 2, y: 2, z: 4, core: 2. Of those that a mesh axis runs over, the one named last changes fastest.
Arguments:
- tokens: bfloat16 [2, 2048, 1024], P('dp', 'ctx'), may hold values from -6 to 6
- segments: int32 [2, 2048], P('dp', 'ctx'), may hold values from 0 to 7
- cotangent: bfloat16 [2, 2048, 1024], P('dp', 'ctx'), may hold values from -6 to 6
- w_query: bfloat16 [1024, 1024], P(('dp', 'ctx')), may hold values from -0.1875 to 0.1875
- w_key: bfloat16 [1024, 1024], P(('dp', 'ctx')), may hold values from -0.1875 to 0.1875
- w_value: bfloat16 [1024, 1024], P(('dp', 'ctx')), may hold values from -0.1875 to 0.1875
- w_out: bfloat16 [1024, 1024], P(('dp', 'ctx')), may hold values from -0.1875 to 0.1875
- w_up: bfloat16 [1024, 4096], P(('dp', 'ctx')), may hold values from -0.1875 to 0.1875
- w_down: bfloat16 [4096, 1024], P(('dp', 'ctx')), may hold values from -0.09375 to 0.09375
- gain_attn_in: bfloat16 [1024], P(('dp', 'ctx')), may hold values from 0.5 to 1.5
- bias_attn_in: bfloat16 [1024], P(('dp', 'ctx')), may hold values from -1 to 1
- gain_attn_out: bfloat16 [1024], P(('dp', 'ctx')), may hold values from 0.5 to 1.5
- bias_attn_out: bfloat16 [1024], P(('dp', 'ctx')), may hold values from -1 to 1
- gain_mlp_in: bfloat16 [1024], P(('dp', 'ctx')), may hold values from 0.5 to 1.5
- bias_mlp_in: bfloat16 [1024], P(('dp', 'ctx')), may hold values from -1 to 1
- gain_mlp_out: bfloat16 [1024], P(('dp', 'ctx')), may hold values from 0.5 to 1.5
- bias_mlp_out: bfloat16 [1024], P(('dp', 'ctx')), may hold values from -1 to 1
Outputs:
- activations: bfloat16 [2, 2048, 1024], P('dp', 'ctx')
- input_grad: float32 [2, 2048, 1024], P('dp', 'ctx')
- grad_query: float32 [1024, 1024], P(('dp', 'ctx'))
- grad_key: float32 [1024, 1024], P(('dp', 'ctx'))
- grad_value: float32 [1024, 1024], P(('dp', 'ctx'))
- grad_out: float32 [1024, 1024], P(('dp', 'ctx'))
- grad_up: float32 [1024, 4096], P(('dp', 'ctx'))
- grad_down: float32 [4096, 1024], P(('dp', 'ctx'))
- grad_gain_attn_in: float32 [1024], P(('dp', 'ctx'))
- grad_bias_attn_in: float32 [1024], P(('dp', 'ctx'))
- grad_gain_attn_out: float32 [1024], P(('dp', 'ctx'))
- grad_bias_attn_out: float32 [1024], P(('dp', 'ctx'))
- grad_gain_mlp_in: float32 [1024], P(('dp', 'ctx'))
- grad_bias_mlp_in: float32 [1024], P(('dp', 'ctx'))
- grad_gain_mlp_out: float32 [1024], P(('dp', 'ctx'))
- grad_bias_mlp_out: float32 [1024], P(('dp', 'ctx'))
The draws below stay inside these ranges and needn't reach their ends.
All inputs are finite; a program needn't handle non-finite values.
Results may differ from the reference program's by a relative error of at most 0.018.
Values may be sent and summed in bfloat16 or wider, within the bound.
A program may use at most 384 MiB of HBM per device.

```python
import jax
import jax.numpy as jnp
from jax import lax

D = 1024
HEADS = 16
HD = 64
FF = 4096
TOK_DEV = 128
SEQS = 2
LENGTH = 2048
N_CTX = 16


def draw_segments(key, part):
    level_key, score_key, order_key = jax.random.split(jax.random.fold_in(key, 17), 3)
    doc_count = max(2, LENGTH // 256)
    levels = jax.random.randint(level_key, (SEQS, LENGTH // 64), 0, 4)
    weight_table = jnp.array([1, 2, 4, 8], dtype=jnp.int32)
    weights = jnp.repeat(weight_table[levels], 64, axis=1)[:, 1:]
    raw = jax.random.randint(score_key, (SEQS, LENGTH - 1), 0, 4096) * weights
    order_keys = jax.random.split(order_key, SEQS)
    ranks = jnp.stack([jax.random.permutation(order_keys[seq], LENGTH - 1) for seq in range(SEQS)]).astype(jnp.int32)
    scores = raw * 32768 + ranks
    chosen = lax.top_k(scores, doc_count - 1)[1] + 1
    flags = jnp.zeros((SEQS, LENGTH), jnp.int32)
    flags = jax.vmap(lambda row, idx: row.at[idx].set(1))(flags, chosen.astype(jnp.int32))
    ids_true = jnp.cumsum(flags, axis=1).astype(jnp.int32)
    half_rows = TOK_DEV // 2
    places = jnp.arange(LENGTH, dtype=jnp.int32)
    device_of = places // TOK_DEV
    offset_in = places % TOK_DEV
    true_at = jnp.where(offset_in < half_rows, device_of * half_rows + offset_in, (2 * N_CTX - 1 - device_of) * half_rows + offset_in - half_rows)
    return ids_true[:, true_at].astype(jnp.int32)


def level_of(rng, extent, cuts, least, largest):
    level = 1.0
    for axis_at, shards_of in cuts:
        draws = jax.random.uniform(jax.random.fold_in(jax.random.fold_in(rng, 6), axis_at), (shards_of,), jnp.float32, least / len(cuts), largest / len(cuts))
        level = level * jnp.repeat(jnp.exp(draws), extent[axis_at] // shards_of).reshape((-1,) + (1,) * (len(extent) - 1 - axis_at))
    return level


def noise(stream_key, dims, spread, limit, pieces=(), held_as=jnp.bfloat16):
    values = spread * jax.random.normal(stream_key, dims, jnp.float32)
    if pieces:
        values = values * level_of(stream_key, dims, pieces, -0.22, 0.18)
    return jnp.clip(values, -limit, limit).astype(held_as)


def setup_inputs(seed: int = 0) -> dict:
    arg_keys = jax.random.split(jax.random.key(seed), 18)
    return {
        "tokens": noise(arg_keys[0], (SEQS, LENGTH, D), 1.0, 6.0, ((0, 2), (1, 16))),
        "segments": draw_segments(jax.random.fold_in(arg_keys[17], 71), 0),
        "cotangent": noise(arg_keys[2], (SEQS, LENGTH, D), 1.0, 6.0, ((0, 2), (1, 16))),
        "w_query": noise(arg_keys[3], (D, D), D ** -0.5, 0.1875, ((0, 32),)),
        "w_key": noise(arg_keys[4], (D, D), D ** -0.5, 0.1875, ((0, 32),)),
        "w_value": noise(arg_keys[5], (D, D), D ** -0.5, 0.1875, ((0, 32),)),
        "w_out": noise(arg_keys[6], (D, D), D ** -0.5, 0.1875, ((0, 32),)),
        "w_up": noise(arg_keys[7], (D, FF), D ** -0.5, 0.1875, ((0, 32),)),
        "w_down": noise(arg_keys[8], (FF, D), FF ** -0.5, 0.09375, ((0, 32),)),
        "gain_attn_in": jnp.clip(1.0 + 0.1 * jax.random.normal(arg_keys[9], (D,), jnp.float32), 0.5, 1.5).astype(jnp.bfloat16),
        "bias_attn_in": noise(arg_keys[10], (D,), 0.2, 1.0, ((0, 32),)),
        "gain_attn_out": jnp.clip(1.0 + 0.1 * jax.random.normal(arg_keys[11], (D,), jnp.float32), 0.5, 1.5).astype(jnp.bfloat16),
        "bias_attn_out": noise(arg_keys[12], (D,), 0.2, 1.0, ((0, 32),)),
        "gain_mlp_in": jnp.clip(1.0 + 0.1 * jax.random.normal(arg_keys[13], (D,), jnp.float32), 0.5, 1.5).astype(jnp.bfloat16),
        "bias_mlp_in": noise(arg_keys[14], (D,), 0.2, 1.0, ((0, 32),)),
        "gain_mlp_out": jnp.clip(1.0 + 0.1 * jax.random.normal(arg_keys[15], (D,), jnp.float32), 0.5, 1.5).astype(jnp.bfloat16),
        "bias_mlp_out": noise(arg_keys[16], (D,), 0.2, 1.0, ((0, 32),)),
    }


@jax.custom_vjp
def low(v):
    return lax.optimization_barrier(v.astype(jnp.bfloat16)).astype(jnp.float32)

@jax.custom_vjp
def low_back(v):
    return v

def low_keep(v):
    return (low(v), None)

def low_pass(kept, grad):
    return (grad,)

def back_keep(v):
    return (v, None)

def back_low(kept, grad):
    return (low(grad),)
low.defvjp(low_keep, low_pass)
low_back.defvjp(back_keep, back_low)
norm_eps = 1e-05
masked_value = -1e+30

def layer_norm(value, gain, bias):
    row_mean = lax.optimization_barrier(jnp.mean(value, -1, keepdims=True))
    centred = value - row_mean
    scaled = centred * lax.rsqrt(lax.optimization_barrier(jnp.mean(centred * centred, -1, keepdims=True)) + norm_eps)
    return scaled * gain + bias

def project(left, right):
    return jnp.einsum('...i,ij->...j', left, right, precision=lax.Precision.HIGHEST)

def rotate(values, cos_t, sin_t):
    half_dim = values.shape[-1] // 2
    first = values[..., :half_dim]
    second = values[..., half_dim:]
    return jnp.concatenate([first * cos_t - second * sin_t, second * cos_t + first * sin_t], -1)

def rope_tables(offsets):
    freq = 10000.0 ** (-jnp.arange(HD // 2, dtype=jnp.float32) / (HD // 2))
    angle = offsets.astype(jnp.float32)[..., None] * freq
    return (jnp.cos(angle)[..., None, :], jnp.sin(angle)[..., None, :])

def attend_block(query_block, seg_block, pos_block, keys, values, seg_keys, pos_keys):
    scores = low_back(jnp.einsum('qhd,khd->hqk', query_block, keys, precision=lax.Precision.HIGHEST) * HD ** (-0.5))
    allowed = (seg_block[:, None] == seg_keys[None, :]) & (pos_keys[None, :] <= pos_block[:, None])
    scores = jnp.where(allowed[None], scores, masked_value)
    row_top = lax.optimization_barrier(jnp.max(scores, -1, keepdims=True))
    expd = jnp.exp(scores - row_top)
    attn_probs = low(expd / lax.optimization_barrier(jnp.sum(expd, -1, keepdims=True)))
    return jnp.einsum('hqk,khd->qhd', attn_probs, values, precision=lax.Precision.HIGHEST)

def attend(queries, keys, values, seg_ids):
    positions = jnp.arange(LENGTH, dtype=jnp.int32)
    query_rows = min(256, LENGTH)
    block_count = LENGTH // query_rows
    checked = jax.checkpoint(attend_block)

    def attend_one(parts):
        return checked(parts[0], parts[1], parts[2], keys, values, seg_ids, positions)
    result = lax.map(attend_one, (queries.reshape(block_count, query_rows, HEADS, HD), seg_ids.reshape(block_count, query_rows), positions.reshape(block_count, query_rows)))
    return result.reshape(LENGTH, HEADS, HD)

def make_forward(seg_true, cos_t, sin_t):

    def forward(inputs, query_w, key_w, value_w, out_w, up_w, down_w, gain_ai, bias_ai, gain_ao, bias_ao, gain_mi, bias_mi, gain_mo, bias_mo):
        attn_in = low(layer_norm(inputs, gain_ai, bias_ai))
        queries = low(rotate(low_back(project(attn_in, query_w)).reshape(SEQS, LENGTH, HEADS, HD), cos_t, sin_t))
        keys = low(rotate(low_back(project(attn_in, key_w)).reshape(SEQS, LENGTH, HEADS, HD), cos_t, sin_t))
        values = low(low_back(project(attn_in, value_w))).reshape(SEQS, LENGTH, HEADS, HD)
        attended = jnp.stack([attend(queries[seq], keys[seq], values[seq], seg_true[seq]) for seq in range(SEQS)])
        attended = low_back(low(attended.reshape(SEQS, LENGTH, D)))
        branch = low_back(project(attended, out_w))
        resid = inputs + layer_norm(branch, gain_ao, bias_ao)
        mlp_in = low(layer_norm(resid, gain_mi, bias_mi))
        hidden_pre = low_back(project(mlp_in, up_w))
        hidden = low(jax.nn.gelu(hidden_pre, approximate=True))
        mlp_out = low_back(project(hidden, down_w))
        return resid + layer_norm(mlp_out, gain_mo, bias_mo)
    return forward

def reference(tokens, segments, cotangent, w_query, w_key, w_value, w_out, w_up, w_down, gain_attn_in, bias_attn_in, gain_attn_out, bias_attn_out, gain_mlp_in, bias_mlp_in, gain_mlp_out, bias_mlp_out):
    half_rows = TOK_DEV // 2
    places = jnp.arange(LENGTH, dtype=jnp.int32)
    block_id = places // half_rows
    within = places % half_rows
    owner = jnp.where(block_id < N_CTX, block_id, 2 * N_CTX - 1 - block_id)
    stored_at = (owner * TOK_DEV + jnp.where(block_id < N_CTX, within, half_rows + within)).astype(jnp.int32)
    device_of = places // TOK_DEV
    offset_in = places % TOK_DEV
    true_at = jnp.where(offset_in < half_rows, device_of * half_rows + offset_in, (2 * N_CTX - 1 - device_of) * half_rows + offset_in - half_rows).astype(jnp.int32)
    seg_true = segments[:, stored_at]
    inputs = tokens[:, stored_at].astype(jnp.float32)
    upstream = cotangent[:, stored_at].astype(jnp.float32)
    starts = jnp.concatenate([jnp.ones((SEQS, 1), jnp.bool_), seg_true[:, 1:] != seg_true[:, :-1]], 1)
    doc_first = lax.cummax(jnp.where(starts, places[None, :], 0), axis=1)
    cos_t, sin_t = rope_tables(places[None, :] - doc_first)
    params = tuple((w.astype(jnp.float32) for w in (w_query, w_key, w_value, w_out, w_up, w_down, gain_attn_in, bias_attn_in, gain_attn_out, bias_attn_out, gain_mlp_in, bias_mlp_in, gain_mlp_out, bias_mlp_out)))
    forward = make_forward(seg_true, cos_t, sin_t)
    result, pullback = jax.vjp(forward, inputs, *params)
    grads = pullback(upstream)
    return (result[:, true_at].astype(jnp.bfloat16), grads[0][:, true_at], grads[1], grads[2], grads[3], grads[4], grads[5], grads[6], grads[7], grads[8], grads[9], grads[10], grads[11], grads[12], grads[13], grads[14])
```

```python
import math

import jax
import jax.numpy as jnp
from jax import lax
from jax.experimental import pallas as pl
from jax.experimental.pallas import tpu as pltpu
from jax.sharding import PartitionSpec as P

HEADS = 16
HD = 64


norm_eps = 1e-05
masked_value = -1e30


def layer_norm(value, gain, bias):
    row_mean = jnp.mean(value, -1, keepdims=True)
    centred = value - row_mean
    scaled = centred * lax.rsqrt(jnp.mean(centred * centred, -1, keepdims=True) + norm_eps)
    return scaled * gain + bias


def norm_back(value, gain, upstream):
    row_mean = jnp.mean(value, -1, keepdims=True)
    centred = value - row_mean
    inv_std = lax.rsqrt(jnp.mean(centred * centred, -1, keepdims=True) + norm_eps)
    normed = centred * inv_std
    d_normed = upstream * gain
    d_value = inv_std * (
        d_normed
        - jnp.mean(d_normed, -1, keepdims=True)
        - normed * jnp.mean(d_normed * normed, -1, keepdims=True)
    )
    return (d_value, jnp.sum(upstream * normed, 0), jnp.sum(upstream, 0))


def rope_tables(offsets, head_dim):
    freq = 10000.0 ** (-jnp.arange(head_dim // 2, dtype=jnp.float32) / (head_dim // 2))
    angle = offsets.astype(jnp.float32)[..., None] * freq
    return (jnp.cos(angle)[..., None, :], jnp.sin(angle)[..., None, :])


def rotate(values, cos_t, sin_t):
    half_dim = values.shape[-1] // 2
    first = values[..., :half_dim]
    second = values[..., half_dim:]
    return jnp.concatenate([first * cos_t - second * sin_t, second * cos_t + first * sin_t], -1)


def unrotate(grads, cos_t, sin_t):
    half_dim = grads.shape[-1] // 2
    first = grads[..., :half_dim]
    second = grads[..., half_dim:]
    return jnp.concatenate([first * cos_t + second * sin_t, second * cos_t - first * sin_t], -1)


def true_position(flat_index, row_count, ctx_size):
    device_of = flat_index // row_count
    offset_in = flat_index % row_count
    half_rows = row_count // 2
    return jnp.where(
        offset_in < half_rows,
        device_of * half_rows + offset_in,
        (2 * ctx_size - 1 - device_of) * half_rows + offset_in - half_rows,
    )


def split_blocks(array, block_rows):
    return array.reshape((array.shape[0] // block_rows, block_rows) + array.shape[1:])


def score_block(queries, keys, query_pos, query_seg, key_pos, key_seg):
    scores = jnp.einsum(
        "qhd,khd->hqk", queries, keys, preferred_element_type=jnp.float32
    ) * queries.shape[-1] ** (-0.5)
    allowed = (query_seg[:, None] == key_seg[None, :]) & (key_pos[None, :] <= query_pos[:, None])
    return (scores, allowed[None])


def grad_block(queries, d_attn, lse, delta, keys, values, query_pos, query_seg, key_pos, key_seg):
    scores, allowed = score_block(queries, keys, query_pos, query_seg, key_pos, key_seg)
    attn_probs = jnp.where(allowed, jnp.exp(scores - lse[:, :, None]), 0.0)
    d_probs = jnp.einsum("qhd,khd->hqk", d_attn, values, preferred_element_type=jnp.float32)
    d_scores = (attn_probs * (d_probs - delta[:, :, None])).astype(jnp.bfloat16)
    return (attn_probs, d_scores)


def key_terms(
    query_rows,
    dattn_rows,
    lse_rows,
    delta_rows,
    query_pos,
    query_seg,
    key_block,
    value_block,
    key_pos,
    key_seg,
):
    attn_probs, d_scores = grad_block(
        query_rows,
        dattn_rows,
        lse_rows,
        delta_rows,
        key_block,
        value_block,
        query_pos,
        query_seg,
        key_pos,
        key_seg,
    )
    d_keys = jnp.einsum(
        "hqk,qhd->khd", d_scores, query_rows, preferred_element_type=jnp.float32
    ) * query_rows.shape[-1] ** (-0.5)
    d_values = jnp.einsum(
        "hqk,qhd->khd",
        attn_probs.astype(jnp.bfloat16),
        dattn_rows,
        preferred_element_type=jnp.float32,
    )
    return (d_keys, d_values)


def on_device(
    tokens,
    segments,
    cotangent,
    w_query,
    w_key,
    w_value,
    w_out,
    w_up,
    w_down,
    gain_attn_in,
    bias_attn_in,
    gain_attn_out,
    bias_attn_out,
    gain_mlp_in,
    bias_mlp_in,
    gain_mlp_out,
    bias_mlp_out,
):
    whole = (
        lax.all_gather(w_query, ("dp", "ctx"), axis=0, tiled=True),
        lax.all_gather(w_key, ("dp", "ctx"), axis=0, tiled=True),
        lax.all_gather(w_value, ("dp", "ctx"), axis=0, tiled=True),
        lax.all_gather(w_out, ("dp", "ctx"), axis=0, tiled=True),
        lax.all_gather(w_up, ("dp", "ctx"), axis=0, tiled=True),
        lax.all_gather(w_down, ("dp", "ctx"), axis=0, tiled=True),
        lax.all_gather(gain_attn_in, ("dp", "ctx"), axis=0, tiled=True),
        lax.all_gather(bias_attn_in, ("dp", "ctx"), axis=0, tiled=True),
        lax.all_gather(gain_attn_out, ("dp", "ctx"), axis=0, tiled=True),
        lax.all_gather(bias_attn_out, ("dp", "ctx"), axis=0, tiled=True),
        lax.all_gather(gain_mlp_in, ("dp", "ctx"), axis=0, tiled=True),
        lax.all_gather(bias_mlp_in, ("dp", "ctx"), axis=0, tiled=True),
        lax.all_gather(gain_mlp_out, ("dp", "ctx"), axis=0, tiled=True),
        lax.all_gather(bias_mlp_out, ("dp", "ctx"), axis=0, tiled=True),
    )
    query_w, key_w, value_w, out_w, up_w, down_w = whole[:6]
    gain_ai, bias_ai, gain_ao, bias_ao, gain_mi, bias_mi, gain_mo, bias_mo = [
        entry.astype(jnp.float32) for entry in whole[6:]
    ]
    row_count = tokens.shape[1]
    model_width = tokens.shape[2]
    ctx_size = lax.axis_size("ctx")
    seq_length = row_count * ctx_size
    score_scale = HD ** (-0.5)
    seg_all = lax.all_gather(segments, "ctx", axis=1, tiled=True)[0]
    my_seg = segments[0]
    all_pos = true_position(jnp.arange(seq_length, dtype=jnp.int32), row_count, ctx_size)
    my_pos = true_position(
        lax.axis_index("ctx") * row_count + jnp.arange(row_count, dtype=jnp.int32),
        row_count,
        ctx_size,
    )
    doc_first = jnp.min(
        jnp.where(seg_all[None, :] == my_seg[:, None], all_pos[None, :], seq_length), axis=1
    )
    cos_t, sin_t = rope_tables(my_pos - doc_first, HD)
    inputs = tokens[0].astype(jnp.float32)
    attn_in = layer_norm(inputs, gain_ai, bias_ai).astype(jnp.bfloat16)
    query_pre = jnp.dot(attn_in, query_w, preferred_element_type=jnp.float32).reshape(
        row_count, HEADS, HD
    )
    key_pre = jnp.dot(attn_in, key_w, preferred_element_type=jnp.float32).reshape(
        row_count, HEADS, HD
    )
    queries = rotate(query_pre, cos_t, sin_t).astype(jnp.bfloat16)
    keys_rot = rotate(key_pre, cos_t, sin_t).astype(jnp.bfloat16)
    values_flat = jnp.dot(attn_in, value_w, preferred_element_type=jnp.float32).astype(jnp.bfloat16)
    values_heads = values_flat.reshape(row_count, HEADS, HD)
    keys_flat = keys_rot.reshape(row_count, model_width)
    start_state = (
        jnp.full((HEADS, row_count), masked_value, jnp.float32),
        jnp.zeros((HEADS, row_count), jnp.float32),
        jnp.zeros((row_count, HEADS, HD), jnp.float32),
    )
    key_rows = lax.all_gather(keys_flat, "ctx", axis=0, tiled=True)
    value_rows = lax.all_gather(values_flat, "ctx", axis=0, tiled=True)
    span = key_rows.shape[0]
    block_rows = math.gcd(span, 1024)
    key_pos = true_position(jnp.arange(span, dtype=jnp.int32), row_count, ctx_size)
    key_seg = seg_all

    def visit(state_now, parts):
        row_top, row_total, weighted = state_now
        key_block = parts[0].reshape(block_rows, HEADS, HD)
        value_block = parts[1].reshape(block_rows, HEADS, HD)
        scores, allowed = score_block(queries, key_block, my_pos, my_seg, parts[2], parts[3])
        top_new = jnp.maximum(row_top, jnp.max(jnp.where(allowed, scores, masked_value), -1))
        fade = jnp.exp(row_top - top_new)
        attn_probs = jnp.where(allowed, jnp.exp(scores - top_new[:, :, None]), 0.0)
        row_total = row_total * fade + jnp.sum(attn_probs, -1)
        weighted = weighted * fade.T[:, :, None] + jnp.einsum(
            "hqk,khd->qhd",
            attn_probs.astype(jnp.bfloat16),
            value_block,
            preferred_element_type=jnp.float32,
        )
        return ((top_new, row_total, weighted), None)

    blocks = (
        split_blocks(key_rows, block_rows),
        split_blocks(value_rows, block_rows),
        split_blocks(key_pos, block_rows),
        split_blocks(key_seg, block_rows),
    )
    row_top, row_total, weighted = lax.scan(visit, start_state, blocks)[0]
    lse = row_top + jnp.log(row_total)
    attn_f = weighted / row_total.T[:, :, None]
    attn_b = attn_f.reshape(row_count, model_width).astype(jnp.bfloat16)
    branch = jnp.dot(attn_b, out_w, preferred_element_type=jnp.float32)
    resid = inputs + layer_norm(branch, gain_ao, bias_ao)
    mlp_in = layer_norm(resid, gain_mi, bias_mi).astype(jnp.bfloat16)
    hidden_pre = jnp.dot(mlp_in, up_w, preferred_element_type=jnp.float32)
    hidden = jax.nn.gelu(hidden_pre, approximate=True).astype(jnp.bfloat16)
    mlp_out = jnp.dot(hidden, down_w, preferred_element_type=jnp.float32)
    result = resid + layer_norm(mlp_out, gain_mo, bias_mo)
    upstream = cotangent[0].astype(jnp.float32)
    d_mlp_out, dgain_mo, dbias_mo = norm_back(mlp_out, gain_mo, upstream)
    d_mlp_b = d_mlp_out.astype(jnp.bfloat16)
    grad_down = jnp.dot(hidden.T, d_mlp_b, preferred_element_type=jnp.float32)
    d_hidden = jnp.dot(d_mlp_b, down_w.T, preferred_element_type=jnp.float32)
    gelu_back = jax.vjp(lambda pre: jax.nn.gelu(pre, approximate=True), hidden_pre)[1]
    d_pre = gelu_back(d_hidden)[0].astype(jnp.bfloat16)
    grad_up = jnp.dot(mlp_in.T, d_pre, preferred_element_type=jnp.float32)
    d_mlp_in = jnp.dot(d_pre, up_w.T, preferred_element_type=jnp.float32)
    d_resid_n, dgain_mi, dbias_mi = norm_back(resid, gain_mi, d_mlp_in)
    d_resid = upstream + d_resid_n
    d_branch, dgain_ao, dbias_ao = norm_back(branch, gain_ao, d_resid)
    d_branch_b = d_branch.astype(jnp.bfloat16)
    grad_out = jnp.dot(attn_b.T, d_branch_b, preferred_element_type=jnp.float32)
    d_attn_flat = jnp.dot(d_branch_b, out_w.T, preferred_element_type=jnp.float32).astype(
        jnp.bfloat16
    )
    d_attn = d_attn_flat.reshape(row_count, HEADS, HD)
    delta = jnp.sum(d_attn.astype(jnp.float32) * attn_f, -1).T
    zero_heads = jnp.zeros((row_count, HEADS, HD), jnp.float32)

    def query_grad(dq_now, key_rows, value_rows, key_pos, key_seg):
        block_rows = math.gcd(key_rows.shape[0], 1024)

        def visit(dq_run, parts):
            key_block = parts[0].reshape(block_rows, HEADS, HD)
            value_block = parts[1].reshape(block_rows, HEADS, HD)
            d_scores = grad_block(
                queries,
                d_attn,
                lse,
                delta,
                key_block,
                value_block,
                my_pos,
                my_seg,
                parts[2],
                parts[3],
            )[1]
            return (
                dq_run
                + jnp.einsum(
                    "hqk,khd->qhd", d_scores, key_block, preferred_element_type=jnp.float32
                )
                * score_scale,
                None,
            )

        blocks = (
            split_blocks(key_rows, block_rows),
            split_blocks(value_rows, block_rows),
            split_blocks(key_pos, block_rows),
            split_blocks(key_seg, block_rows),
        )
        return lax.scan(visit, dq_now, blocks)[0]

    lse_all, delta_all = (
        lax.all_gather(lse.T, "ctx", axis=0, tiled=True),
        lax.all_gather(delta.T, "ctx", axis=0, tiled=True),
    )
    query_rows = lax.all_gather(queries.reshape(row_count, model_width), "ctx", axis=0, tiled=True)
    dattn_rows = lax.all_gather(d_attn_flat, "ctx", axis=0, tiled=True)
    span = query_rows.shape[0]
    query_block_rows = math.gcd(span, 1024)
    query_pos = true_position(jnp.arange(span, dtype=jnp.int32), row_count, ctx_size)

    def visit(sums, parts):
        d_keys, d_values = key_terms(
            parts[0].reshape(query_block_rows, HEADS, HD),
            parts[1].reshape(query_block_rows, HEADS, HD),
            parts[2].T,
            parts[3].T,
            parts[4],
            parts[5],
            keys_rot,
            values_heads,
            my_pos,
            my_seg,
        )
        return ((sums[0] + d_keys, sums[1] + d_values), None)

    blocks = (
        split_blocks(query_rows, query_block_rows),
        split_blocks(dattn_rows, query_block_rows),
        split_blocks(lse_all, query_block_rows),
        split_blocks(delta_all, query_block_rows),
        split_blocks(query_pos, query_block_rows),
        split_blocks(seg_all, query_block_rows),
    )
    dk_rot, dv_sum = lax.scan(visit, (zero_heads, zero_heads), blocks)[0]
    pieces = (
        lax.all_gather(keys_flat, "ctx", axis=0, tiled=True),
        lax.all_gather(values_flat, "ctx", axis=0, tiled=True),
    )
    span = pieces[0].shape[0]
    key_pos = true_position(jnp.arange(span, dtype=jnp.int32), row_count, ctx_size)
    key_seg = seg_all
    dq_rot = query_grad(zero_heads, pieces[0], pieces[1], key_pos, key_seg)
    d_query = unrotate(dq_rot, cos_t, sin_t).reshape(row_count, model_width).astype(jnp.bfloat16)
    d_key = unrotate(dk_rot, cos_t, sin_t).reshape(row_count, model_width).astype(jnp.bfloat16)
    d_value = dv_sum.reshape(row_count, model_width).astype(jnp.bfloat16)
    grad_query = jnp.dot(attn_in.T, d_query, preferred_element_type=jnp.float32)
    grad_key = jnp.dot(attn_in.T, d_key, preferred_element_type=jnp.float32)
    grad_value = jnp.dot(attn_in.T, d_value, preferred_element_type=jnp.float32)
    d_attn_in = (
        jnp.dot(d_query, query_w.T, preferred_element_type=jnp.float32)
        + jnp.dot(d_key, key_w.T, preferred_element_type=jnp.float32)
        + jnp.dot(d_value, value_w.T, preferred_element_type=jnp.float32)
    )
    d_inputs_n, dgain_ai, dbias_ai = norm_back(inputs, gain_ai, d_attn_in)
    input_grad = (d_resid + d_inputs_n)[None]
    shares = (
        lax.psum_scatter(grad_query, ("dp", "ctx"), scatter_dimension=0, tiled=True),
        lax.psum_scatter(grad_key, ("dp", "ctx"), scatter_dimension=0, tiled=True),
        lax.psum_scatter(grad_value, ("dp", "ctx"), scatter_dimension=0, tiled=True),
        lax.psum_scatter(grad_out, ("dp", "ctx"), scatter_dimension=0, tiled=True),
        lax.psum_scatter(grad_up, ("dp", "ctx"), scatter_dimension=0, tiled=True),
        lax.psum_scatter(grad_down, ("dp", "ctx"), scatter_dimension=0, tiled=True),
        lax.psum_scatter(dgain_ai, ("dp", "ctx"), scatter_dimension=0, tiled=True),
        lax.psum_scatter(dbias_ai, ("dp", "ctx"), scatter_dimension=0, tiled=True),
        lax.psum_scatter(dgain_ao, ("dp", "ctx"), scatter_dimension=0, tiled=True),
        lax.psum_scatter(dbias_ao, ("dp", "ctx"), scatter_dimension=0, tiled=True),
        lax.psum_scatter(dgain_mi, ("dp", "ctx"), scatter_dimension=0, tiled=True),
        lax.psum_scatter(dbias_mi, ("dp", "ctx"), scatter_dimension=0, tiled=True),
        lax.psum_scatter(dgain_mo, ("dp", "ctx"), scatter_dimension=0, tiled=True),
        lax.psum_scatter(dbias_mo, ("dp", "ctx"), scatter_dimension=0, tiled=True),
    )
    return (result.astype(jnp.bfloat16)[None], input_grad) + tuple(shares)


BF = jnp.bfloat16
F32 = jnp.float32
MESH_ID = pl.DeviceIdType.MESH
GROUP = 4
SPOTS = 8
ROWS = 128
WIDTH = 1024
VMEM_BYTES = 60 << 20


def dot(left, right, left_dim, right_dim):
    return lax.dot_general(
        left, right, (((left_dim,), (right_dim,)), ((), ())), preferred_element_type=F32
    )


class Here:
    def __init__(self):
        self.x = lax.axis_index("dp")
        at = lax.axis_index("ctx")
        self.z, self.y, self.c = at // 4, (at // 2) % 2, at % 2
        self.member = at % 4
        self.shard = 4 * self.x + self.z
        self.spot = self.z + self.x * (7 - 2 * self.z)
        self.core_mate = self.place(self.x, self.z, self.y, 1 - self.c)
        self.link_mate = self.place(self.x, self.z, 1 - self.y, self.c)
        self.far_mate = self.place(self.x, self.z, 1 - self.y, 1 - self.c)
        self.core_member = 2 * self.y + (1 - self.c)
        self.link_member = 2 * (1 - self.y) + self.c
        self.far_member = 2 * (1 - self.y) + (1 - self.c)
        self.right = self.on_ring(self.spot + 1)
        self.left = self.on_ring(self.spot + SPOTS - 1)

    @staticmethod
    def place(x, z, y, c):
        return (x, 4 * z + 2 * y + c)

    def on_ring(self, spot):
        spot = lax.rem(spot, SPOTS)
        x = spot // 4
        return self.place(x, spot + x * (7 - 2 * spot), self.y, self.c)

    @staticmethod
    def shard_at(spot):
        spot = lax.rem(spot, SPOTS)
        x = spot // 4
        return 4 * x + spot + x * (7 - 2 * spot)

    def plane(self, step):
        shard = lax.rem(self.shard + step, SPOTS)
        return shard, self.place(shard // 4, shard % 4, self.y, self.c)

    def along_z(self, step):
        z = lax.rem(self.z + step, 4)
        return z, self.place(self.x, z, self.y, self.c)

    def mates(self):
        return (
            (self.core_member, self.core_mate),
            (self.link_member, self.link_mate),
            (self.far_member, self.far_mate),
        )


class Post:
    def __init__(self, send_sems, recv_sems):
        self.send_sems, self.recv_sems = send_sems, recv_sems
        self.count = 0
        self.started = []

    def send(self, src, dst, to):
        copy = pltpu.make_async_remote_copy(
            src_ref=src,
            dst_ref=dst,
            send_sem=self.send_sems.at[self.count],
            recv_sem=self.recv_sems.at[self.count],
            device_id=to,
            device_id_type=MESH_ID,
        )
        copy.start()
        self.started.append(copy)
        self.count += 1
        return self.count - 1, to

    def arrived(self, sent, landing):
        number, to = sent
        pltpu.make_async_remote_copy(
            src_ref=landing,
            dst_ref=landing,
            send_sem=self.send_sems.at[number],
            recv_sem=self.recv_sems.at[number],
            device_id=to,
            device_id_type=MESH_ID,
        ).wait_recv()

    def finish(self):
        for copy in self.started:
            copy.wait_send()


class Local:
    def __init__(self, sems):
        self.sems = sems
        self.started = []

    def copy(self, src, dst):
        copy = pltpu.make_async_copy(src, dst, self.sems.at[len(self.started)])
        copy.start()
        self.started.append(copy)

    def finish(self):
        for copy in self.started:
            copy.wait()


def greet(places):
    barrier = pltpu.get_barrier_semaphore()
    for place in places:
        pl.semaphore_signal(barrier, inc=1, device_id=place, device_id_type=MESH_ID)
    pl.semaphore_wait(barrier, len(places))


class RingGather:
    STREAMS = ((1, 0, 4), (-1, 1, 4), (1, 1, 3), (-1, 0, 3))

    def __init__(self, here, post, held, own):
        self.here, self.post, self.held, self.own = here, post, held, own
        self.half = held.shape[1] // 2
        self.waiting = {}
        self.hops = 0

    def piece(self, shard, half):
        return self.held.at[shard, pl.ds(half * self.half, self.half)]

    def hop(self):
        self.hops += 1
        for way, half, length in self.STREAMS:
            if self.hops > length:
                continue
            if self.hops > 1:
                self.take(way, half)
            origin = self.here.shard_at(self.here.spot + SPOTS - way * (self.hops - 1))
            src = self.piece(origin, half)
            if self.hops == 1:
                src = self.own.at[pl.ds(half * self.half, self.half)]
            sent = self.post.send(
                src, self.piece(origin, half), self.here.right if way == 1 else self.here.left
            )
            came = self.here.shard_at(self.here.spot + SPOTS - way * self.hops)
            self.waiting[way, half] = (sent, self.piece(came, half))

    def take(self, way, half):
        sent, landing = self.waiting.pop((way, half))
        self.post.arrived(sent, landing)

    def finish(self):
        while self.hops < 4:
            self.hop()
        for key in list(self.waiting):
            self.take(*key)


class RingSum:
    def __init__(self, here, post, parts, landing):
        self.here, self.post, self.parts, self.landing = here, post, parts, landing
        self.half = parts.shape[1] // 2
        self.waiting = {}
        self.slots = 0
        self.hops = 0

    def part(self, distance, half):
        shard = self.here.shard_at(self.here.spot + SPOTS + distance)
        return self.parts.at[shard, pl.ds(half * self.half, self.half)]

    def hop(self):
        self.hops += 1
        distance = 5 - self.hops
        for way, half, first in ((1, 0, 1), (-1, 1, 1), (1, 1, 2), (-1, 0, 2)):
            if self.hops < first:
                continue
            src = self.part(way * distance, half)
            if self.hops > first:
                held = self.take(way, half)
                held[...] = (held[...].astype(F32) + src[...].astype(F32)).astype(held.dtype)
                src = held
            slot = self.landing.at[self.slots]
            self.slots += 1
            sent = self.post.send(src, slot, self.here.right if way == 1 else self.here.left)
            self.waiting[way, half] = (sent, slot)

    def take(self, way, half):
        sent, slot = self.waiting.pop((way, half))
        self.post.arrived(sent, slot)
        return slot

    def total(self):
        halves = []
        for half in (0, 1):
            value = self.part(0, half)[...].astype(F32)
            for way in (1, -1):
                value = value + self.take(way, half)[...].astype(F32)
            halves.append(value)
        return halves


def group_gather(here, post, held):
    mine = held.at[here.member]
    over = post.send(mine, mine, here.link_mate)
    near = post.send(mine, mine, here.core_mate)
    linked = held.at[here.link_member]
    post.arrived(over, linked)
    passed = post.send(linked, linked, here.core_mate)
    post.arrived(near, held.at[here.core_member])
    post.arrived(passed, held.at[here.far_member])


class GroupSum:
    def __init__(self, here, post, near_send, near_in, far_send, far_in):
        self.here, self.post = here, post
        self.near_send, self.near_in = near_send, near_in
        self.far_send, self.far_in = far_send, far_in

    def start(self, term):
        here, post = self.here, self.post
        near = []
        for slot, member in ((0, here.far_member), (1, here.core_member)):
            self.near_send[slot] = term(member).astype(BF)
            near.append(
                post.send(self.near_send.at[slot], self.near_in.at[slot], here.core_mate)
            )
        over = term(here.link_member)
        post.arrived(near[0], self.near_in.at[0])
        self.far_send[...] = (over + self.near_in[0].astype(F32)).astype(BF)
        self.far = post.send(self.far_send, self.far_in, here.link_mate)
        self.near = near[1]
        self.mine = term(here.member)

    def total(self):
        self.post.arrived(self.near, self.near_in.at[1])
        value = self.mine + self.near_in[1].astype(F32)
        self.post.arrived(self.far, self.far_in)
        return value + self.far_in[...].astype(F32)


def swap_along_z(here, post, local, src, dst):
    local.copy(src.at[here.z], dst.at[here.z])
    sent = []
    for step in (1, 2, 3):
        z, place = here.along_z(step)
        came = lax.rem(here.z + 4 - step, 4)
        sent.append((post.send(src.at[z], dst.at[here.z], place), dst.at[came]))
    return sent


def out_rows_target(here):
    return here.z % 2, 2 * here.y + here.c, here.z // 2, here.x


def out_rows_source(here):
    return here.c, 2 * here.y + here.x, here.z // 2, here.z % 2


def same_place(here, spot):
    x, z, y, c = spot
    return (x == here.x) & (z == here.z) & (y == here.y) & (c == here.c)


def turn_tables(rot):
    index = lax.broadcasted_iota(jnp.int32, (HD // 2, 1), 0).astype(F32)
    angle = rot * jnp.exp(index * (-math.log(10000.0) / (HD // 2)))
    return jnp.cos(angle), jnp.sin(angle)


def norm_parts(value):
    centred = value - jnp.mean(value, -1, keepdims=True)
    inv_std = lax.rsqrt(jnp.mean(centred * centred, -1, keepdims=True) + norm_eps)
    return centred * inv_std, inv_std


def norm_pull(normed, inv_std, gain, upstream):
    d_normed = upstream * gain
    return inv_std * (
        d_normed
        - jnp.mean(d_normed, -1, keepdims=True)
        - normed * jnp.mean(d_normed * normed, -1, keepdims=True)
    )


def first_kernel(
    tok, small, wq, wk, wv, wo, wu,
    qkv_heads, a_t, wqkv_out, wo_all, wu_shard, vectors, starts,
    x_all, wqkv, wqkv_send, wu_send, wu_in, small_in, small_all, qkv_send, wo_in,
    send_sems, recv_sems, local_sems, self_sems,
):
    here = Here()
    post = Post(send_sems, recv_sems)
    local = Local(local_sems)
    out_to, out_from = out_rows_target(here), out_rows_source(here)
    out_stays = same_place(here, out_to)
    barrier = pltpu.get_barrier_semaphore()
    partners = [place for _, place in here.mates()] + [here.plane(n)[1] for n in range(1, SPOTS)]
    for place in partners:
        pl.semaphore_signal(barrier, inc=1, device_id=place, device_id_type=MESH_ID)
    pl.when(jnp.logical_not(out_stays))(
        lambda: pl.semaphore_signal(
            barrier, inc=1, device_id=here.place(*out_from), device_id_type=MESH_ID
        )
    )
    for member in range(GROUP):
        base = 512 * (member % 2) + 256 * (member // 2)
        for slot, weight in enumerate((wq, wk, wv)):
            wqkv_send[member, :, 256 * slot : 256 * (slot + 1)] = weight[:, base : base + 256]
        for shard in range(SPOTS):
            at = 512 * shard + 128 * member
            wu_send[member, :, 128 * shard : 128 * (shard + 1)] = wu[:, at : at + 128]
    small_in[here.member] = small[...]
    x_all[here.member] = tok[...]
    wqkv[here.shard, pl.ds(pl.multiple_of(32 * here.member, 32), 32)] = wqkv_send[here.member]
    wu_in[here.member] = wu_send[here.member]

    @pl.when(out_stays)
    def _():
        pl.semaphore_wait(barrier, len(partners))
        wo_in[...] = wo[...]

    @pl.when(jnp.logical_not(out_stays))
    def _():
        pl.semaphore_wait(barrier, len(partners) + 1)

    wo_copy = pltpu.make_async_remote_copy(
        src_ref=wo, dst_ref=wo_in, send_sem=self_sems.at[0], recv_sem=self_sems.at[1],
        device_id=here.place(*out_to), device_id_type=MESH_ID,
    )
    small_sent, wqkv_sent, wu_sent = [], [], []
    for member, place in here.mates():
        small_sent.append(
            (post.send(small_in.at[here.member], small_in.at[here.member], place), small_in.at[member])
        )
    for member, place in here.mates():
        mine = wqkv.at[here.shard, pl.ds(pl.multiple_of(32 * here.member, 32), 32)]
        theirs = wqkv.at[here.shard, pl.ds(pl.multiple_of(32 * member, 32), 32)]
        wqkv_sent.append((post.send(wqkv_send.at[member], mine, place), theirs))
    pl.when(jnp.logical_not(out_stays))(wo_copy.start)
    x_over = post.send(x_all.at[here.member], x_all.at[here.member], here.link_mate)
    x_near = post.send(x_all.at[here.member], x_all.at[here.member], here.core_mate)
    for member, place in here.mates():
        wu_sent.append(
            (post.send(wu_send.at[member], wu_in.at[here.member], place), wu_in.at[member])
        )

    for sent, landing in small_sent:
        post.arrived(sent, landing)
    small_all[here.shard, 0:8] = (
        small_in[0, 0:8] + small_in[1, 0:8] + small_in[2, 0:8] + small_in[3, 0:8]
    )
    for member in range(GROUP):
        small_all[here.shard, 8 + member : 9 + member] = small_in[member, 8:9]
    plane_sent = []
    for step in range(1, SPOTS):
        _, place = here.plane(step)
        came = lax.rem(here.shard + SPOTS - step, SPOTS)
        mine = small_all.at[here.shard]
        plane_sent.append((post.send(mine, mine, place), small_all.at[came]))

    for sent, landing in wqkv_sent:
        post.arrived(sent, landing)
    qkv_ring = RingGather(here, post, wqkv, wqkv.at[here.shard])
    qkv_ring.hop()

    @pl.when(jnp.logical_not(out_stays))
    def _():
        wo_copy.wait_recv()
        wo_copy.wait_send()

    out_ring = RingGather(here, post, wo_all, wo_in)
    local.copy(wo_in, wo_all.at[here.shard])
    out_ring.hop()
    post.arrived(x_over, x_all.at[here.link_member])
    x_pass = post.send(
        x_all.at[here.link_member], x_all.at[here.link_member], here.core_mate
    )
    qkv_ring.hop()
    out_ring.hop()
    post.arrived(x_near, x_all.at[here.core_member])
    post.arrived(x_pass, x_all.at[here.far_member])
    for sent, landing in plane_sent:
        post.arrived(sent, landing)
    for shard in range(SPOTS):
        vectors[:, 128 * shard : 128 * (shard + 1)] = small_all[shard, 0:8]
    qkv_ring.hop()
    out_ring.hop()

    gain, bias = vectors[0:1], vectors[1:2]
    for member in range(GROUP):
        normed, _ = norm_parts(x_all[member].astype(F32))
        a_t[:, 128 * member : 128 * (member + 1)] = (normed * gain + bias).astype(BF).T

    segs = jnp.concatenate([small_all[4 * here.x + z, 8:12] for z in range(4)], 0)
    start = jnp.zeros_like(segs)
    for doc in range(1, 8):
        size = jnp.sum(
            jnp.sum((segs == doc - 1.0).astype(F32), 1, keepdims=True), 0, keepdims=True
        )
        start = start + jnp.where(segs >= doc, size, 0.0)
    starts[...] = start
    lane = lax.broadcasted_iota(jnp.int32, (1, ROWS), 1)
    rots = []
    for member in range(GROUP):
        at = 4 * here.z + member
        position = jnp.where(lane < 64, 64 * at + lane, 64 * (31 - at) + lane - 64)
        rots.append(position.astype(F32) - starts[pl.ds(at, 1)])
    cos_t, sin_t = turn_tables(jnp.concatenate(rots, 1))

    qkv_ring.finish()
    wqkv_flat = wqkv[...].reshape(WIDTH, 768)
    for part in range(3):
        product = dot(wqkv_flat[:, 256 * part : 256 * (part + 1)], a_t[...], 0, 0)
        for head in range(4):
            rows = product[HD * head : HD * (head + 1)]
            if part < 2:
                first, second = rows[: HD // 2], rows[HD // 2 :]
                rows = jnp.concatenate(
                    [first * cos_t - second * sin_t, second * cos_t + first * sin_t], 0
                )
            qkv_send[head, HD * part : HD * (part + 1)] = rows.astype(BF)
    swapped = swap_along_z(here, post, local, qkv_send, qkv_heads)
    local.copy(wqkv, wqkv_out)
    for sent, landing in wu_sent:
        post.arrived(sent, landing)
    local.copy(wu_in, wu_shard)
    out_ring.finish()
    for sent, landing in swapped:
        post.arrived(sent, landing)
    local.finish()
    post.finish()


def call_first(tok, small, wq, wk, wv, wo, wu):
    vmem = pl.BlockSpec(memory_space=pltpu.VMEM)
    anywhere = pl.BlockSpec(memory_space=pl.ANY)
    shape = jax.ShapeDtypeStruct
    return pl.pallas_call(
        first_kernel,
        out_shape=[
            shape((4, 192, 512), BF),
            shape((WIDTH, 512), BF),
            shape((SPOTS, ROWS, 768), BF),
            shape((SPOTS, 32, WIDTH), BF),
            shape((GROUP, 32, WIDTH), BF),
            shape((8, WIDTH), F32),
            shape((16, ROWS), F32),
        ],
        in_specs=[vmem] * 7,
        out_specs=[anywhere, vmem, anywhere, anywhere, anywhere, vmem, vmem],
        scratch_shapes=[
            pltpu.VMEM((GROUP, ROWS, WIDTH), BF),
            pltpu.VMEM((SPOTS, ROWS, 768), BF),
            pltpu.VMEM((GROUP, 32, 768), BF),
            pltpu.VMEM((GROUP, 32, WIDTH), BF),
            pltpu.VMEM((GROUP, 32, WIDTH), BF),
            pltpu.VMEM((GROUP, 16, ROWS), F32),
            pltpu.VMEM((SPOTS, 16, ROWS), F32),
            pltpu.VMEM((4, 192, 512), BF),
            pltpu.VMEM((32, WIDTH), BF),
            pltpu.SemaphoreType.DMA((64,)),
            pltpu.SemaphoreType.DMA((64,)),
            pltpu.SemaphoreType.DMA((8,)),
            pltpu.SemaphoreType.DMA((2,)),
        ],
        compiler_params=pltpu.CompilerParams(
            collective_id=0, has_side_effects=True, vmem_limit_bytes=VMEM_BYTES
        ),
        name="gather_and_project",
    )(tok, small, wq, wk, wv, wo, wu)


def true_group(ref, group):
    def chunk(at, late):
        tile = ref[at // 4, :, 128 * (at % 4) : 128 * (at % 4) + 128]
        return tile[:, 64:] if late else tile[:, :64]

    if group < 8:
        return jnp.concatenate([chunk(2 * group, False), chunk(2 * group + 1, False)], 1)
    return jnp.concatenate([chunk(31 - 2 * group, True), chunk(30 - 2 * group, True)], 1)


def stored_group(ref, at):
    def block(number):
        tile = ref[:, 128 * (number // 2) : 128 * (number // 2) + 128]
        return tile[:, 64:] if number % 2 else tile[:, :64]

    return jnp.concatenate([block(at), block(31 - at)], 1)


STEP = 256


def allowed_pairs(query_block, key_block, start):
    key_pos = STEP * key_block + lax.broadcasted_iota(jnp.int32, (STEP, STEP), 0)
    query_pos = STEP * query_block + lax.broadcasted_iota(jnp.int32, (STEP, STEP), 1)
    return (key_pos <= query_pos) & (key_pos >= start)


def attend_kernel(low, qkv_heads, start, o_heads, o_true, lse, qkv):
    for group in range(16):
        qkv[:, 128 * group : 128 * group + 128] = true_group(qkv_heads, group)
    for block in range(8):
        here = slice(STEP * block, STEP * (block + 1))
        query = qkv[0:HD, here]
        first = start[:, here]

        def visit(key_block, state, block=block, query=query, first=first):
            top, total, weighted = state
            keys = pl.ds(pl.multiple_of(key_block * STEP, STEP), STEP)
            scores = dot(qkv[HD : 2 * HD, keys], query, 0, 0) * HD**-0.5
            allowed = allowed_pairs(block, key_block, first)
            scores = jnp.where(allowed, scores, masked_value)
            top_new = jnp.maximum(top, jnp.max(scores, 0, keepdims=True))
            fade = jnp.exp(top - top_new)
            probs = jnp.where(allowed, jnp.exp(scores - top_new), 0.0)
            total = total * fade + jnp.sum(probs, 0, keepdims=True)
            weighted = weighted * fade + dot(qkv[2 * HD :, keys], probs.astype(BF), 1, 0)
            return top_new, total, weighted

        top, total, weighted = lax.fori_loop(
            low[block],
            block + 1,
            visit,
            (
                jnp.full((1, STEP), masked_value, F32),
                jnp.zeros((1, STEP), F32),
                jnp.zeros((HD, STEP), F32),
            ),
        )
        o_true[:, here] = weighted / total
        lse[:, here] = top + jnp.log(total)
    for at in range(16):
        o_heads[at // 4, :, 128 * (at % 4) : 128 * (at % 4) + 128] = stored_group(o_true, at).astype(BF)


def call_attend(low, qkv_heads, start):
    vmem = pl.BlockSpec(memory_space=pltpu.VMEM)
    shape = jax.ShapeDtypeStruct
    return pl.pallas_call(
        attend_kernel,
        out_shape=[
            shape((4, HD, 512), BF),
            shape((HD, 2048), F32),
            shape((1, 2048), F32),
            shape((192, 2048), BF),
        ],
        in_specs=[pl.BlockSpec(memory_space=pltpu.SMEM), vmem, vmem],
        out_specs=[vmem] * 4,
        compiler_params=pltpu.CompilerParams(vmem_limit_bytes=VMEM_BYTES),
        name="attend",
    )(low, qkv_heads, start)


def attend_back_kernel(low, qkv, o_true, lse, start, do_heads, out, d_out, delta, grads):
    for group in range(16):
        d_out[:, 128 * group : 128 * group + 128] = true_group(do_heads, group)
    delta[...] = jnp.sum(d_out[...].astype(F32) * o_true[...], 0, keepdims=True)
    grads[...] = jnp.zeros_like(grads)
    for block in range(8):
        here = slice(STEP * block, STEP * (block + 1))
        query, d_attn = qkv[0:HD, here], d_out[:, here]
        first, norm, less = start[:, here], lse[:, here], delta[:, here]

        def visit(
            key_block, d_query, block=block, query=query, d_attn=d_attn, first=first, norm=norm, less=less
        ):
            keys = pl.ds(pl.multiple_of(key_block * STEP, STEP), STEP)
            key = qkv[HD : 2 * HD, keys]
            scores = dot(key, query, 0, 0) * HD**-0.5
            probs = jnp.where(allowed_pairs(block, key_block, first), jnp.exp(scores - norm), 0.0)
            d_probs = dot(qkv[2 * HD :, keys], d_attn, 0, 0)
            d_scores = (probs * (d_probs - less)).astype(BF)
            grads[HD : 2 * HD, keys] += dot(query, d_scores, 1, 1)
            grads[2 * HD :, keys] += dot(d_attn, probs.astype(BF), 1, 1)
            return d_query + dot(key, d_scores, 1, 0)

        grads[0:HD, here] = lax.fori_loop(
            low[block], block + 1, visit, jnp.zeros((HD, STEP), F32)
        )
    position = lax.broadcasted_iota(jnp.int32, (1, 2048), 1).astype(F32)
    cos_t, sin_t = turn_tables(position - start[...])
    for part in range(2):
        first = grads[HD * part : HD * part + HD // 2] * HD**-0.5
        second = grads[HD * part + HD // 2 : HD * (part + 1)] * HD**-0.5
        grads[HD * part : HD * part + HD // 2] = first * cos_t + second * sin_t
        grads[HD * part + HD // 2 : HD * (part + 1)] = second * cos_t - first * sin_t
    for at in range(16):
        out[at // 4, :, 128 * (at % 4) : 128 * (at % 4) + 128] = stored_group(grads, at).astype(BF)


def call_attend_back(low, qkv, o_true, lse, start, do_heads):
    vmem = pl.BlockSpec(memory_space=pltpu.VMEM)
    return pl.pallas_call(
        attend_back_kernel,
        out_shape=jax.ShapeDtypeStruct((4, 192, 512), BF),
        in_specs=[pl.BlockSpec(memory_space=pltpu.SMEM)] + [vmem] * 5,
        out_specs=vmem,
        scratch_shapes=[
            pltpu.VMEM((HD, 2048), BF),
            pltpu.VMEM((1, 2048), F32),
            pltpu.VMEM((192, 2048), F32),
        ],
        compiler_params=pltpu.CompilerParams(vmem_limit_bytes=VMEM_BYTES),
        name="attend_back",
    )(low, qkv, o_true, lse, start, do_heads)


GELU_K = math.sqrt(2.0 / math.pi)


def gelu_and_slope(pre):
    square = pre * pre
    bend = jnp.tanh(GELU_K * pre * (1.0 + 0.044715 * square))
    half = 0.5 * (1.0 + bend)
    slope = half + 0.5 * pre * (1.0 - bend * bend) * GELU_K * (1.0 + 3 * 0.044715 * square)
    return pre * half, slope


def middle_kernel(
    o_heads, tok, cot, wo_all, wu_own, wd_own, vectors,
    act, d_res, do_heads, g_down, g_up, g_out, d_vec,
    o_all, wu_all, wd_all, c_all, dm_all, dt_all, gl_all, slope_all, du_all, do_send,
    near_send, near_in, far_send, far_in, down_parts, down_in, res,
    send_sems, recv_sems, local_sems,
):
    here = Here()
    post = Post(send_sems, recv_sems)
    local = Local(local_sems)
    greet([place for _, place in here.mates()] + [here.right, here.left]
          + [here.along_z(step)[1] for step in (1, 2, 3)])
    swapped = swap_along_z(here, post, local, o_heads, o_all)
    up_ring = RingGather(here, post, wu_all, wu_own)
    down_ring = RingGather(here, post, wd_all, wd_own)
    local.copy(wu_own, wu_all.at[here.shard])
    local.copy(wd_own, wd_all.at[here.shard])
    up_ring.hop()
    sums = [
        GroupSum(here, post, near_send.at[n], near_in.at[n], far_send.at[n], far_in.at[n])
        for n in range(3)
    ]
    for sent, landing in swapped:
        post.arrived(sent, landing)
    local.finish()

    o_flat = o_all[...].reshape(256, 512)
    wo_flat = wo_all[...].reshape(256, WIDTH)

    def token_rows(member):
        return pl.ds(pl.multiple_of(ROWS * member, ROWS), ROWS)

    def out_term(member):
        heads = [o_all[z, :, token_rows(member)] for z in range(4)]
        return dot(jnp.concatenate(heads, 0), wo_flat, 0, 0)

    sums[0].start(out_term)
    up_ring.hop()
    down_ring.hop()
    branch = sums[0].total()
    t_normed, t_inv = norm_parts(branch)
    hres = tok[...].astype(F32) + t_normed * vectors[2:3] + vectors[3:4]
    res[0] = t_normed
    h_normed, h_inv = norm_parts(hres)
    res[1] = h_normed
    res[2] = hres
    c_all[here.member] = (h_normed * vectors[4:5] + vectors[5:6]).astype(BF)
    group_gather(here, post, c_all)
    up_ring.finish()
    down_ring.hop()
    wu_flat = wu_all[...].reshape(WIDTH, WIDTH)
    for member in range(GROUP):
        gl, slope = gelu_and_slope(dot(c_all[member], wu_flat, 1, 0))
        gl_all[member] = gl.astype(BF)
        slope_all[member] = slope
    down_ring.finish()
    wd_flat = wd_all[...].reshape(WIDTH, WIDTH)
    sums[1].start(lambda member: dot(gl_all[member], wd_flat, 1, 0))
    branch = sums[1].total()
    m_normed, m_inv = norm_parts(branch)
    act[...] = (res[2] + m_normed * vectors[6:7] + vectors[7:8]).astype(BF)
    upstream = cot[...].astype(F32)
    dm_all[here.member] = norm_pull(m_normed, m_inv, vectors[6:7], upstream).astype(BF)
    d_vec[0:2] = jnp.zeros((2, WIDTH), F32)
    d_vec[6:7] = jnp.sum(upstream * m_normed, 0, keepdims=True)
    d_vec[7:8] = jnp.sum(upstream, 0, keepdims=True)
    group_gather(here, post, dm_all)
    for member in range(GROUP):
        du_all[member] = (dot(dm_all[member], wd_flat, 1, 1) * slope_all[member]).astype(BF)
    sums[2].start(lambda member: dot(du_all[member], wu_flat, 1, 1))
    gl_flat = gl_all[...].reshape(512, WIDTH)
    dm_flat = dm_all[...].reshape(512, WIDTH)
    for shard in range(SPOTS):
        down_parts[shard] = dot(gl_flat[:, ROWS * shard : ROWS * (shard + 1)], dm_flat, 0, 0).astype(BF)
    down_sum = RingSum(here, post, down_parts, down_in)
    down_sum.hop()
    du_flat = du_all[...].reshape(512, WIDTH)
    c_flat = c_all[...].reshape(512, WIDTH)
    for shard in range(SPOTS):
        g_up[shard] = dot(c_flat[:, ROWS * shard : ROWS * (shard + 1)], du_flat, 0, 0).astype(BF)
    d_c = sums[2].total()
    h_normed = res[1]
    d_h = upstream + norm_pull(h_normed, h_inv, vectors[4:5], d_c)
    d_vec[4:5] = jnp.sum(d_c * h_normed, 0, keepdims=True)
    d_vec[5:6] = jnp.sum(d_c, 0, keepdims=True)
    t_normed = res[0]
    dt_all[here.member] = norm_pull(t_normed, t_inv, vectors[2:3], d_h).astype(BF)
    d_vec[2:3] = jnp.sum(d_h * t_normed, 0, keepdims=True)
    d_vec[3:4] = jnp.sum(d_h, 0, keepdims=True)
    d_res[...] = d_h
    down_sum.hop()
    group_gather(here, post, dt_all)
    dt_flat = dt_all[...].reshape(512, WIDTH)
    d_o = dot(wo_flat, dt_flat, 1, 1)
    for head in range(4):
        do_send[head] = d_o[HD * head : HD * (head + 1)].astype(BF)
    late_local = Local(local_sems)
    swapped = swap_along_z(here, post, late_local, do_send, do_heads)
    down_sum.hop()
    g_out[...] = dot(o_flat, dt_flat, 1, 0).astype(BF).reshape(SPOTS, 32, WIDTH)
    down_sum.hop()
    low_half, high_half = down_sum.total()
    g_down[0:64] = low_half
    g_down[64:128] = high_half
    for sent, landing in swapped:
        post.arrived(sent, landing)
    late_local.finish()
    post.finish()


def call_middle(o_heads, tok, cot, wo_all, wu_own, wd_own, vectors):
    vmem = pl.BlockSpec(memory_space=pltpu.VMEM)
    anywhere = pl.BlockSpec(memory_space=pl.ANY)
    shape = jax.ShapeDtypeStruct
    dma = pltpu.SemaphoreType.DMA
    return pl.pallas_call(
        middle_kernel,
        out_shape=[
            shape((ROWS, WIDTH), BF),
            shape((ROWS, WIDTH), F32),
            shape((4, HD, 512), BF),
            shape((ROWS, WIDTH), F32),
            shape((SPOTS, ROWS, WIDTH), BF),
            shape((SPOTS, 32, WIDTH), BF),
            shape((8, WIDTH), F32),
        ],
        in_specs=[vmem] * 7,
        out_specs=[vmem, vmem, anywhere, vmem, vmem, vmem, vmem],
        scratch_shapes=[
            pltpu.VMEM((4, HD, 512), BF),
            pltpu.VMEM((SPOTS, ROWS, WIDTH), BF),
            pltpu.VMEM((SPOTS, ROWS, WIDTH), BF),
            pltpu.VMEM((GROUP, ROWS, WIDTH), BF),
            pltpu.VMEM((GROUP, ROWS, WIDTH), BF),
            pltpu.VMEM((GROUP, ROWS, WIDTH), BF),
            pltpu.VMEM((GROUP, ROWS, WIDTH), BF),
            pltpu.VMEM((GROUP, ROWS, WIDTH), F32),
            pltpu.VMEM((GROUP, ROWS, WIDTH), BF),
            pltpu.VMEM((4, HD, 512), BF),
            pltpu.VMEM((3, 2, ROWS, WIDTH), BF),
            pltpu.VMEM((3, 2, ROWS, WIDTH), BF),
            pltpu.VMEM((3, ROWS, WIDTH), BF),
            pltpu.VMEM((3, ROWS, WIDTH), BF),
            pltpu.VMEM((SPOTS, ROWS, WIDTH), BF),
            pltpu.VMEM((14, ROWS // 2, WIDTH), BF),
            pltpu.VMEM((3, ROWS, WIDTH), F32),
            dma((80,)),
            dma((80,)),
            dma((8,)),
        ],
        compiler_params=pltpu.CompilerParams(
            collective_id=1, has_side_effects=True, vmem_limit_bytes=VMEM_BYTES
        ),
        name="feed_forward",
    )(o_heads, tok, cot, wo_all, wu_own, wd_own, vectors)


def last_kernel(
    d_heads, a_t, wqkv, up_parts, out_parts, d_res, tok, vectors, d_vec,
    in_grad, g_q, g_k, g_v, g_out, g_up, g_vec,
    d_in, d_all, qkv_parts, up_in, out_in, qkv_in, near_send, near_in, far_send, far_in,
    vec_send, vec_in, vec_group, up_send, up_got, qkv_end, qkv_got, out_end, out_got,
    send_sems, recv_sems, local_sems, self_sems,
):
    here = Here()
    post = Post(send_sems, recv_sems)
    local = Local(local_sems)
    out_to, out_from = out_rows_source(here), out_rows_target(here)
    out_stays = same_place(here, out_to)
    barrier = pltpu.get_barrier_semaphore()
    partners = [place for _, place in here.mates()] + [here.plane(n)[1] for n in range(1, SPOTS)]
    for place in partners:
        pl.semaphore_signal(barrier, inc=1, device_id=place, device_id_type=MESH_ID)
    pl.when(jnp.logical_not(out_stays))(
        lambda: pl.semaphore_signal(
            barrier, inc=1, device_id=here.place(*out_from), device_id_type=MESH_ID
        )
    )

    @pl.when(out_stays)
    def _():
        pl.semaphore_wait(barrier, len(partners))

    @pl.when(jnp.logical_not(out_stays))
    def _():
        pl.semaphore_wait(barrier, len(partners) + 1)

    swapped = swap_along_z(here, post, local, d_heads, d_in)
    up_sum = RingSum(here, post, up_parts, up_in)
    out_sum = RingSum(here, post, out_parts, out_in)
    qkv_sum = RingSum(here, post, qkv_parts, qkv_in)
    up_sum.hop()
    out_sum.hop()
    for sent, landing in swapped:
        post.arrived(sent, landing)
    local.finish()
    for part in range(3):
        for head in range(4):
            at = 256 * part + HD * head
            d_all[at : at + HD] = d_in[head, HD * part : HD * (part + 1)]
    wqkv_flat = wqkv[...].reshape(WIDTH, 768)

    def in_term(member):
        rows = pl.ds(pl.multiple_of(ROWS * member, ROWS), ROWS)
        return dot(d_all[:, rows], wqkv_flat, 0, 1)

    in_sum = GroupSum(here, post, near_send, near_in, far_send, far_in)
    in_sum.start(in_term)
    up_sum.hop()
    for shard in range(SPOTS):
        qkv_parts[shard] = dot(a_t[ROWS * shard : ROWS * (shard + 1)], d_all[...], 1, 1).astype(BF)
    qkv_sum.hop()
    out_sum.hop()
    d_a = in_sum.total()
    normed, inv_std = norm_parts(tok[...].astype(F32))
    in_grad[...] = d_res[...] + norm_pull(normed, inv_std, vectors[0:1], d_a)
    row = lax.broadcasted_iota(jnp.int32, (8, WIDTH), 0)
    terms = jnp.where(
        row == 0,
        jnp.sum(d_a * normed, 0, keepdims=True),
        jnp.where(row == 1, jnp.sum(d_a, 0, keepdims=True), d_vec[...]),
    )
    for shard in range(SPOTS):
        vec_send[shard] = terms[:, ROWS * shard : ROWS * (shard + 1)]
    vec_in[here.shard] = vec_send[here.shard]
    vec_sent = []
    for step in range(1, SPOTS):
        shard, place = here.plane(step)
        came = lax.rem(here.shard + SPOTS - step, SPOTS)
        vec_sent.append((post.send(vec_send.at[shard], vec_in.at[here.shard], place), vec_in.at[came]))
    up_sum.hop()
    qkv_sum.hop()
    out_sum.hop()
    for sent, landing in vec_sent:
        post.arrived(sent, landing)
    total = vec_in[0]
    for shard in range(1, SPOTS):
        total = total + vec_in[shard]
    vec_group[here.member] = total
    vec_sent = []
    for member, place in here.mates():
        mine = vec_group.at[here.member]
        vec_sent.append((post.send(mine, mine, place), vec_group.at[member]))
    up_sum.hop()
    qkv_sum.hop()
    out_sum.hop()

    low_half, high_half = up_sum.total()
    for member in range(GROUP):
        half = low_half if member < 2 else high_half
        up_send[member] = half[32 * (member % 2) : 32 * (member % 2) + 32].astype(BF)
    up_got[here.member] = up_send[here.member]
    ends = []
    for member, place in here.mates():
        ends.append((post.send(up_send.at[member], up_got.at[here.member], place), up_got.at[member]))
    qkv_sum.hop()
    low_half, high_half = out_sum.total()
    out_end[0:16] = low_half.astype(BF)
    out_end[16:32] = high_half.astype(BF)
    out_copy = pltpu.make_async_remote_copy(
        src_ref=out_end, dst_ref=out_got, send_sem=self_sems.at[0], recv_sem=self_sems.at[1],
        device_id=here.place(*out_to), device_id_type=MESH_ID,
    )

    @pl.when(out_stays)
    def _():
        out_got[...] = out_end[...]

    pl.when(jnp.logical_not(out_stays))(out_copy.start)
    low_half, high_half = qkv_sum.total()
    for member in range(GROUP):
        half = low_half if member < 2 else high_half
        qkv_end[member] = half[32 * (member % 2) : 32 * (member % 2) + 32].astype(BF)
    qkv_got[here.member] = qkv_end[here.member]
    for member, place in here.mates():
        ends.append((post.send(qkv_end.at[member], qkv_got.at[here.member], place), qkv_got.at[member]))
    for sent, landing in vec_sent:
        post.arrived(sent, landing)
    g_vec[...] = vec_group[0] + vec_group[1] + vec_group[2] + vec_group[3]

    for sent, landing in ends[:3]:
        post.arrived(sent, landing)
    for member in range(GROUP):
        for shard in range(SPOTS):
            at = 512 * shard + 128 * member
            g_up[:, at : at + 128] = up_got[member, :, 128 * shard : 128 * (shard + 1)].astype(F32)

    @pl.when(jnp.logical_not(out_stays))
    def _():
        out_copy.wait_recv()
        out_copy.wait_send()

    g_out[...] = out_got[...].astype(F32)
    for sent, landing in ends[3:]:
        post.arrived(sent, landing)
    for member in range(GROUP):
        base = 512 * (member % 2) + 256 * (member // 2)
        for slot, out in enumerate((g_q, g_k, g_v)):
            out[:, base : base + 256] = qkv_got[member, :, 256 * slot : 256 * (slot + 1)].astype(F32)
    post.finish()


def call_last(d_heads, a_t, wqkv, up_parts, out_parts, d_res, tok, vectors, d_vec):
    vmem = pl.BlockSpec(memory_space=pltpu.VMEM)
    shape = jax.ShapeDtypeStruct
    dma = pltpu.SemaphoreType.DMA
    return pl.pallas_call(
        last_kernel,
        out_shape=[
            shape((ROWS, WIDTH), F32),
            shape((32, WIDTH), F32),
            shape((32, WIDTH), F32),
            shape((32, WIDTH), F32),
            shape((32, WIDTH), F32),
            shape((32, 4 * WIDTH), F32),
            shape((8, ROWS), F32),
        ],
        in_specs=[vmem] * 9,
        out_specs=[vmem] * 7,
        scratch_shapes=[
            pltpu.VMEM((4, 192, 512), BF),
            pltpu.VMEM((768, 512), BF),
            pltpu.VMEM((SPOTS, ROWS, 768), BF),
            pltpu.VMEM((14, ROWS // 2, WIDTH), BF),
            pltpu.VMEM((14, 16, WIDTH), BF),
            pltpu.VMEM((14, ROWS // 2, 768), BF),
            pltpu.VMEM((2, ROWS, WIDTH), BF),
            pltpu.VMEM((2, ROWS, WIDTH), BF),
            pltpu.VMEM((ROWS, WIDTH), BF),
            pltpu.VMEM((ROWS, WIDTH), BF),
            pltpu.VMEM((SPOTS, 8, ROWS), F32),
            pltpu.VMEM((SPOTS, 8, ROWS), F32),
            pltpu.VMEM((GROUP, 8, ROWS), F32),
            pltpu.VMEM((GROUP, 32, WIDTH), BF),
            pltpu.VMEM((GROUP, 32, WIDTH), BF),
            pltpu.VMEM((GROUP, 32, 768), BF),
            pltpu.VMEM((GROUP, 32, 768), BF),
            pltpu.VMEM((32, WIDTH), BF),
            pltpu.VMEM((32, WIDTH), BF),
            dma((80,)),
            dma((80,)),
            dma((8,)),
            dma((2,)),
        ],
        compiler_params=pltpu.CompilerParams(
            collective_id=2, has_side_effects=True, vmem_limit_bytes=VMEM_BYTES
        ),
        name="gradients",
    )(d_heads, a_t, wqkv, up_parts, out_parts, d_res, tok, vectors, d_vec)


def on_device_grouped(
    tokens, segments, cotangent, w_query, w_key, w_value, w_out, w_up, w_down,
    gain_attn_in, bias_attn_in, gain_attn_out, bias_attn_out,
    gain_mlp_in, bias_mlp_in, gain_mlp_out, bias_mlp_out,
):
    member = lax.axis_index("ctx") % GROUP
    norms = jnp.stack([
        gain_attn_in, bias_attn_in, gain_attn_out, bias_attn_out,
        gain_mlp_in, bias_mlp_in, gain_mlp_out, bias_mlp_out,
    ]).astype(F32)
    lane_member = jnp.arange(ROWS, dtype=jnp.int32)[None] // 32
    spread = jnp.where(lane_member == member, jnp.tile(norms, (1, GROUP)), 0.0)
    small = jnp.concatenate([spread, segments.astype(F32), jnp.zeros((7, ROWS), F32)], 0)
    tok, cot = tokens[0], cotangent[0]
    qkv_heads, a_t, wqkv, wo_all, wu_own, vectors, starts = call_first(
        tok, small, w_query, w_key, w_value, w_out, w_up
    )
    halves = starts.reshape(16, 2, 64)
    start = jnp.concatenate([halves[:, 0], halves[::-1, 1]], 0).reshape(1, 2048)
    low = (start[0, ::STEP] * (1.0 / STEP)).astype(jnp.int32)
    o_heads, o_true, lse, qkv = call_attend(low, qkv_heads, start)
    act, d_res, do_heads, g_down, up_parts, out_parts, d_vec = call_middle(
        o_heads, tok, cot, wo_all, wu_own.reshape(ROWS, WIDTH), w_down, vectors
    )
    d_heads = call_attend_back(low, qkv, o_true, lse, start, do_heads)
    in_grad, g_q, g_k, g_v, g_out, g_up, g_vec = call_last(
        d_heads, a_t, wqkv, up_parts, out_parts, d_res, tok, vectors, d_vec
    )
    g_vec = lax.dynamic_slice_in_dim(g_vec, member * 32, 32, 1)
    return (act[None], in_grad[None], g_q, g_k, g_v, g_out, g_up, g_down) + tuple(
        g_vec[row] for row in range(8)
    )


def solution(mesh):
    in_specs = (
        P("dp", "ctx", None),
        P("dp", "ctx"),
        P("dp", "ctx", None),
        P(("dp", "ctx"), None),
        P(("dp", "ctx"), None),
        P(("dp", "ctx"), None),
        P(("dp", "ctx"), None),
        P(("dp", "ctx"), None),
        P(("dp", "ctx"), None),
        P(("dp", "ctx")),
        P(("dp", "ctx")),
        P(("dp", "ctx")),
        P(("dp", "ctx")),
        P(("dp", "ctx")),
        P(("dp", "ctx")),
        P(("dp", "ctx")),
        P(("dp", "ctx")),
    )
    out_specs = (
        P("dp", "ctx", None),
        P("dp", "ctx", None),
        P(("dp", "ctx"), None),
        P(("dp", "ctx"), None),
        P(("dp", "ctx"), None),
        P(("dp", "ctx"), None),
        P(("dp", "ctx"), None),
        P(("dp", "ctx"), None),
        P(("dp", "ctx")),
        P(("dp", "ctx")),
        P(("dp", "ctx")),
        P(("dp", "ctx")),
        P(("dp", "ctx")),
        P(("dp", "ctx")),
        P(("dp", "ctx")),
        P(("dp", "ctx")),
    )
    grouped = mesh.shape["dp"] == 2 and mesh.shape["ctx"] == 16
    return jax.shard_map(
        on_device_grouped if grouped else on_device, mesh=mesh, in_specs=in_specs, out_specs=out_specs, check_vma=False
    )
```

```python
import math

import jax
import jax.numpy as jnp
from jax import lax
from jax.experimental import pallas as pl
from jax.experimental.pallas import tpu as pltpu
from jax.sharding import PartitionSpec as P

HEADS = 16
HD = 64


norm_eps = 1e-05
masked_value = -1e30


def layer_norm(value, gain, bias):
    row_mean = jnp.mean(value, -1, keepdims=True)
    centred = value - row_mean
    scaled = centred * lax.rsqrt(jnp.mean(centred * centred, -1, keepdims=True) + norm_eps)
    return scaled * gain + bias


def norm_back(value, gain, upstream):
    row_mean = jnp.mean(value, -1, keepdims=True)
    centred = value - row_mean
    inv_std = lax.rsqrt(jnp.mean(centred * centred, -1, keepdims=True) + norm_eps)
    normed = centred * inv_std
    d_normed = upstream * gain
    d_value = inv_std * (
        d_normed
        - jnp.mean(d_normed, -1, keepdims=True)
        - normed * jnp.mean(d_normed * normed, -1, keepdims=True)
    )
    return (d_value, jnp.sum(upstream * normed, 0), jnp.sum(upstream, 0))


def rope_tables(offsets, head_dim):
    freq = 10000.0 ** (-jnp.arange(head_dim // 2, dtype=jnp.float32) / (head_dim // 2))
    angle = offsets.astype(jnp.float32)[..., None] * freq
    return (jnp.cos(angle)[..., None, :], jnp.sin(angle)[..., None, :])


def rotate(values, cos_t, sin_t):
    half_dim = values.shape[-1] // 2
    first = values[..., :half_dim]
    second = values[..., half_dim:]
    return jnp.concatenate([first * cos_t - second * sin_t, second * cos_t + first * sin_t], -1)


def unrotate(grads, cos_t, sin_t):
    half_dim = grads.shape[-1] // 2
    first = grads[..., :half_dim]
    second = grads[..., half_dim:]
    return jnp.concatenate([first * cos_t + second * sin_t, second * cos_t - first * sin_t], -1)


def true_position(flat_index, row_count, ctx_size):
    device_of = flat_index // row_count
    offset_in = flat_index % row_count
    half_rows = row_count // 2
    return jnp.where(
        offset_in < half_rows,
        device_of * half_rows + offset_in,
        (2 * ctx_size - 1 - device_of) * half_rows + offset_in - half_rows,
    )


def split_blocks(array, block_rows):
    return array.reshape((array.shape[0] // block_rows, block_rows) + array.shape[1:])


def score_block(queries, keys, query_pos, query_seg, key_pos, key_seg):
    scores = jnp.einsum(
        "qhd,khd->hqk", queries, keys, preferred_element_type=jnp.float32
    ) * queries.shape[-1] ** (-0.5)
    allowed = (query_seg[:, None] == key_seg[None, :]) & (key_pos[None, :] <= query_pos[:, None])
    return (scores, allowed[None])


def grad_block(queries, d_attn, lse, delta, keys, values, query_pos, query_seg, key_pos, key_seg):
    scores, allowed = score_block(queries, keys, query_pos, query_seg, key_pos, key_seg)
    attn_probs = jnp.where(allowed, jnp.exp(scores - lse[:, :, None]), 0.0)
    d_probs = jnp.einsum("qhd,khd->hqk", d_attn, values, preferred_element_type=jnp.float32)
    d_scores = (attn_probs * (d_probs - delta[:, :, None])).astype(jnp.bfloat16)
    return (attn_probs, d_scores)


def key_terms(
    query_rows,
    dattn_rows,
    lse_rows,
    delta_rows,
    query_pos,
    query_seg,
    key_block,
    value_block,
    key_pos,
    key_seg,
):
    attn_probs, d_scores = grad_block(
        query_rows,
        dattn_rows,
        lse_rows,
        delta_rows,
        key_block,
        value_block,
        query_pos,
        query_seg,
        key_pos,
        key_seg,
    )
    d_keys = jnp.einsum(
        "hqk,qhd->khd", d_scores, query_rows, preferred_element_type=jnp.float32
    ) * query_rows.shape[-1] ** (-0.5)
    d_values = jnp.einsum(
        "hqk,qhd->khd",
        attn_probs.astype(jnp.bfloat16),
        dattn_rows,
        preferred_element_type=jnp.float32,
    )
    return (d_keys, d_values)


def on_device(
    tokens,
    segments,
    cotangent,
    w_query,
    w_key,
    w_value,
    w_out,
    w_up,
    w_down,
    gain_attn_in,
    bias_attn_in,
    gain_attn_out,
    bias_attn_out,
    gain_mlp_in,
    bias_mlp_in,
    gain_mlp_out,
    bias_mlp_out,
):
    whole = (
        lax.all_gather(w_query, ("dp", "ctx"), axis=0, tiled=True),
        lax.all_gather(w_key, ("dp", "ctx"), axis=0, tiled=True),
        lax.all_gather(w_value, ("dp", "ctx"), axis=0, tiled=True),
        lax.all_gather(w_out, ("dp", "ctx"), axis=0, tiled=True),
        lax.all_gather(w_up, ("dp", "ctx"), axis=0, tiled=True),
        lax.all_gather(w_down, ("dp", "ctx"), axis=0, tiled=True),
        lax.all_gather(gain_attn_in, ("dp", "ctx"), axis=0, tiled=True),
        lax.all_gather(bias_attn_in, ("dp", "ctx"), axis=0, tiled=True),
        lax.all_gather(gain_attn_out, ("dp", "ctx"), axis=0, tiled=True),
        lax.all_gather(bias_attn_out, ("dp", "ctx"), axis=0, tiled=True),
        lax.all_gather(gain_mlp_in, ("dp", "ctx"), axis=0, tiled=True),
        lax.all_gather(bias_mlp_in, ("dp", "ctx"), axis=0, tiled=True),
        lax.all_gather(gain_mlp_out, ("dp", "ctx"), axis=0, tiled=True),
        lax.all_gather(bias_mlp_out, ("dp", "ctx"), axis=0, tiled=True),
    )
    query_w, key_w, value_w, out_w, up_w, down_w = whole[:6]
    gain_ai, bias_ai, gain_ao, bias_ao, gain_mi, bias_mi, gain_mo, bias_mo = [
        entry.astype(jnp.float32) for entry in whole[6:]
    ]
    row_count = tokens.shape[1]
    model_width = tokens.shape[2]
    ctx_size = lax.axis_size("ctx")
    seq_length = row_count * ctx_size
    score_scale = HD ** (-0.5)
    seg_all = lax.all_gather(segments, "ctx", axis=1, tiled=True)[0]
    my_seg = segments[0]
    all_pos = true_position(jnp.arange(seq_length, dtype=jnp.int32), row_count, ctx_size)
    my_pos = true_position(
        lax.axis_index("ctx") * row_count + jnp.arange(row_count, dtype=jnp.int32),
        row_count,
        ctx_size,
    )
    doc_first = jnp.min(
        jnp.where(seg_all[None, :] == my_seg[:, None], all_pos[None, :], seq_length), axis=1
    )
    cos_t, sin_t = rope_tables(my_pos - doc_first, HD)
    inputs = tokens[0].astype(jnp.float32)
    attn_in = layer_norm(inputs, gain_ai, bias_ai).astype(jnp.bfloat16)
    query_pre = jnp.dot(attn_in, query_w, preferred_element_type=jnp.float32).reshape(
        row_count, HEADS, HD
    )
    key_pre = jnp.dot(attn_in, key_w, preferred_element_type=jnp.float32).reshape(
        row_count, HEADS, HD
    )
    queries = rotate(query_pre, cos_t, sin_t).astype(jnp.bfloat16)
    keys_rot = rotate(key_pre, cos_t, sin_t).astype(jnp.bfloat16)
    values_flat = jnp.dot(attn_in, value_w, preferred_element_type=jnp.float32).astype(jnp.bfloat16)
    values_heads = values_flat.reshape(row_count, HEADS, HD)
    keys_flat = keys_rot.reshape(row_count, model_width)
    start_state = (
        jnp.full((HEADS, row_count), masked_value, jnp.float32),
        jnp.zeros((HEADS, row_count), jnp.float32),
        jnp.zeros((row_count, HEADS, HD), jnp.float32),
    )
    key_rows = lax.all_gather(keys_flat, "ctx", axis=0, tiled=True)
    value_rows = lax.all_gather(values_flat, "ctx", axis=0, tiled=True)
    span = key_rows.shape[0]
    block_rows = math.gcd(span, 1024)
    key_pos = true_position(jnp.arange(span, dtype=jnp.int32), row_count, ctx_size)
    key_seg = seg_all

    def visit(state_now, parts):
        row_top, row_total, weighted = state_now
        key_block = parts[0].reshape(block_rows, HEADS, HD)
        value_block = parts[1].reshape(block_rows, HEADS, HD)
        scores, allowed = score_block(queries, key_block, my_pos, my_seg, parts[2], parts[3])
        top_new = jnp.maximum(row_top, jnp.max(jnp.where(allowed, scores, masked_value), -1))
        fade = jnp.exp(row_top - top_new)
        attn_probs = jnp.where(allowed, jnp.exp(scores - top_new[:, :, None]), 0.0)
        row_total = row_total * fade + jnp.sum(attn_probs, -1)
        weighted = weighted * fade.T[:, :, None] + jnp.einsum(
            "hqk,khd->qhd",
            attn_probs.astype(jnp.bfloat16),
            value_block,
            preferred_element_type=jnp.float32,
        )
        return ((top_new, row_total, weighted), None)

    blocks = (
        split_blocks(key_rows, block_rows),
        split_blocks(value_rows, block_rows),
        split_blocks(key_pos, block_rows),
        split_blocks(key_seg, block_rows),
    )
    row_top, row_total, weighted = lax.scan(visit, start_state, blocks)[0]
    lse = row_top + jnp.log(row_total)
    attn_f = weighted / row_total.T[:, :, None]
    attn_b = attn_f.reshape(row_count, model_width).astype(jnp.bfloat16)
    branch = jnp.dot(attn_b, out_w, preferred_element_type=jnp.float32)
    resid = inputs + layer_norm(branch, gain_ao, bias_ao)
    mlp_in = layer_norm(resid, gain_mi, bias_mi).astype(jnp.bfloat16)
    hidden_pre = jnp.dot(mlp_in, up_w, preferred_element_type=jnp.float32)
    hidden = jax.nn.gelu(hidden_pre, approximate=True).astype(jnp.bfloat16)
    mlp_out = jnp.dot(hidden, down_w, preferred_element_type=jnp.float32)
    result = resid + layer_norm(mlp_out, gain_mo, bias_mo)
    upstream = cotangent[0].astype(jnp.float32)
    d_mlp_out, dgain_mo, dbias_mo = norm_back(mlp_out, gain_mo, upstream)
    d_mlp_b = d_mlp_out.astype(jnp.bfloat16)
    grad_down = jnp.dot(hidden.T, d_mlp_b, preferred_element_type=jnp.float32)
    d_hidden = jnp.dot(d_mlp_b, down_w.T, preferred_element_type=jnp.float32)
    gelu_back = jax.vjp(lambda pre: jax.nn.gelu(pre, approximate=True), hidden_pre)[1]
    d_pre = gelu_back(d_hidden)[0].astype(jnp.bfloat16)
    grad_up = jnp.dot(mlp_in.T, d_pre, preferred_element_type=jnp.float32)
    d_mlp_in = jnp.dot(d_pre, up_w.T, preferred_element_type=jnp.float32)
    d_resid_n, dgain_mi, dbias_mi = norm_back(resid, gain_mi, d_mlp_in)
    d_resid = upstream + d_resid_n
    d_branch, dgain_ao, dbias_ao = norm_back(branch, gain_ao, d_resid)
    d_branch_b = d_branch.astype(jnp.bfloat16)
    grad_out = jnp.dot(attn_b.T, d_branch_b, preferred_element_type=jnp.float32)
    d_attn_flat = jnp.dot(d_branch_b, out_w.T, preferred_element_type=jnp.float32).astype(
        jnp.bfloat16
    )
    d_attn = d_attn_flat.reshape(row_count, HEADS, HD)
    delta = jnp.sum(d_attn.astype(jnp.float32) * attn_f, -1).T
    zero_heads = jnp.zeros((row_count, HEADS, HD), jnp.float32)

    def query_grad(dq_now, key_rows, value_rows, key_pos, key_seg):
        block_rows = math.gcd(key_rows.shape[0], 1024)

        def visit(dq_run, parts):
            key_block = parts[0].reshape(block_rows, HEADS, HD)
            value_block = parts[1].reshape(block_rows, HEADS, HD)
            d_scores = grad_block(
                queries,
                d_attn,
                lse,
                delta,
                key_block,
                value_block,
                my_pos,
                my_seg,
                parts[2],
                parts[3],
            )[1]
            return (
                dq_run
                + jnp.einsum(
                    "hqk,khd->qhd", d_scores, key_block, preferred_element_type=jnp.float32
                )
                * score_scale,
                None,
            )

        blocks = (
            split_blocks(key_rows, block_rows),
            split_blocks(value_rows, block_rows),
            split_blocks(key_pos, block_rows),
            split_blocks(key_seg, block_rows),
        )
        return lax.scan(visit, dq_now, blocks)[0]

    lse_all, delta_all = (
        lax.all_gather(lse.T, "ctx", axis=0, tiled=True),
        lax.all_gather(delta.T, "ctx", axis=0, tiled=True),
    )
    query_rows = lax.all_gather(queries.reshape(row_count, model_width), "ctx", axis=0, tiled=True)
    dattn_rows = lax.all_gather(d_attn_flat, "ctx", axis=0, tiled=True)
    span = query_rows.shape[0]
    query_block_rows = math.gcd(span, 1024)
    query_pos = true_position(jnp.arange(span, dtype=jnp.int32), row_count, ctx_size)

    def visit(sums, parts):
        d_keys, d_values = key_terms(
            parts[0].reshape(query_block_rows, HEADS, HD),
            parts[1].reshape(query_block_rows, HEADS, HD),
            parts[2].T,
            parts[3].T,
            parts[4],
            parts[5],
            keys_rot,
            values_heads,
            my_pos,
            my_seg,
        )
        return ((sums[0] + d_keys, sums[1] + d_values), None)

    blocks = (
        split_blocks(query_rows, query_block_rows),
        split_blocks(dattn_rows, query_block_rows),
        split_blocks(lse_all, query_block_rows),
        split_blocks(delta_all, query_block_rows),
        split_blocks(query_pos, query_block_rows),
        split_blocks(seg_all, query_block_rows),
    )
    dk_rot, dv_sum = lax.scan(visit, (zero_heads, zero_heads), blocks)[0]
    pieces = (
        lax.all_gather(keys_flat, "ctx", axis=0, tiled=True),
        lax.all_gather(values_flat, "ctx", axis=0, tiled=True),
    )
    span = pieces[0].shape[0]
    key_pos = true_position(jnp.arange(span, dtype=jnp.int32), row_count, ctx_size)
    key_seg = seg_all
    dq_rot = query_grad(zero_heads, pieces[0], pieces[1], key_pos, key_seg)
    d_query = unrotate(dq_rot, cos_t, sin_t).reshape(row_count, model_width).astype(jnp.bfloat16)
    d_key = unrotate(dk_rot, cos_t, sin_t).reshape(row_count, model_width).astype(jnp.bfloat16)
    d_value = dv_sum.reshape(row_count, model_width).astype(jnp.bfloat16)
    grad_query = jnp.dot(attn_in.T, d_query, preferred_element_type=jnp.float32)
    grad_key = jnp.dot(attn_in.T, d_key, preferred_element_type=jnp.float32)
    grad_value = jnp.dot(attn_in.T, d_value, preferred_element_type=jnp.float32)
    d_attn_in = (
        jnp.dot(d_query, query_w.T, preferred_element_type=jnp.float32)
        + jnp.dot(d_key, key_w.T, preferred_element_type=jnp.float32)
        + jnp.dot(d_value, value_w.T, preferred_element_type=jnp.float32)
    )
    d_inputs_n, dgain_ai, dbias_ai = norm_back(inputs, gain_ai, d_attn_in)
    input_grad = (d_resid + d_inputs_n)[None]
    shares = (
        lax.psum_scatter(grad_query, ("dp", "ctx"), scatter_dimension=0, tiled=True),
        lax.psum_scatter(grad_key, ("dp", "ctx"), scatter_dimension=0, tiled=True),
        lax.psum_scatter(grad_value, ("dp", "ctx"), scatter_dimension=0, tiled=True),
        lax.psum_scatter(grad_out, ("dp", "ctx"), scatter_dimension=0, tiled=True),
        lax.psum_scatter(grad_up, ("dp", "ctx"), scatter_dimension=0, tiled=True),
        lax.psum_scatter(grad_down, ("dp", "ctx"), scatter_dimension=0, tiled=True),
        lax.psum_scatter(dgain_ai, ("dp", "ctx"), scatter_dimension=0, tiled=True),
        lax.psum_scatter(dbias_ai, ("dp", "ctx"), scatter_dimension=0, tiled=True),
        lax.psum_scatter(dgain_ao, ("dp", "ctx"), scatter_dimension=0, tiled=True),
        lax.psum_scatter(dbias_ao, ("dp", "ctx"), scatter_dimension=0, tiled=True),
        lax.psum_scatter(dgain_mi, ("dp", "ctx"), scatter_dimension=0, tiled=True),
        lax.psum_scatter(dbias_mi, ("dp", "ctx"), scatter_dimension=0, tiled=True),
        lax.psum_scatter(dgain_mo, ("dp", "ctx"), scatter_dimension=0, tiled=True),
        lax.psum_scatter(dbias_mo, ("dp", "ctx"), scatter_dimension=0, tiled=True),
    )
    return (result.astype(jnp.bfloat16)[None], input_grad) + tuple(shares)


BF = jnp.bfloat16
F32 = jnp.float32
MESH_ID = pl.DeviceIdType.MESH
GROUP = 4
SPOTS = 8
ROWS = 128
WIDTH = 1024
VMEM_BYTES = 60 << 20


def dot(left, right, left_dim, right_dim):
    return lax.dot_general(
        left, right, (((left_dim,), (right_dim,)), ((), ())), preferred_element_type=F32
    )


class Here:
    def __init__(self):
        self.x = lax.axis_index("dp")
        at = lax.axis_index("ctx")
        self.z, self.y, self.c = at // 4, (at // 2) % 2, at % 2
        self.member = at % 4
        self.shard = 4 * self.x + self.z
        self.spot = self.z + self.x * (7 - 2 * self.z)
        self.core_mate = self.place(self.x, self.z, self.y, 1 - self.c)
        self.link_mate = self.place(self.x, self.z, 1 - self.y, self.c)
        self.far_mate = self.place(self.x, self.z, 1 - self.y, 1 - self.c)
        self.core_member = 2 * self.y + (1 - self.c)
        self.link_member = 2 * (1 - self.y) + self.c
        self.far_member = 2 * (1 - self.y) + (1 - self.c)
        self.right = self.on_ring(self.spot + 1)
        self.left = self.on_ring(self.spot + SPOTS - 1)

    @staticmethod
    def place(x, z, y, c):
        return (x, 4 * z + 2 * y + c)

    def on_ring(self, spot):
        spot = lax.rem(spot, SPOTS)
        x = spot // 4
        return self.place(x, spot + x * (7 - 2 * spot), self.y, self.c)

    @staticmethod
    def shard_at(spot):
        spot = lax.rem(spot, SPOTS)
        x = spot // 4
        return 4 * x + spot + x * (7 - 2 * spot)

    def plane(self, step):
        shard = lax.rem(self.shard + step, SPOTS)
        return shard, self.place(shard // 4, shard % 4, self.y, self.c)

    def along_z(self, step):
        z = lax.rem(self.z + step, 4)
        return z, self.place(self.x, z, self.y, self.c)

    def mates(self):
        return (
            (self.core_member, self.core_mate),
            (self.link_member, self.link_mate),
            (self.far_member, self.far_mate),
        )


class Post:
    def __init__(self, send_sems, recv_sems):
        self.send_sems, self.recv_sems = send_sems, recv_sems
        self.count = 0
        self.started = []

    def send(self, src, dst, to):
        copy = pltpu.make_async_remote_copy(
            src_ref=src,
            dst_ref=dst,
            send_sem=self.send_sems.at[self.count],
            recv_sem=self.recv_sems.at[self.count],
            device_id=to,
            device_id_type=MESH_ID,
        )
        copy.start()
        self.started.append(copy)
        self.count += 1
        return self.count - 1, to

    def arrived(self, sent, landing):
        number, to = sent
        pltpu.make_async_remote_copy(
            src_ref=landing,
            dst_ref=landing,
            send_sem=self.send_sems.at[number],
            recv_sem=self.recv_sems.at[number],
            device_id=to,
            device_id_type=MESH_ID,
        ).wait_recv()

    def finish(self):
        for copy in self.started:
            copy.wait_send()


class Local:
    def __init__(self, sems):
        self.sems = sems
        self.started = []

    def copy(self, src, dst):
        copy = pltpu.make_async_copy(src, dst, self.sems.at[len(self.started)])
        copy.start()
        self.started.append(copy)
        return copy


class RingGather:
    STREAMS = ((1, 0, 4), (-1, 1, 4), (1, 1, 3), (-1, 0, 3))

    def __init__(self, here, post, held, own):
        self.here, self.post, self.held, self.own = here, post, held, own
        self.half = held.shape[1] // 2
        self.waiting = {}
        self.hops = 0

    def piece(self, shard, half):
        return self.held.at[shard, pl.ds(half * self.half, self.half)]

    def hop(self):
        self.hops += 1
        for way, half, length in self.STREAMS:
            if self.hops > length:
                continue
            if self.hops > 1:
                self.take(way, half)
            origin = self.here.shard_at(self.here.spot + SPOTS - way * (self.hops - 1))
            src = self.piece(origin, half)
            if self.hops == 1:
                src = self.own.at[pl.ds(half * self.half, self.half)]
            sent = self.post.send(
                src, self.piece(origin, half), self.here.right if way == 1 else self.here.left
            )
            came = self.here.shard_at(self.here.spot + SPOTS - way * self.hops)
            self.waiting[way, half] = (sent, self.piece(came, half))

    def take(self, way, half):
        sent, landing = self.waiting.pop((way, half))
        self.post.arrived(sent, landing)

    def finish(self):
        while self.hops < 4:
            self.hop()
        for key in list(self.waiting):
            self.take(*key)


class RingSum:
    def __init__(self, here, post, parts, landing):
        self.here, self.post, self.parts, self.landing = here, post, parts, landing
        self.half = parts.shape[1] // 2
        self.waiting = {}
        self.slots = 0
        self.hops = 0

    def part(self, distance, half):
        shard = self.here.shard_at(self.here.spot + SPOTS + distance)
        return self.parts.at[shard, pl.ds(half * self.half, self.half)]

    def hop(self):
        self.hops += 1
        distance = 5 - self.hops
        for way, half, first in ((1, 0, 1), (-1, 1, 1), (1, 1, 2), (-1, 0, 2)):
            if self.hops < first:
                continue
            src = self.part(way * distance, half)
            if self.hops > first:
                held = self.take(way, half)
                held[...] = (held[...].astype(F32) + src[...].astype(F32)).astype(held.dtype)
                src = held
            slot = self.landing.at[self.slots]
            self.slots += 1
            sent = self.post.send(src, slot, self.here.right if way == 1 else self.here.left)
            self.waiting[way, half] = (sent, slot)

    def take(self, way, half):
        sent, slot = self.waiting.pop((way, half))
        self.post.arrived(sent, slot)
        return slot

    def total(self):
        halves = []
        for half in (0, 1):
            value = self.part(0, half)[...].astype(F32)
            for way in (1, -1):
                value = value + self.take(way, half)[...].astype(F32)
            halves.append(value)
        return halves


class GroupGather:
    def __init__(self, here, post, held):
        self.here, self.post, self.held = here, post, held
        self.over = []
        for half in (0, 1):
            mine = self.piece(here.member, half)
            self.over.append(post.send(mine, mine, here.link_mate))
        mine = held.at[here.member]
        self.core = post.send(mine, mine, here.core_mate)

    def piece(self, member, half):
        return self.held.at[member, pl.ds(64 * half, 64)]

    def near(self):
        self.post.arrived(self.core, self.held.at[self.here.core_member])

    def rest(self):
        here, passed = self.here, []
        for half in (0, 1):
            linked = self.piece(here.link_member, half)
            self.post.arrived(self.over[half], linked)
            passed.append(self.post.send(linked, linked, here.core_mate))
        for half in (0, 1):
            self.post.arrived(passed[half], self.piece(here.far_member, half))


class GroupSum:
    def __init__(self, here, post, near_send, near_in, far_send, far_in, terms):
        self.here, self.post = here, post
        self.near_send, self.near_in = near_send, near_in
        self.far_send, self.far_in = far_send, far_in
        self.terms = terms
        self.near = [None, None]

    def give(self, slot, value):
        here = self.here
        self.terms[slot] = value.reshape(2, ROWS, WIDTH)
        self.near_send[slot] = self.terms[slot, 1 - here.c].astype(BF)
        self.near[slot] = self.post.send(
            self.near_send.at[slot], self.near_in.at[slot], here.core_mate
        )

    def cross(self):
        here = self.here
        self.post.arrived(self.near[0], self.near_in.at[0])
        self.far_send[...] = (self.terms[0, here.c] + self.near_in[0].astype(F32)).astype(BF)
        self.far = self.post.send(self.far_send, self.far_in, here.link_mate)

    def total(self):
        self.post.arrived(self.near[1], self.near_in.at[1])
        value = self.terms[1, self.here.c] + self.near_in[1].astype(F32)
        self.post.arrived(self.far, self.far_in)
        return value + self.far_in[...].astype(F32)


class SwapAlongZ:
    def __init__(self, here, post, local, src, dst):
        self.post = post
        self.sent = []
        for step in (2, 1, 3):
            z, place = here.along_z(step)
            came = lax.rem(here.z + 4 - step, 4)
            self.sent.append((post.send(src.at[z], dst.at[here.z], place), dst.at[came]))
        self.own = local.copy(src.at[here.z], dst.at[here.z])

    def finish(self):
        self.own.wait()
        for sent, landing in self.sent:
            self.post.arrived(sent, landing)


def out_rows_target(here):
    return here.z % 2, 2 * here.y + here.c, here.z // 2, here.x


def out_rows_source(here):
    return here.c, 2 * here.y + here.x, here.z // 2, here.z % 2


def same_place(here, spot):
    x, z, y, c = spot
    return (x == here.x) & (z == here.z) & (y == here.y) & (c == here.c)


def turn_tables(rot):
    index = lax.broadcasted_iota(jnp.int32, (HD // 2, 1), 0).astype(F32)
    angle = rot * jnp.exp(index * (-math.log(10000.0) / (HD // 2)))
    return jnp.cos(angle), jnp.sin(angle)


def norm_parts(value):
    centred = value - jnp.mean(value, -1, keepdims=True)
    inv_std = lax.rsqrt(jnp.mean(centred * centred, -1, keepdims=True) + norm_eps)
    return centred * inv_std, inv_std


def norm_pull(normed, inv_std, gain, upstream):
    d_normed = upstream * gain
    return inv_std * (
        d_normed
        - jnp.mean(d_normed, -1, keepdims=True)
        - normed * jnp.mean(d_normed * normed, -1, keepdims=True)
    )


def true_group(ref, group):
    def chunk(at, late):
        tile = ref[at // 4, :, 128 * (at % 4) : 128 * (at % 4) + 128]
        return tile[:, 64:] if late else tile[:, :64]

    if group < 8:
        return jnp.concatenate([chunk(2 * group, False), chunk(2 * group + 1, False)], 1)
    return jnp.concatenate([chunk(31 - 2 * group, True), chunk(30 - 2 * group, True)], 1)


def stored_group(ref, at):
    def block(number):
        tile = ref[:, 128 * (number // 2) : 128 * (number // 2) + 128]
        return tile[:, 64:] if number % 2 else tile[:, :64]

    return jnp.concatenate([block(at), block(31 - at)], 1)


def allowed_pairs(key_at, keys, query_at, queries, start):
    key_pos = key_at + lax.broadcasted_iota(jnp.int32, (keys, queries), 0)
    allowed = key_pos >= start
    if key_at + keys > query_at:
        allowed &= key_pos <= query_at + lax.broadcasted_iota(jnp.int32, (keys, queries), 1)
    return allowed


def attend_block(qkv, start, o_true, lse, query_at, queries, keys):
    here = slice(query_at, query_at + queries)
    query, first = qkv[0:HD, here], start[:, here]
    parts, top = [], None
    for key_at in range(0, query_at + queries, keys):
        scores = dot(qkv[HD : 2 * HD, key_at : key_at + keys], query, 0, 0)
        scores = jnp.where(
            allowed_pairs(key_at, keys, query_at, queries, first), scores, masked_value
        )
        peak = jnp.max(scores, 0, keepdims=True)
        top = peak if top is None else jnp.maximum(top, peak)
        parts.append((key_at, scores))
    total, weighted = 0.0, 0.0
    for key_at, scores in parts:
        probs = jnp.exp(scores - top)
        total = total + jnp.sum(probs, 0, keepdims=True)
        weighted = weighted + dot(qkv[2 * HD :, key_at : key_at + keys], probs.astype(BF), 1, 0)
    o_true[:, here] = weighted / total
    lse[:, here] = top + jnp.log(total)


def attend_back_block(qkv, start, o_true, lse, d_out, grads, query_at, queries):
    here = slice(query_at, query_at + queries)
    reach = slice(0, query_at + queries)
    query, d_attn = qkv[0:HD, here], d_out[:, here]
    key = qkv[HD : 2 * HD, reach]
    delta = jnp.sum(d_attn.astype(F32) * o_true[:, here], 0, keepdims=True)
    allowed = allowed_pairs(0, query_at + queries, query_at, queries, start[:, here])
    probs = jnp.where(allowed, jnp.exp(dot(key, query, 0, 0) - lse[:, here]), 0.0)
    d_probs = dot(qkv[2 * HD :, reach], d_attn, 0, 0)
    d_scores = (probs * (d_probs - delta)).astype(BF)
    grads[HD : 2 * HD, reach] += dot(query, d_scores, 1, 1)
    grads[2 * HD :, reach] += dot(d_attn, probs.astype(BF), 1, 1)
    grads[0:HD, here] = dot(key, d_scores, 1, 0) * HD**-0.5


GELU_K = math.sqrt(2.0 / math.pi)


def gelu_and_slope(pre):
    square = pre * pre
    bend = jnp.tanh(GELU_K * pre * (1.0 + 0.044715 * square))
    half = 0.5 * (1.0 + bend)
    slope = half + 0.5 * pre * (1.0 - bend * bend) * GELU_K * (1.0 + 3 * 0.044715 * square)
    return pre * half, slope


def layer_kernel(
    tok_hbm, seg_hbm, cot_hbm, wq, wk, wv, wo, wu, wd, *rest
):
    norms = rest[:8]
    act, in_grad, g_down, up_got, qkv_got, out_got, g_vec = rest[8:15]
    (
        tok, cot, wqkv_own, wu_own, seg_in,
        x_all, wqkv, wqkv_send, wu_send, wu_in, small_in, small_all, wo_in, wo_all, wu_all, wd_all,
        vectors, starts, start, a_t, qkv_send, qkv_heads, qkv, o_true, lse, o_send, o_all,
        c_all, dm_all, dt_all, gl_all, slope_all, du_all, res,
        near_send, near_in, far_send, far_in, terms,
        do_send, do_heads, d_out, grads, d_send, d_in, d_all,
        down_parts, down_in, up_parts, up_in, out_parts, out_in, qkv_parts, qkv_in,
        vec_send, vec_in, vec_group, d_vec, up_send, qkv_end, out_end,
        send_sems, recv_sems, local_sems, self_sems,
    ) = rest[15:]
    here = Here()
    post = Post(send_sems, recv_sems)
    local = Local(local_sems)
    out_to, out_from = out_rows_target(here), out_rows_source(here)
    out_stays = same_place(here, out_to)
    out_moves = jnp.logical_not(out_stays)
    barrier = pltpu.get_barrier_semaphore()
    partners = [place for _, place in here.mates()] + [here.plane(n)[1] for n in range(1, SPOTS)]
    for place in partners:
        pl.semaphore_signal(barrier, inc=1, device_id=place, device_id_type=MESH_ID)

    @pl.when(out_moves)
    def _():
        for spot in (out_from, out_to):
            pl.semaphore_signal(
                barrier, inc=1, device_id=here.place(*spot), device_id_type=MESH_ID
            )

    loads = [
        local.copy(weight, wqkv_own.at[slot]) for slot, weight in enumerate((wq, wk, wv))
    ]
    load_wu = local.copy(wu, wu_own)
    load_tok = local.copy(tok_hbm, tok)
    load_seg = local.copy(seg_hbm, seg_in)
    load_cot = local.copy(cot_hbm, cot)
    load_wd = local.copy(wd, wd_all.at[here.shard])

    lane = lax.broadcasted_iota(jnp.int32, (1, ROWS), 1)
    for row, vector in enumerate(norms):
        value = vector[...].astype(F32)
        value = jnp.concatenate([value] * GROUP, 1)
        small_in[here.member, row : row + 1] = jnp.where(lane // 32 == here.member, value, 0.0)
    load_seg.wait()
    small_in[here.member, 8:9] = seg_in[...].astype(F32)
    for load in loads:
        load.wait()
    for member in range(GROUP):
        base = 512 * (member % 2) + 256 * (member // 2)
        for slot in range(3):
            wqkv_send[member, :, 256 * slot : 256 * (slot + 1)] = wqkv_own[slot, :, base : base + 256]
    wqkv[here.shard, pl.ds(pl.multiple_of(32 * here.member, 32), 32)] = wqkv_send[here.member]
    load_tok.wait()
    x_all[here.member] = tok[...]

    @pl.when(out_stays)
    def _():
        pl.semaphore_wait(barrier, len(partners))

    @pl.when(out_moves)
    def _():
        pl.semaphore_wait(barrier, len(partners) + 2)

    small_sent, wqkv_sent, wu_sent = [], [], []
    for member, place in here.mates():
        mine = small_in.at[here.member]
        small_sent.append((post.send(mine, mine, place), small_in.at[member]))
    for member, place in here.mates():
        mine = wqkv.at[here.shard, pl.ds(pl.multiple_of(32 * here.member, 32), 32)]
        theirs = wqkv.at[here.shard, pl.ds(pl.multiple_of(32 * member, 32), 32)]
        wqkv_sent.append((post.send(wqkv_send.at[member], mine, place), theirs))
    x_gather = GroupGather(here, post, x_all)
    down_ring = RingGather(here, post, wd_all, wd)
    down_ring.hop()
    wo_copy = pltpu.make_async_remote_copy(
        src_ref=wo, dst_ref=wo_in, send_sem=self_sems.at[0], recv_sem=self_sems.at[1],
        device_id=here.place(*out_to), device_id_type=MESH_ID,
    )
    wo_keep = pltpu.make_async_copy(wo, wo_in, self_sems.at[2])
    pl.when(out_moves)(wo_copy.start)
    pl.when(out_stays)(wo_keep.start)
    load_wu.wait()
    for member in range(GROUP):
        for shard in range(SPOTS):
            at = 512 * shard + 128 * member
            wu_send[member, :, 128 * shard : 128 * (shard + 1)] = wu_own[:, at : at + 128]
    wu_in[pl.ds(pl.multiple_of(32 * here.member, 32), 32)] = wu_send[here.member]
    for member, place in here.mates():
        mine = wu_in.at[pl.ds(pl.multiple_of(32 * here.member, 32), 32)]
        theirs = wu_in.at[pl.ds(pl.multiple_of(32 * member, 32), 32)]
        wu_sent.append((post.send(wu_send.at[member], mine, place), theirs))

    for sent, landing in small_sent:
        post.arrived(sent, landing)
    small_all[here.shard, 0:8] = (
        small_in[0, 0:8] + small_in[1, 0:8] + small_in[2, 0:8] + small_in[3, 0:8]
    )
    for member in range(GROUP):
        small_all[here.shard, 8 + member : 9 + member] = small_in[member, 8:9]
    plane_sent = []
    for step in range(1, SPOTS):
        _, place = here.plane(step)
        came = lax.rem(here.shard + SPOTS - step, SPOTS)
        mine = small_all.at[here.shard]
        plane_sent.append((post.send(mine, mine, place), small_all.at[came]))

    for sent, landing in wqkv_sent:
        post.arrived(sent, landing)
    qkv_ring = RingGather(here, post, wqkv, wqkv.at[here.shard])
    qkv_ring.hop()
    x_gather.near()
    for sent, landing in plane_sent:
        post.arrived(sent, landing)
    for shard in range(SPOTS):
        vectors[:, 128 * shard : 128 * (shard + 1)] = small_all[shard, 0:8]
    gain, bias = vectors[0:1], vectors[1:2]

    def put_a(member):
        normed, _ = norm_parts(x_all[member].astype(F32))
        at = pl.ds(pl.multiple_of(ROWS * member, ROWS), ROWS)
        a_t[:, at] = (normed * gain + bias).astype(BF).T

    x_gather.rest()
    qkv_ring.hop()

    @pl.when(out_moves)
    def _():
        wo_copy.wait_recv()
        wo_copy.wait_send()

    pl.when(out_stays)(wo_keep.wait)
    out_ring = RingGather(here, post, wo_all, wo_in)
    wo_all[here.shard] = wo_in[...]
    out_ring.hop()
    put_a(here.member)
    put_a(here.core_member)
    qkv_ring.hop()
    out_ring.hop()
    put_a(here.link_member)
    put_a(here.far_member)

    segs = jnp.concatenate([small_all[4 * here.x + z, 8:12] for z in range(4)], 0)
    begin = jnp.zeros_like(segs)
    for doc in range(1, 8):
        size = jnp.sum(
            jnp.sum((segs == doc - 1.0).astype(F32), 1, keepdims=True), 0, keepdims=True
        )
        begin = begin + jnp.where(segs >= doc, size, 0.0)
    starts[...] = begin
    for group in range(16):
        a, b, cut = 2 * group, 2 * group + 1, slice(0, 64)
        if group >= 8:
            a, b, cut = 31 - a, 31 - b, slice(64, 128)
        start[:, ROWS * group : ROWS * (group + 1)] = jnp.concatenate(
            [starts[a : a + 1, cut], starts[b : b + 1, cut]], 1
        ).astype(jnp.int32)
    rots = []
    for member in range(GROUP):
        at = 4 * here.z + member
        position = jnp.where(lane < 64, 64 * at + lane, 64 * (31 - at) + lane - 64)
        rots.append(position.astype(F32) - starts[pl.ds(at, 1)])
    cos_t, sin_t = turn_tables(jnp.concatenate(rots, 1))
    qkv_ring.hop()
    out_ring.hop()
    for sent, landing in wu_sent:
        post.arrived(sent, landing)
    up_ring = RingGather(here, post, wu_all, wu_in)
    wu_all[here.shard] = wu_in[...]
    up_ring.hop()
    qkv_ring.finish()

    wqkv_flat = wqkv[...].reshape(WIDTH, 768)
    for part in range(3):
        product = dot(wqkv_flat[:, 256 * part : 256 * (part + 1)], a_t[...], 0, 0)
        for head in range(4):
            rows = product[HD * head : HD * (head + 1)]
            if part < 2:
                first, second = rows[: HD // 2], rows[HD // 2 :]
                rows = jnp.concatenate(
                    [first * cos_t - second * sin_t, second * cos_t + first * sin_t], 0
                )
            if part == 0:
                rows = rows * HD**-0.5
            qkv_send[head, HD * part : HD * (part + 1)] = rows.astype(BF)
    swap = SwapAlongZ(here, post, local, qkv_send, qkv_heads)
    out_ring.finish()
    swap.finish()
    down_ring.hop()
    up_ring.hop()
    for group in range(16):
        qkv[:, ROWS * group : ROWS * (group + 1)] = true_group(qkv_heads, group)
    for query_at in range(0, 2048, 512):
        attend_block(qkv, start, o_true, lse, query_at, 512, 512)
    for at in range(16):
        o_send[at // 4, :, 128 * (at % 4) : 128 * (at % 4) + 128] = stored_group(o_true, at).astype(BF)
    swap = SwapAlongZ(here, post, local, o_send, o_all)
    swap.finish()
    down_ring.hop()
    up_ring.hop()

    sums = [
        GroupSum(here, post, near_send.at[n], near_in.at[n], far_send.at[n], far_in.at[n], terms)
        for n in range(4)
    ]
    wo_flat = wo_all[...].reshape(256, WIDTH)

    def half_lanes(y):
        return pl.ds(pl.multiple_of(256 * y, 256), 256)

    def out_half(y):
        heads = [o_all[z, :, half_lanes(y)] for z in range(4)]
        return dot(jnp.concatenate(heads, 0), wo_flat, 0, 0)

    sums[0].give(0, out_half(1 - here.y))
    sums[0].give(1, out_half(here.y))
    sums[0].cross()
    branch = sums[0].total()
    t_normed, t_inv = norm_parts(branch)
    hres = tok[...].astype(F32) + t_normed * vectors[2:3] + vectors[3:4]
    res[0] = t_normed
    h_normed, h_inv = norm_parts(hres)
    res[1] = h_normed
    res[2] = hres
    c_all[here.member] = (h_normed * vectors[4:5] + vectors[5:6]).astype(BF)
    gather = GroupGather(here, post, c_all)
    down_ring.hop()
    up_ring.hop()
    gather.near()
    up_ring.finish()
    wu_flat = wu_all[...].reshape(WIDTH, WIDTH)

    def half(held, y):
        return held[pl.ds(2 * y, 2)].reshape(2 * ROWS, WIDTH)

    def up_half(y):
        gl, slope = gelu_and_slope(dot(half(c_all, y), wu_flat, 1, 0))
        gl_all[pl.ds(2 * y, 2)] = gl.astype(BF).reshape(2, ROWS, WIDTH)
        slope_all[pl.ds(2 * y, 2)] = slope.reshape(2, ROWS, WIDTH)

    up_half(here.y)
    load_wd.wait()
    down_ring.finish()
    wd_flat = wd_all[...].reshape(WIDTH, WIDTH)
    sums[1].give(1, dot(half(gl_all, here.y), wd_flat, 1, 0))
    gather.rest()
    up_half(1 - here.y)
    sums[1].give(0, dot(half(gl_all, 1 - here.y), wd_flat, 1, 0))
    sums[1].cross()
    branch = sums[1].total()
    m_normed, m_inv = norm_parts(branch)
    act[...] = (res[2] + m_normed * vectors[6:7] + vectors[7:8]).astype(BF)
    load_cot.wait()
    upstream = cot[...].astype(F32)
    dm_all[here.member] = norm_pull(m_normed, m_inv, vectors[6:7], upstream).astype(BF)
    gather = GroupGather(here, post, dm_all)
    d_vec[6:7] = jnp.sum(upstream * m_normed, 0, keepdims=True)
    d_vec[7:8] = jnp.sum(upstream, 0, keepdims=True)
    gather.near()

    def du_half(y):
        d_gl = dot(half(dm_all, y), wd_flat, 1, 1)
        slope = slope_all[pl.ds(2 * y, 2)].reshape(2 * ROWS, WIDTH)
        du_all[pl.ds(2 * y, 2)] = (d_gl * slope).astype(BF).reshape(2, ROWS, WIDTH)

    du_half(here.y)
    sums[2].give(1, dot(half(du_all, here.y), wu_flat, 1, 1))
    gather.rest()
    du_half(1 - here.y)
    sums[2].give(0, dot(half(du_all, 1 - here.y), wu_flat, 1, 1))
    sums[2].cross()
    gl_flat = gl_all[...].reshape(512, WIDTH)
    dm_flat = dm_all[...].reshape(512, WIDTH)
    for shard in range(SPOTS):
        down_parts[shard] = dot(gl_flat[:, ROWS * shard : ROWS * (shard + 1)], dm_flat, 0, 0).astype(BF)
    down_sum = RingSum(here, post, down_parts, down_in)
    up_sum = RingSum(here, post, up_parts, up_in)
    out_sum = RingSum(here, post, out_parts, out_in)
    qkv_sum = RingSum(here, post, qkv_parts, qkv_in)
    down_sum.hop()
    du_flat = du_all[...].reshape(512, WIDTH)
    c_flat = c_all[...].reshape(512, WIDTH)
    for shard in range(SPOTS):
        up_parts[shard] = dot(c_flat[:, ROWS * shard : ROWS * (shard + 1)], du_flat, 0, 0).astype(BF)
    up_sum.hop()
    d_c = sums[2].total()
    h_normed = res[1]
    d_h = upstream + norm_pull(h_normed, h_inv, vectors[4:5], d_c)
    t_normed = res[0]
    dt_all[here.member] = norm_pull(t_normed, t_inv, vectors[2:3], d_h).astype(BF)
    gather = GroupGather(here, post, dt_all)
    d_vec[4:5] = jnp.sum(d_c * h_normed, 0, keepdims=True)
    d_vec[5:6] = jnp.sum(d_c, 0, keepdims=True)
    d_vec[2:3] = jnp.sum(d_h * t_normed, 0, keepdims=True)
    d_vec[3:4] = jnp.sum(d_h, 0, keepdims=True)
    res[2] = d_h
    down_sum.hop()
    gather.near()
    gather.rest()
    dt_flat = dt_all[...].reshape(512, WIDTH)
    d_o = dot(wo_flat, dt_flat, 1, 1)
    for head in range(4):
        do_send[head] = d_o[HD * head : HD * (head + 1)].astype(BF)
    swap = SwapAlongZ(here, post, local, do_send, do_heads)
    o_flat = o_all[...].reshape(256, 512)
    out_parts[...] = dot(o_flat, dt_flat, 1, 0).astype(BF).reshape(SPOTS, 32, WIDTH)
    up_sum.hop()
    out_sum.hop()
    swap.finish()
    down_sum.hop()
    for group in range(16):
        d_out[:, ROWS * group : ROWS * (group + 1)] = true_group(do_heads, group)
    grads[HD:] = jnp.zeros((2 * HD, 2048), F32)
    for query_at in range(0, 2048, 256):
        attend_back_block(qkv, start, o_true, lse, d_out, grads, query_at, 256)
        if query_at == 768:
            up_sum.hop()
        if query_at == 1280:
            down_sum.hop()
            out_sum.hop()
        if query_at == 1792:
            up_sum.hop()
    position = lax.broadcasted_iota(jnp.int32, (1, 2048), 1) - start[...]
    cos_t, sin_t = turn_tables(position.astype(F32))
    for part in range(2):
        first = grads[HD * part : HD * part + HD // 2]
        second = grads[HD * part + HD // 2 : HD * (part + 1)]
        grads[HD * part : HD * part + HD // 2] = first * cos_t + second * sin_t
        grads[HD * part + HD // 2 : HD * (part + 1)] = second * cos_t - first * sin_t
    for at in range(16):
        d_send[at // 4, :, 128 * (at % 4) : 128 * (at % 4) + 128] = stored_group(grads, at).astype(BF)
    swap = SwapAlongZ(here, post, local, d_send, d_in)
    out_sum.hop()
    low_half, high_half = down_sum.total()
    g_down[0:64] = low_half
    g_down[64:128] = high_half
    low_half, high_half = up_sum.total()
    for member in range(GROUP):
        halved = low_half if member < 2 else high_half
        up_send[member] = halved[32 * (member % 2) : 32 * (member % 2) + 32].astype(BF)
    up_got[here.member] = up_send[here.member]
    ends = []
    for member, place in here.mates():
        ends.append((post.send(up_send.at[member], up_got.at[here.member], place), up_got.at[member]))
    out_sum.hop()
    swap.finish()
    for part in range(3):
        for head in range(4):
            at = 256 * part + HD * head
            d_all[at : at + HD] = d_in[head, HD * part : HD * (part + 1)]
    for shard in range(SPOTS):
        qkv_parts[shard] = dot(a_t[ROWS * shard : ROWS * (shard + 1)], d_all[...], 1, 1).astype(BF)
    qkv_sum.hop()

    def in_half(y):
        return dot(d_all[:, half_lanes(y)], wqkv_flat, 0, 1)

    sums[3].give(0, in_half(1 - here.y))
    sums[3].give(1, in_half(here.y))
    sums[3].cross()
    qkv_sum.hop()
    low_half, high_half = out_sum.total()
    out_end[0:16] = low_half.astype(BF)
    out_end[16:32] = high_half.astype(BF)
    out_copy = pltpu.make_async_remote_copy(
        src_ref=out_end, dst_ref=out_got, send_sem=self_sems.at[3], recv_sem=self_sems.at[4],
        device_id=here.place(*out_from), device_id_type=MESH_ID,
    )
    pl.when(out_moves)(out_copy.start)

    @pl.when(out_stays)
    def _():
        out_got[...] = out_end[...]

    d_a = sums[3].total()
    normed, inv_std = norm_parts(tok[...].astype(F32))
    in_grad[...] = res[2] + norm_pull(normed, inv_std, vectors[0:1], d_a)
    d_vec[0:1] = jnp.sum(d_a * normed, 0, keepdims=True)
    d_vec[1:2] = jnp.sum(d_a, 0, keepdims=True)
    for shard in range(SPOTS):
        vec_send[shard] = d_vec[:, ROWS * shard : ROWS * (shard + 1)]
    vec_in[here.shard] = vec_send[here.shard]
    vec_sent = []
    for step in range(1, SPOTS):
        shard, place = here.plane(step)
        came = lax.rem(here.shard + SPOTS - step, SPOTS)
        vec_sent.append((post.send(vec_send.at[shard], vec_in.at[here.shard], place), vec_in.at[came]))
    qkv_sum.hop()
    for sent, landing in vec_sent:
        post.arrived(sent, landing)
    total = vec_in[0]
    for shard in range(1, SPOTS):
        total = total + vec_in[shard]
    vec_group[here.member] = total
    vec_sent = []
    for member, place in here.mates():
        mine = vec_group.at[here.member]
        vec_sent.append((post.send(mine, mine, place), vec_group.at[member]))
    qkv_sum.hop()
    for sent, landing in ends:
        post.arrived(sent, landing)

    @pl.when(out_moves)
    def _():
        out_copy.wait_recv()
        out_copy.wait_send()

    for sent, landing in vec_sent:
        post.arrived(sent, landing)
    total = vec_group[0] + vec_group[1] + vec_group[2] + vec_group[3]
    mine = total[:, 0:32]
    for member in range(1, GROUP):
        mine = jnp.where(here.member == member, total[:, 32 * member : 32 * (member + 1)], mine)
    g_vec[...] = mine
    low_half, high_half = qkv_sum.total()
    for member in range(GROUP):
        halved = low_half if member < 2 else high_half
        qkv_end[member] = halved[32 * (member % 2) : 32 * (member % 2) + 32].astype(BF)
    qkv_got[here.member] = qkv_end[here.member]
    ends = []
    for member, place in here.mates():
        ends.append((post.send(qkv_end.at[member], qkv_got.at[here.member], place), qkv_got.at[member]))
    for sent, landing in ends:
        post.arrived(sent, landing)
    post.finish()


def call_layer(*args):
    vmem = pl.BlockSpec(memory_space=pltpu.VMEM)
    anywhere = pl.BlockSpec(memory_space=pl.ANY)
    shape = jax.ShapeDtypeStruct
    dma = pltpu.SemaphoreType.DMA

    def held(*dims, kind=BF):
        return pltpu.VMEM(dims, kind)

    rows = (GROUP, ROWS, WIDTH)
    return pl.pallas_call(
        layer_kernel,
        out_shape=[
            shape((ROWS, WIDTH), BF),
            shape((ROWS, WIDTH), F32),
            shape((ROWS, WIDTH), F32),
            shape((GROUP, 32, WIDTH), BF),
            shape((GROUP, 32, 768), BF),
            shape((32, WIDTH), BF),
            shape((8, 32), F32),
        ],
        in_specs=[anywhere] * 9 + [vmem] * 8,
        out_specs=[vmem] * 7,
        scratch_shapes=[
            held(ROWS, WIDTH), held(ROWS, WIDTH), held(3, 32, WIDTH), held(32, 4 * WIDTH),
            held(1, ROWS, kind=jnp.int32),
            held(*rows), held(SPOTS, ROWS, 768), held(GROUP, 32, 768), held(GROUP, 32, WIDTH),
            held(ROWS, WIDTH), held(GROUP, 16, ROWS, kind=F32), held(SPOTS, 16, ROWS, kind=F32),
            held(32, WIDTH), held(SPOTS, 32, WIDTH), held(SPOTS, ROWS, WIDTH), held(SPOTS, ROWS, WIDTH),
            held(8, WIDTH, kind=F32), held(16, ROWS, kind=F32), held(1, 2048, kind=jnp.int32),
            held(WIDTH, 512), held(4, 192, 512), held(4, 192, 512), held(192, 2048),
            held(HD, 2048, kind=F32), held(1, 2048, kind=F32), held(4, HD, 512), held(4, HD, 512),
            held(*rows), held(*rows), held(*rows), held(*rows), held(*rows, kind=F32), held(*rows),
            held(3, ROWS, WIDTH, kind=F32),
            held(4, 2, ROWS, WIDTH), held(4, 2, ROWS, WIDTH), held(4, ROWS, WIDTH), held(4, ROWS, WIDTH),
            held(2, 2, ROWS, WIDTH, kind=F32),
            held(4, HD, 512), held(4, HD, 512), held(HD, 2048), held(192, 2048, kind=F32),
            held(4, 192, 512), held(4, 192, 512), held(768, 512),
            held(SPOTS, ROWS, WIDTH), held(14, ROWS // 2, WIDTH),
            held(SPOTS, ROWS, WIDTH), held(14, ROWS // 2, WIDTH),
            held(SPOTS, 32, WIDTH), held(14, 16, WIDTH),
            held(SPOTS, ROWS, 768), held(14, ROWS // 2, 768),
            held(SPOTS, 8, ROWS, kind=F32), held(SPOTS, 8, ROWS, kind=F32), held(GROUP, 8, ROWS, kind=F32),
            held(8, WIDTH, kind=F32), held(GROUP, 32, WIDTH), held(GROUP, 32, 768), held(32, WIDTH),
            dma((200,)), dma((200,)), dma((24,)), dma((5,)),
        ],
        compiler_params=pltpu.CompilerParams(
            collective_id=0, has_side_effects=True, vmem_limit_bytes=VMEM_BYTES
        ),
        name="layer",
    )(*args)


def finish_kernel(
    act_in, grad_in, down_in, up_got, qkv_got, out_got, vec,
    act, in_grad, g_q, g_k, g_v, g_out, g_up, g_down, *g_norms
):
    act[...] = act_in[...]
    in_grad[...] = grad_in[...]
    g_down[...] = down_in[...]
    g_out[...] = out_got[...].astype(F32)
    for member in range(GROUP):
        for shard in range(SPOTS):
            at = 512 * shard + 128 * member
            g_up[:, at : at + 128] = up_got[member, :, 128 * shard : 128 * (shard + 1)].astype(F32)
        base = 512 * (member % 2) + 256 * (member // 2)
        for slot, out in enumerate((g_q, g_k, g_v)):
            out[:, base : base + 256] = qkv_got[member, :, 256 * slot : 256 * (slot + 1)].astype(F32)
    for row, out in enumerate(g_norms):
        out[...] = vec[row : row + 1]


def call_finish(*args):
    vmem = pl.BlockSpec(memory_space=pltpu.VMEM)
    shape = jax.ShapeDtypeStruct
    narrow = shape((32, WIDTH), F32)
    return pl.pallas_call(
        finish_kernel,
        out_shape=[
            shape((ROWS, WIDTH), BF), shape((ROWS, WIDTH), F32), narrow, narrow, narrow, narrow,
            shape((32, 4 * WIDTH), F32), shape((ROWS, WIDTH), F32),
        ] + [shape((1, 32), F32)] * 8,
        in_specs=[vmem] * 7,
        out_specs=[vmem] * 16,
        compiler_params=pltpu.CompilerParams(vmem_limit_bytes=VMEM_BYTES // 2),
        name="finish",
    )(*args)


def on_device_grouped(tokens, segments, cotangent, *params):
    weights, norms = params[:6], params[6:]
    results = call_layer(
        tokens[0], segments, cotangent[0], *weights, *[vector[None] for vector in norms]
    )
    outs = call_finish(*results)
    act, in_grad, *rest = outs
    return (act[None], in_grad[None], *rest[:6]) + tuple(vector[0] for vector in rest[6:])


def solution(mesh):
    in_specs = (
        P("dp", "ctx", None),
        P("dp", "ctx"),
        P("dp", "ctx", None),
        P(("dp", "ctx"), None),
        P(("dp", "ctx"), None),
        P(("dp", "ctx"), None),
        P(("dp", "ctx"), None),
        P(("dp", "ctx"), None),
        P(("dp", "ctx"), None),
        P(("dp", "ctx")),
        P(("dp", "ctx")),
        P(("dp", "ctx")),
        P(("dp", "ctx")),
        P(("dp", "ctx")),
        P(("dp", "ctx")),
        P(("dp", "ctx")),
        P(("dp", "ctx")),
    )
    out_specs = (
        P("dp", "ctx", None),
        P("dp", "ctx", None),
        P(("dp", "ctx"), None),
        P(("dp", "ctx"), None),
        P(("dp", "ctx"), None),
        P(("dp", "ctx"), None),
        P(("dp", "ctx"), None),
        P(("dp", "ctx"), None),
        P(("dp", "ctx")),
        P(("dp", "ctx")),
        P(("dp", "ctx")),
        P(("dp", "ctx")),
        P(("dp", "ctx")),
        P(("dp", "ctx")),
        P(("dp", "ctx")),
        P(("dp", "ctx")),
    )
    grouped = mesh.shape["dp"] == 2 and mesh.shape["ctx"] == 16
    return jax.shard_map(
        on_device_grouped if grouped else on_device, mesh=mesh, in_specs=in_specs, out_specs=out_specs, check_vma=False
    )
```

```python
import math

import jax
import jax.numpy as jnp
from jax import lax
from jax.experimental import pallas as pl
from jax.experimental.pallas import tpu as pltpu
from jax.sharding import PartitionSpec as P

HEADS = 16
HD = 64


norm_eps = 1e-05
masked_value = -1e30


def layer_norm(value, gain, bias):
    row_mean = jnp.mean(value, -1, keepdims=True)
    centred = value - row_mean
    scaled = centred * lax.rsqrt(jnp.mean(centred * centred, -1, keepdims=True) + norm_eps)
    return scaled * gain + bias


def norm_back(value, gain, upstream):
    row_mean = jnp.mean(value, -1, keepdims=True)
    centred = value - row_mean
    inv_std = lax.rsqrt(jnp.mean(centred * centred, -1, keepdims=True) + norm_eps)
    normed = centred * inv_std
    d_normed = upstream * gain
    d_value = inv_std * (
        d_normed
        - jnp.mean(d_normed, -1, keepdims=True)
        - normed * jnp.mean(d_normed * normed, -1, keepdims=True)
    )
    return (d_value, jnp.sum(upstream * normed, 0), jnp.sum(upstream, 0))


def rope_tables(offsets, head_dim):
    freq = 10000.0 ** (-jnp.arange(head_dim // 2, dtype=jnp.float32) / (head_dim // 2))
    angle = offsets.astype(jnp.float32)[..., None] * freq
    return (jnp.cos(angle)[..., None, :], jnp.sin(angle)[..., None, :])


def rotate(values, cos_t, sin_t):
    half_dim = values.shape[-1] // 2
    first = values[..., :half_dim]
    second = values[..., half_dim:]
    return jnp.concatenate([first * cos_t - second * sin_t, second * cos_t + first * sin_t], -1)


def unrotate(grads, cos_t, sin_t):
    half_dim = grads.shape[-1] // 2
    first = grads[..., :half_dim]
    second = grads[..., half_dim:]
    return jnp.concatenate([first * cos_t + second * sin_t, second * cos_t - first * sin_t], -1)


def true_position(flat_index, row_count, ctx_size):
    device_of = flat_index // row_count
    offset_in = flat_index % row_count
    half_rows = row_count // 2
    return jnp.where(
        offset_in < half_rows,
        device_of * half_rows + offset_in,
        (2 * ctx_size - 1 - device_of) * half_rows + offset_in - half_rows,
    )


def split_blocks(array, block_rows):
    return array.reshape((array.shape[0] // block_rows, block_rows) + array.shape[1:])


def score_block(queries, keys, query_pos, query_seg, key_pos, key_seg):
    scores = jnp.einsum(
        "qhd,khd->hqk", queries, keys, preferred_element_type=jnp.float32
    ) * queries.shape[-1] ** (-0.5)
    allowed = (query_seg[:, None] == key_seg[None, :]) & (key_pos[None, :] <= query_pos[:, None])
    return (scores, allowed[None])


def grad_block(queries, d_attn, lse, delta, keys, values, query_pos, query_seg, key_pos, key_seg):
    scores, allowed = score_block(queries, keys, query_pos, query_seg, key_pos, key_seg)
    attn_probs = jnp.where(allowed, jnp.exp(scores - lse[:, :, None]), 0.0)
    d_probs = jnp.einsum("qhd,khd->hqk", d_attn, values, preferred_element_type=jnp.float32)
    d_scores = (attn_probs * (d_probs - delta[:, :, None])).astype(jnp.bfloat16)
    return (attn_probs, d_scores)


def key_terms(
    query_rows,
    dattn_rows,
    lse_rows,
    delta_rows,
    query_pos,
    query_seg,
    key_block,
    value_block,
    key_pos,
    key_seg,
):
    attn_probs, d_scores = grad_block(
        query_rows,
        dattn_rows,
        lse_rows,
        delta_rows,
        key_block,
        value_block,
        query_pos,
        query_seg,
        key_pos,
        key_seg,
    )
    d_keys = jnp.einsum(
        "hqk,qhd->khd", d_scores, query_rows, preferred_element_type=jnp.float32
    ) * query_rows.shape[-1] ** (-0.5)
    d_values = jnp.einsum(
        "hqk,qhd->khd",
        attn_probs.astype(jnp.bfloat16),
        dattn_rows,
        preferred_element_type=jnp.float32,
    )
    return (d_keys, d_values)


def on_device(
    tokens,
    segments,
    cotangent,
    w_query,
    w_key,
    w_value,
    w_out,
    w_up,
    w_down,
    gain_attn_in,
    bias_attn_in,
    gain_attn_out,
    bias_attn_out,
    gain_mlp_in,
    bias_mlp_in,
    gain_mlp_out,
    bias_mlp_out,
):
    whole = (
        lax.all_gather(w_query, ("dp", "ctx"), axis=0, tiled=True),
        lax.all_gather(w_key, ("dp", "ctx"), axis=0, tiled=True),
        lax.all_gather(w_value, ("dp", "ctx"), axis=0, tiled=True),
        lax.all_gather(w_out, ("dp", "ctx"), axis=0, tiled=True),
        lax.all_gather(w_up, ("dp", "ctx"), axis=0, tiled=True),
        lax.all_gather(w_down, ("dp", "ctx"), axis=0, tiled=True),
        lax.all_gather(gain_attn_in, ("dp", "ctx"), axis=0, tiled=True),
        lax.all_gather(bias_attn_in, ("dp", "ctx"), axis=0, tiled=True),
        lax.all_gather(gain_attn_out, ("dp", "ctx"), axis=0, tiled=True),
        lax.all_gather(bias_attn_out, ("dp", "ctx"), axis=0, tiled=True),
        lax.all_gather(gain_mlp_in, ("dp", "ctx"), axis=0, tiled=True),
        lax.all_gather(bias_mlp_in, ("dp", "ctx"), axis=0, tiled=True),
        lax.all_gather(gain_mlp_out, ("dp", "ctx"), axis=0, tiled=True),
        lax.all_gather(bias_mlp_out, ("dp", "ctx"), axis=0, tiled=True),
    )
    query_w, key_w, value_w, out_w, up_w, down_w = whole[:6]
    gain_ai, bias_ai, gain_ao, bias_ao, gain_mi, bias_mi, gain_mo, bias_mo = [
        entry.astype(jnp.float32) for entry in whole[6:]
    ]
    row_count = tokens.shape[1]
    model_width = tokens.shape[2]
    ctx_size = lax.axis_size("ctx")
    seq_length = row_count * ctx_size
    score_scale = HD ** (-0.5)
    seg_all = lax.all_gather(segments, "ctx", axis=1, tiled=True)[0]
    my_seg = segments[0]
    all_pos = true_position(jnp.arange(seq_length, dtype=jnp.int32), row_count, ctx_size)
    my_pos = true_position(
        lax.axis_index("ctx") * row_count + jnp.arange(row_count, dtype=jnp.int32),
        row_count,
        ctx_size,
    )
    doc_first = jnp.min(
        jnp.where(seg_all[None, :] == my_seg[:, None], all_pos[None, :], seq_length), axis=1
    )
    cos_t, sin_t = rope_tables(my_pos - doc_first, HD)
    inputs = tokens[0].astype(jnp.float32)
    attn_in = layer_norm(inputs, gain_ai, bias_ai).astype(jnp.bfloat16)
    query_pre = jnp.dot(attn_in, query_w, preferred_element_type=jnp.float32).reshape(
        row_count, HEADS, HD
    )
    key_pre = jnp.dot(attn_in, key_w, preferred_element_type=jnp.float32).reshape(
        row_count, HEADS, HD
    )
    queries = rotate(query_pre, cos_t, sin_t).astype(jnp.bfloat16)
    keys_rot = rotate(key_pre, cos_t, sin_t).astype(jnp.bfloat16)
    values_flat = jnp.dot(attn_in, value_w, preferred_element_type=jnp.float32).astype(jnp.bfloat16)
    values_heads = values_flat.reshape(row_count, HEADS, HD)
    keys_flat = keys_rot.reshape(row_count, model_width)
    start_state = (
        jnp.full((HEADS, row_count), masked_value, jnp.float32),
        jnp.zeros((HEADS, row_count), jnp.float32),
        jnp.zeros((row_count, HEADS, HD), jnp.float32),
    )
    key_rows = lax.all_gather(keys_flat, "ctx", axis=0, tiled=True)
    value_rows = lax.all_gather(values_flat, "ctx", axis=0, tiled=True)
    span = key_rows.shape[0]
    block_rows = math.gcd(span, 1024)
    key_pos = true_position(jnp.arange(span, dtype=jnp.int32), row_count, ctx_size)
    key_seg = seg_all

    def visit(state_now, parts):
        row_top, row_total, weighted = state_now
        key_block = parts[0].reshape(block_rows, HEADS, HD)
        value_block = parts[1].reshape(block_rows, HEADS, HD)
        scores, allowed = score_block(queries, key_block, my_pos, my_seg, parts[2], parts[3])
        top_new = jnp.maximum(row_top, jnp.max(jnp.where(allowed, scores, masked_value), -1))
        fade = jnp.exp(row_top - top_new)
        attn_probs = jnp.where(allowed, jnp.exp(scores - top_new[:, :, None]), 0.0)
        row_total = row_total * fade + jnp.sum(attn_probs, -1)
        weighted = weighted * fade.T[:, :, None] + jnp.einsum(
            "hqk,khd->qhd",
            attn_probs.astype(jnp.bfloat16),
            value_block,
            preferred_element_type=jnp.float32,
        )
        return ((top_new, row_total, weighted), None)

    blocks = (
        split_blocks(key_rows, block_rows),
        split_blocks(value_rows, block_rows),
        split_blocks(key_pos, block_rows),
        split_blocks(key_seg, block_rows),
    )
    row_top, row_total, weighted = lax.scan(visit, start_state, blocks)[0]
    lse = row_top + jnp.log(row_total)
    attn_f = weighted / row_total.T[:, :, None]
    attn_b = attn_f.reshape(row_count, model_width).astype(jnp.bfloat16)
    branch = jnp.dot(attn_b, out_w, preferred_element_type=jnp.float32)
    resid = inputs + layer_norm(branch, gain_ao, bias_ao)
    mlp_in = layer_norm(resid, gain_mi, bias_mi).astype(jnp.bfloat16)
    hidden_pre = jnp.dot(mlp_in, up_w, preferred_element_type=jnp.float32)
    hidden = jax.nn.gelu(hidden_pre, approximate=True).astype(jnp.bfloat16)
    mlp_out = jnp.dot(hidden, down_w, preferred_element_type=jnp.float32)
    result = resid + layer_norm(mlp_out, gain_mo, bias_mo)
    upstream = cotangent[0].astype(jnp.float32)
    d_mlp_out, dgain_mo, dbias_mo = norm_back(mlp_out, gain_mo, upstream)
    d_mlp_b = d_mlp_out.astype(jnp.bfloat16)
    grad_down = jnp.dot(hidden.T, d_mlp_b, preferred_element_type=jnp.float32)
    d_hidden = jnp.dot(d_mlp_b, down_w.T, preferred_element_type=jnp.float32)
    gelu_back = jax.vjp(lambda pre: jax.nn.gelu(pre, approximate=True), hidden_pre)[1]
    d_pre = gelu_back(d_hidden)[0].astype(jnp.bfloat16)
    grad_up = jnp.dot(mlp_in.T, d_pre, preferred_element_type=jnp.float32)
    d_mlp_in = jnp.dot(d_pre, up_w.T, preferred_element_type=jnp.float32)
    d_resid_n, dgain_mi, dbias_mi = norm_back(resid, gain_mi, d_mlp_in)
    d_resid = upstream + d_resid_n
    d_branch, dgain_ao, dbias_ao = norm_back(branch, gain_ao, d_resid)
    d_branch_b = d_branch.astype(jnp.bfloat16)
    grad_out = jnp.dot(attn_b.T, d_branch_b, preferred_element_type=jnp.float32)
    d_attn_flat = jnp.dot(d_branch_b, out_w.T, preferred_element_type=jnp.float32).astype(
        jnp.bfloat16
    )
    d_attn = d_attn_flat.reshape(row_count, HEADS, HD)
    delta = jnp.sum(d_attn.astype(jnp.float32) * attn_f, -1).T
    zero_heads = jnp.zeros((row_count, HEADS, HD), jnp.float32)

    def query_grad(dq_now, key_rows, value_rows, key_pos, key_seg):
        block_rows = math.gcd(key_rows.shape[0], 1024)

        def visit(dq_run, parts):
            key_block = parts[0].reshape(block_rows, HEADS, HD)
            value_block = parts[1].reshape(block_rows, HEADS, HD)
            d_scores = grad_block(
                queries,
                d_attn,
                lse,
                delta,
                key_block,
                value_block,
                my_pos,
                my_seg,
                parts[2],
                parts[3],
            )[1]
            return (
                dq_run
                + jnp.einsum(
                    "hqk,khd->qhd", d_scores, key_block, preferred_element_type=jnp.float32
                )
                * score_scale,
                None,
            )

        blocks = (
            split_blocks(key_rows, block_rows),
            split_blocks(value_rows, block_rows),
            split_blocks(key_pos, block_rows),
            split_blocks(key_seg, block_rows),
        )
        return lax.scan(visit, dq_now, blocks)[0]

    lse_all, delta_all = (
        lax.all_gather(lse.T, "ctx", axis=0, tiled=True),
        lax.all_gather(delta.T, "ctx", axis=0, tiled=True),
    )
    query_rows = lax.all_gather(queries.reshape(row_count, model_width), "ctx", axis=0, tiled=True)
    dattn_rows = lax.all_gather(d_attn_flat, "ctx", axis=0, tiled=True)
    span = query_rows.shape[0]
    query_block_rows = math.gcd(span, 1024)
    query_pos = true_position(jnp.arange(span, dtype=jnp.int32), row_count, ctx_size)

    def visit(sums, parts):
        d_keys, d_values = key_terms(
            parts[0].reshape(query_block_rows, HEADS, HD),
            parts[1].reshape(query_block_rows, HEADS, HD),
            parts[2].T,
            parts[3].T,
            parts[4],
            parts[5],
            keys_rot,
            values_heads,
            my_pos,
            my_seg,
        )
        return ((sums[0] + d_keys, sums[1] + d_values), None)

    blocks = (
        split_blocks(query_rows, query_block_rows),
        split_blocks(dattn_rows, query_block_rows),
        split_blocks(lse_all, query_block_rows),
        split_blocks(delta_all, query_block_rows),
        split_blocks(query_pos, query_block_rows),
        split_blocks(seg_all, query_block_rows),
    )
    dk_rot, dv_sum = lax.scan(visit, (zero_heads, zero_heads), blocks)[0]
    pieces = (
        lax.all_gather(keys_flat, "ctx", axis=0, tiled=True),
        lax.all_gather(values_flat, "ctx", axis=0, tiled=True),
    )
    span = pieces[0].shape[0]
    key_pos = true_position(jnp.arange(span, dtype=jnp.int32), row_count, ctx_size)
    key_seg = seg_all
    dq_rot = query_grad(zero_heads, pieces[0], pieces[1], key_pos, key_seg)
    d_query = unrotate(dq_rot, cos_t, sin_t).reshape(row_count, model_width).astype(jnp.bfloat16)
    d_key = unrotate(dk_rot, cos_t, sin_t).reshape(row_count, model_width).astype(jnp.bfloat16)
    d_value = dv_sum.reshape(row_count, model_width).astype(jnp.bfloat16)
    grad_query = jnp.dot(attn_in.T, d_query, preferred_element_type=jnp.float32)
    grad_key = jnp.dot(attn_in.T, d_key, preferred_element_type=jnp.float32)
    grad_value = jnp.dot(attn_in.T, d_value, preferred_element_type=jnp.float32)
    d_attn_in = (
        jnp.dot(d_query, query_w.T, preferred_element_type=jnp.float32)
        + jnp.dot(d_key, key_w.T, preferred_element_type=jnp.float32)
        + jnp.dot(d_value, value_w.T, preferred_element_type=jnp.float32)
    )
    d_inputs_n, dgain_ai, dbias_ai = norm_back(inputs, gain_ai, d_attn_in)
    input_grad = (d_resid + d_inputs_n)[None]
    shares = (
        lax.psum_scatter(grad_query, ("dp", "ctx"), scatter_dimension=0, tiled=True),
        lax.psum_scatter(grad_key, ("dp", "ctx"), scatter_dimension=0, tiled=True),
        lax.psum_scatter(grad_value, ("dp", "ctx"), scatter_dimension=0, tiled=True),
        lax.psum_scatter(grad_out, ("dp", "ctx"), scatter_dimension=0, tiled=True),
        lax.psum_scatter(grad_up, ("dp", "ctx"), scatter_dimension=0, tiled=True),
        lax.psum_scatter(grad_down, ("dp", "ctx"), scatter_dimension=0, tiled=True),
        lax.psum_scatter(dgain_ai, ("dp", "ctx"), scatter_dimension=0, tiled=True),
        lax.psum_scatter(dbias_ai, ("dp", "ctx"), scatter_dimension=0, tiled=True),
        lax.psum_scatter(dgain_ao, ("dp", "ctx"), scatter_dimension=0, tiled=True),
        lax.psum_scatter(dbias_ao, ("dp", "ctx"), scatter_dimension=0, tiled=True),
        lax.psum_scatter(dgain_mi, ("dp", "ctx"), scatter_dimension=0, tiled=True),
        lax.psum_scatter(dbias_mi, ("dp", "ctx"), scatter_dimension=0, tiled=True),
        lax.psum_scatter(dgain_mo, ("dp", "ctx"), scatter_dimension=0, tiled=True),
        lax.psum_scatter(dbias_mo, ("dp", "ctx"), scatter_dimension=0, tiled=True),
    )
    return (result.astype(jnp.bfloat16)[None], input_grad) + tuple(shares)


BF = jnp.bfloat16
F32 = jnp.float32
MESH_ID = pl.DeviceIdType.MESH
GROUP = 4
SPOTS = 8
ROWS = 128
WIDTH = 1024
VMEM_BYTES = 60 << 20


def dot(left, right, left_dim, right_dim):
    return lax.dot_general(
        left, right, (((left_dim,), (right_dim,)), ((), ())), preferred_element_type=F32
    )


class Here:
    def __init__(self):
        self.x = lax.axis_index("dp")
        at = lax.axis_index("ctx")
        self.high, self.low, self.y, self.c = at // 8, (at // 4) % 2, (at // 2) % 2, at % 2
        self.member = 2 * self.low + self.c
        self.tokens = 2 * self.high + self.y
        self.shard = 4 * self.x + self.tokens
        self.core_mate = self.place(self.x, self.high, self.low, self.y, 1 - self.c)
        self.link_mate = self.place(self.x, self.high, 1 - self.low, self.y, self.c)
        self.far_mate = self.place(self.x, self.high, 1 - self.low, self.y, 1 - self.c)
        self.core_member = 2 * self.low + (1 - self.c)
        self.link_member = 2 * (1 - self.low) + self.c
        self.far_member = 2 * (1 - self.low) + (1 - self.c)

    @staticmethod
    def place(x, high, low, y, c):
        return (x, 8 * high + 4 * low + 2 * y + c)

    def across(self, axes):
        x = 1 - self.x if "x" in axes else self.x
        y = 1 - self.y if "y" in axes else self.y
        high = 1 - self.high if "z" in axes else self.high
        return 4 * x + 2 * high + y, self.place(x, high, self.low, y, self.c)

    def plane(self, step):
        shard = lax.rem(self.shard + step, SPOTS)
        return shard, self.place(shard // 4, (shard // 2) % 2, self.low, shard % 2, self.c)

    def in_sequence(self, step):
        group = lax.rem(self.tokens + step, 4)
        return group, self.place(self.x, group // 2, self.low, group % 2, self.c)

    def mates(self):
        return (
            (self.core_member, self.core_mate),
            (self.link_member, self.link_mate),
            (self.far_member, self.far_mate),
        )


def device_of(shard, member):
    return 8 * (shard // 2) + 4 * (member // 2) + 2 * (shard % 2) + member % 2


def row_piece(held, shard, half):
    return held.at[shard, half]


def group_piece(held, shard, half):
    return held.at[shard // 2, half, shard % 2]


class Post:
    def __init__(self, send_sems, recv_sems):
        self.send_sems, self.recv_sems = send_sems, recv_sems
        self.count = 0
        self.started = []

    def send(self, src, dst, to):
        copy = pltpu.make_async_remote_copy(
            src_ref=src,
            dst_ref=dst,
            send_sem=self.send_sems.at[self.count],
            recv_sem=self.recv_sems.at[self.count],
            device_id=to,
            device_id_type=MESH_ID,
        )
        copy.start()
        self.started.append(copy)
        self.count += 1
        assert self.count <= self.send_sems.shape[0]
        return self.count - 1, to

    def arrived(self, sent, landing):
        number, to = sent
        pltpu.make_async_remote_copy(
            src_ref=landing,
            dst_ref=landing,
            send_sem=self.send_sems.at[number],
            recv_sem=self.recv_sems.at[number],
            device_id=to,
            device_id_type=MESH_ID,
        ).wait_recv()

    def finish(self):
        for copy in self.started:
            copy.wait_send()


class Local:
    def __init__(self, sems):
        self.sems = sems
        self.started = []

    def copy(self, src, dst):
        copy = pltpu.make_async_copy(src, dst, self.sems.at[len(self.started)])
        copy.start()
        self.started.append(copy)
        return copy


class CubeGather:
    def __init__(self, here, post, held, piece, own=None):
        self.here, self.post, self.held, self.piece, self.own = here, post, held, piece, own
        self.waiting = {}

    def move(self, axes, half, way):
        here = self.here
        mine = self.piece(self.held, here.across(axes)[0], half)
        src = mine if axes or self.own is None else self.own(half)
        sent = self.post.send(src, mine, here.across(way)[1])
        axes = "".join(sorted(set(axes) ^ set(way)))
        self.waiting[axes, half] = (sent, self.piece(self.held, here.across(axes)[0], half))

    def take(self, axes, half):
        self.post.arrived(*self.waiting.pop((axes, half)))

    def start(self, ways="zxy"):
        for way in ways:
            for half in (0, 1):
                self.move("", half, way)

    def corners(self):
        self.take("x", 0)
        self.move("x", 0, "y")
        self.take("y", 1)
        self.move("y", 1, "x")

    def spread(self):
        for half in (0, 1):
            self.take("z", half)
            self.move("z", half, "x")
            self.move("z", half, "y")

    def last(self):
        self.take("xz", 0)
        self.move("xz", 0, "y")
        self.take("yz", 1)
        self.move("yz", 1, "x")

    def finish(self):
        for key in list(self.waiting):
            self.take(*key)


class CubeSum:
    def __init__(self, here, post, parts, piece, landing):
        self.here, self.post, self.parts, self.piece, self.landing = here, post, parts, piece, landing
        self.waiting = {}
        self.slots = 0
        self.hops = 0

    def part(self, axes, half):
        return self.piece(self.parts, self.here.across(axes)[0], half)

    def move(self, axes, half, way):
        src = self.part(axes, half)
        came = self.waiting.pop((axes, half), [])
        if came:
            value = src[...].astype(F32)
            for sent, slot in came:
                self.post.arrived(sent, slot)
                value = value + slot[...].astype(F32)
            src = came[0][1]
            src[...] = value.astype(src.dtype)
        slot = self.landing.at[self.slots]
        self.slots += 1
        sent = self.post.send(src, slot, self.here.across(way)[1])
        axes = "".join(sorted(set(axes) ^ set(way)))
        self.waiting.setdefault((axes, half), []).append((sent, slot))

    def hop(self):
        self.hops += 1
        if self.hops == 1:
            for axes in ("xyz", "xy"):
                self.move(axes, 0, "y")
                self.move(axes, 1, "x")
        if self.hops == 2:
            for axes in ("z", ""):
                self.move("x" + axes, 1, "x")
                self.move("y" + axes, 0, "y")
                self.move("x" + axes, 0, "x")
                self.move("y" + axes, 1, "y")
        if self.hops == 3:
            self.move("z", 0, "z")
            self.move("z", 1, "z")

    def total(self):
        halves = []
        for half in (0, 1):
            value = self.part("", half)[...].astype(F32)
            for sent, slot in self.waiting.pop(("", half)):
                self.post.arrived(sent, slot)
                value = value + slot[...].astype(F32)
            halves.append(value)
        return halves


class GroupGather:
    def __init__(self, here, post, held):
        self.here, self.post, self.held = here, post, held
        self.over = []
        for half in (0, 1):
            mine = self.piece(here.member, half)
            self.over.append(post.send(mine, mine, here.link_mate))
        mine = held.at[here.member]
        self.core = post.send(mine, mine, here.core_mate)

    def piece(self, member, half):
        return self.held.at[member, pl.ds(64 * half, 64)]

    def near(self):
        self.post.arrived(self.core, self.held.at[self.here.core_member])

    def rest(self):
        here, passed = self.here, []
        for half in (0, 1):
            linked = self.piece(here.link_member, half)
            self.post.arrived(self.over[half], linked)
            passed.append(self.post.send(linked, linked, here.core_mate))
        for half in (0, 1):
            self.post.arrived(passed[half], self.piece(here.far_member, half))


class GroupSum:
    def __init__(self, here, post, near_send, near_in, far_send, far_in, terms):
        self.here, self.post = here, post
        self.near_send, self.near_in = near_send, near_in
        self.far_send, self.far_in = far_send, far_in
        self.terms = terms
        self.near = [None, None]

    def give(self, slot, value):
        here = self.here
        self.terms[slot] = value.reshape(2, ROWS, WIDTH)
        self.near_send[slot] = self.terms[slot, 1 - here.c].astype(BF)
        self.near[slot] = self.post.send(
            self.near_send.at[slot], self.near_in.at[slot], here.core_mate
        )

    def cross(self):
        here = self.here
        self.post.arrived(self.near[0], self.near_in.at[0])
        self.far_send[...] = (self.terms[0, here.c] + self.near_in[0].astype(F32)).astype(BF)
        self.far = self.post.send(self.far_send, self.far_in, here.link_mate)

    def total(self):
        self.post.arrived(self.near[1], self.near_in.at[1])
        value = self.terms[1, self.here.c] + self.near_in[1].astype(F32)
        self.post.arrived(self.far, self.far_in)
        return value + self.far_in[...].astype(F32)


class Swap:
    def __init__(self, here, post, local, src, dst):
        self.post = post
        self.sent = []
        for step in (2, 1, 3):
            group, place = here.in_sequence(step)
            came = lax.rem(here.tokens + 4 - step, 4)
            self.sent.append((post.send(src.at[group], dst.at[here.tokens], place), dst.at[came]))
        self.own = local.copy(src.at[here.tokens], dst.at[here.tokens])

    def finish(self):
        self.own.wait()
        for sent, landing in self.sent:
            self.post.arrived(sent, landing)


def out_rows_target(here):
    return here.low, here.y, here.x, here.c, here.high


def out_rows_source(here):
    return here.low, here.c, here.x, here.high, here.y


def same_place(here, spot):
    x, high, low, y, c = spot
    return (x == here.x) & (high == here.high) & (low == here.low) & (y == here.y) & (c == here.c)


def turn_tables(rot):
    index = lax.broadcasted_iota(jnp.int32, (HD // 2, 1), 0).astype(F32)
    angle = rot * jnp.exp(index * (-math.log(10000.0) / (HD // 2)))
    return jnp.cos(angle), jnp.sin(angle)


def norm_parts(value):
    centred = value - jnp.mean(value, -1, keepdims=True)
    inv_std = lax.rsqrt(jnp.mean(centred * centred, -1, keepdims=True) + norm_eps)
    return centred * inv_std, inv_std


def norm_pull(normed, inv_std, gain, upstream):
    d_normed = upstream * gain
    return inv_std * (
        d_normed
        - jnp.mean(d_normed, -1, keepdims=True)
        - normed * jnp.mean(d_normed * normed, -1, keepdims=True)
    )


def stored_at(at):
    return 2 * (at // 8) + (at // 2) % 2, 2 * ((at // 4) % 2) + at % 2


def true_group(ref, group):
    def chunk(at, late):
        tokens, member = stored_at(at)
        tile = ref[tokens, :, ROWS * member : ROWS * (member + 1)]
        return tile[:, 64:] if late else tile[:, :64]

    if group < 8:
        return jnp.concatenate([chunk(2 * group, False), chunk(2 * group + 1, False)], 1)
    return jnp.concatenate([chunk(31 - 2 * group, True), chunk(30 - 2 * group, True)], 1)


def put_stored(ref, at, values):
    def block(number):
        tile = values[:, ROWS * (number // 2) : ROWS * (number // 2) + ROWS]
        return tile[:, 64:] if number % 2 else tile[:, :64]

    tokens, member = stored_at(at)
    ref[tokens, :, ROWS * member : ROWS * (member + 1)] = jnp.concatenate(
        [block(at), block(31 - at)], 1
    ).astype(BF)


def allowed_pairs(key_at, keys, query_at, queries, start):
    key_pos = key_at + lax.broadcasted_iota(jnp.int32, (keys, queries), 0)
    allowed = key_pos >= start
    if key_at + keys > query_at:
        allowed &= key_pos <= query_at + lax.broadcasted_iota(jnp.int32, (keys, queries), 1)
    return allowed


def attend_block(qkv, start, o_true, lse, query_at, queries, keys):
    here = slice(query_at, query_at + queries)
    query, first = qkv[0:HD, here], start[:, here]
    parts, top = [], None
    for key_at in range(0, query_at + queries, keys):
        scores = dot(qkv[HD : 2 * HD, key_at : key_at + keys], query, 0, 0)
        scores = jnp.where(
            allowed_pairs(key_at, keys, query_at, queries, first), scores, masked_value
        )
        peak = jnp.max(scores, 0, keepdims=True)
        top = peak if top is None else jnp.maximum(top, peak)
        parts.append((key_at, scores))
    total, weighted = 0.0, 0.0
    for key_at, scores in parts:
        probs = jnp.exp(scores - top)
        total = total + jnp.sum(probs, 0, keepdims=True)
        weighted = weighted + dot(qkv[2 * HD :, key_at : key_at + keys], probs.astype(BF), 1, 0)
    o_true[:, here] = weighted / total
    lse[:, here] = top + jnp.log(total)


def attend_back_block(qkv, start, o_true, lse, d_out, grads, query_at, queries):
    here = slice(query_at, query_at + queries)
    reach = slice(0, query_at + queries)
    query, d_attn = qkv[0:HD, here], d_out[:, here]
    key = qkv[HD : 2 * HD, reach]
    delta = jnp.sum(d_attn.astype(F32) * o_true[:, here], 0, keepdims=True)
    allowed = allowed_pairs(0, query_at + queries, query_at, queries, start[:, here])
    probs = jnp.where(allowed, jnp.exp(dot(key, query, 0, 0) - lse[:, here]), 0.0)
    d_probs = dot(qkv[2 * HD :, reach], d_attn, 0, 0)
    d_scores = (probs * (d_probs - delta)).astype(BF)
    grads[HD : 2 * HD, reach] += dot(query, d_scores, 1, 1)
    grads[2 * HD :, reach] += dot(d_attn, probs.astype(BF), 1, 1)
    grads[0:HD, here] = dot(key, d_scores, 1, 0) * HD**-0.5


GELU_K = math.sqrt(2.0 / math.pi)


def gelu_and_slope(pre):
    square = pre * pre
    bend = jnp.tanh(GELU_K * pre * (1.0 + 0.044715 * square))
    half = 0.5 * (1.0 + bend)
    slope = half + 0.5 * pre * (1.0 - bend * bend) * GELU_K * (1.0 + 3 * 0.044715 * square)
    return pre * half, slope


def layer_kernel(
    tok_hbm, seg_hbm, cot_hbm, wq, wk, wv, wo, wu, wd, *rest
):
    norms_hbm = rest[:8]
    act, in_grad, g_down, up_got, qkv_got, out_got, g_vec = rest[8:15]
    (
        tok, cot, wqkv_own, wu_own, seg_in, norms_in,
        x_all, wqkv, wqkv_send, wu_send, small_in, small_all, wo_in, wo_all, wu_all, wd_all,
        vectors, starts, start, a_t, qkv_send, qkv_heads, qkv, o_true, lse, o_send, o_all,
        c_all, dm_all, dt_all, gl_all, slope_all, du_all, res,
        near_send, near_in, far_send, far_in, terms,
        do_send, do_heads, d_out, grads, d_send, d_in, d_all,
        down_parts, down_in, up_parts, up_in, out_parts, out_in, qkv_parts, qkv_in,
        vec_send, vec_in, vec_group, d_vec, up_send, qkv_end, out_end,
        send_sems, recv_sems, local_sems, self_sems,
    ) = rest[15:]
    here = Here()
    post = Post(send_sems, recv_sems)
    local = Local(local_sems)
    out_to, out_from = out_rows_target(here), out_rows_source(here)
    out_stays = same_place(here, out_to)
    out_moves = jnp.logical_not(out_stays)
    barrier = pltpu.get_barrier_semaphore()
    partners = [place for _, place in here.mates()] + [here.plane(n)[1] for n in range(1, SPOTS)]
    for place in partners:
        pl.semaphore_signal(barrier, inc=1, device_id=place, device_id_type=MESH_ID)

    @pl.when(out_moves)
    def _():
        for spot in (out_from, out_to):
            pl.semaphore_signal(
                barrier, inc=1, device_id=here.place(*spot), device_id_type=MESH_ID
            )

    loads = [
        local.copy(weight, wqkv_own.at[slot]) for slot, weight in enumerate((wq, wk, wv))
    ]
    load_wu = local.copy(wu, wu_own)
    load_seg = local.copy(seg_hbm, seg_in)
    load_norms = [local.copy(vector, norms_in.at[row]) for row, vector in enumerate(norms_hbm)]
    load_tok = local.copy(tok_hbm, tok)
    load_cot = local.copy(cot_hbm, cot)
    load_wd = [
        local.copy(wd.at[pl.ds(64 * half, 64)], wd_all.at[here.shard, half]) for half in (0, 1)
    ]

    lane = lax.broadcasted_iota(jnp.int32, (1, ROWS), 1)
    for row, load in enumerate(load_norms):
        load.wait()
        value = norms_in[row].astype(F32)
        value = jnp.concatenate([value] * GROUP, 1)
        small_in[here.member, row : row + 1] = jnp.where(lane // 32 == here.member, value, 0.0)
    load_seg.wait()
    small_in[here.member, 8:9] = seg_in[...].astype(F32)
    for load in loads:
        load.wait()
    for member in range(GROUP):
        base = 256 * member
        for part in range(3):
            wqkv_send[part, member] = wqkv_own[part, :, base : base + 256]
    def member_rows(held, member):
        at = pl.ds(pl.multiple_of(32 * (member % 2), 32), 32)
        return held.at[here.shard // 2, member // 2, here.shard % 2, at]

    for part in range(3):
        member_rows(wqkv.at[part], here.member)[...] = wqkv_send[part, here.member]
    load_tok.wait()
    x_all[here.member] = tok[...]

    @pl.when(out_stays)
    def _():
        pl.semaphore_wait(barrier, len(partners))

    @pl.when(out_moves)
    def _():
        pl.semaphore_wait(barrier, len(partners) + 2)

    small_sent, wqkv_sent, wu_sent = [], [], []
    for member, place in here.mates():
        mine = small_in.at[here.member]
        small_sent.append((post.send(mine, mine, place), small_in.at[member]))
    for part in range(3):
        for member, place in here.mates():
            mine, theirs = (member_rows(wqkv.at[part], who) for who in (here.member, member))
            wqkv_sent.append((post.send(wqkv_send.at[part, member], mine, place), theirs))
    down_ring = CubeGather(here, post, wd_all, row_piece, lambda half: wd.at[pl.ds(64 * half, 64)])
    down_ring.start("xy")
    x_gather = GroupGather(here, post, x_all)
    wo_copy = pltpu.make_async_remote_copy(
        src_ref=wo, dst_ref=wo_in, send_sem=self_sems.at[0], recv_sem=self_sems.at[1],
        device_id=here.place(*out_to), device_id_type=MESH_ID,
    )
    wo_keep = pltpu.make_async_copy(wo, wo_in, self_sems.at[2])
    pl.when(out_moves)(wo_copy.start)
    pl.when(out_stays)(wo_keep.start)
    load_wu.wait()
    for member in range(GROUP):
        for shard in range(SPOTS):
            at = ROWS * device_of(shard, member)
            wu_send[member, :, 128 * shard : 128 * (shard + 1)] = wu_own[:, at : at + 128]
    member_rows(wu_all, here.member)[...] = wu_send[here.member]
    for member, place in here.mates():
        mine, theirs = member_rows(wu_all, here.member), member_rows(wu_all, member)
        wu_sent.append((post.send(wu_send.at[member], mine, place), theirs))

    for sent, landing in small_sent:
        post.arrived(sent, landing)
    small_all[here.shard, 0:8] = (
        small_in[0, 0:8] + small_in[1, 0:8] + small_in[2, 0:8] + small_in[3, 0:8]
    )
    for member in range(GROUP):
        small_all[here.shard, 8 + member : 9 + member] = small_in[member, 8:9]
    plane_sent = []
    for step in range(1, SPOTS):
        _, place = here.plane(step)
        came = lax.rem(here.shard + SPOTS - step, SPOTS)
        mine = small_all.at[here.shard]
        plane_sent.append((post.send(mine, mine, place), small_all.at[came]))

    qkv_rings = []
    for part in range(3):
        for sent, landing in wqkv_sent[3 * part : 3 * part + 3]:
            post.arrived(sent, landing)
        qkv_rings.append(CubeGather(here, post, wqkv.at[part], group_piece))
        qkv_rings[part].start()
    down_ring.start("z")
    x_gather.near()
    for sent, landing in plane_sent:
        post.arrived(sent, landing)
    for block in range(SPOTS):
        first, cut = 2 * (block // 2), slice(64 * (block % 2), 64 * (block % 2) + 64)
        vectors[:, ROWS * block : ROWS * (block + 1)] = jnp.concatenate(
            [small_all[first, 0:8, cut], small_all[first + 1, 0:8, cut]], 1
        )
    gain, bias = vectors[0:1], vectors[1:2]

    def put_a(member):
        normed, _ = norm_parts(x_all[member].astype(F32))
        at = pl.ds(pl.multiple_of(ROWS * member, ROWS), ROWS)
        a_t[:, at] = (normed * gain + bias).astype(BF).T

    put_a(here.member)
    put_a(here.core_member)
    for ring in qkv_rings:
        ring.corners()
    x_gather.rest()

    @pl.when(out_moves)
    def _():
        wo_copy.wait_recv()
        wo_copy.wait_send()

    pl.when(out_stays)(wo_keep.wait)
    out_ring = CubeGather(here, post, wo_all, row_piece)
    wo_all[here.shard] = wo_in[...].reshape(2, 16, WIDTH)
    for ring in qkv_rings:
        ring.spread()
    out_ring.start()
    put_a(here.link_member)
    put_a(here.far_member)

    segs = jnp.concatenate([small_all[4 * here.x + group, 8:12] for group in range(4)], 0)
    begin = jnp.zeros_like(segs)
    for doc in range(1, 8):
        size = jnp.sum(
            jnp.sum((segs == doc - 1.0).astype(F32), 1, keepdims=True), 0, keepdims=True
        )
        begin = begin + jnp.where(segs >= doc, size, 0.0)
    starts[...] = begin
    rots = []
    for member in range(GROUP):
        at = 8 * here.high + 4 * (member // 2) + 2 * here.y + member % 2
        position = jnp.where(lane < 64, 64 * at + lane, 64 * (31 - at) + lane - 64)
        rots.append(position.astype(F32) - starts[pl.ds(4 * here.tokens + member, 1)])
    cos_t, sin_t = turn_tables(jnp.concatenate(rots, 1))
    for sent, landing in wu_sent:
        post.arrived(sent, landing)
    up_ring = CubeGather(here, post, wu_all, group_piece)
    for ring in qkv_rings:
        ring.last()
    swaps = []
    for part in range(3):
        qkv_rings[part].finish()
        product = dot(wqkv[part].reshape(WIDTH, 256), a_t[...], 0, 0)
        for head in range(4):
            rows = product[HD * head : HD * (head + 1)]
            if part < 2:
                first, second = rows[: HD // 2], rows[HD // 2 :]
                rows = jnp.concatenate(
                    [first * cos_t - second * sin_t, second * cos_t + first * sin_t], 0
                )
            if part == 0:
                rows = rows * HD**-0.5
            qkv_send[part, head] = rows.astype(BF)
        swaps.append(Swap(here, post, local, qkv_send.at[part], qkv_heads.at[part]))
    up_ring.start("xy")
    for group in range(16):
        a, b, cut = 2 * group, 2 * group + 1, slice(0, 64)
        if group >= 8:
            a, b, cut = 31 - a, 31 - b, slice(64, 128)
        a, b = (4 * tokens + member for tokens, member in (stored_at(a), stored_at(b)))
        start[:, ROWS * group : ROWS * (group + 1)] = jnp.concatenate(
            [starts[a : a + 1, cut], starts[b : b + 1, cut]], 1
        ).astype(jnp.int32)
    down_ring.corners()
    down_ring.spread()
    out_ring.corners()
    out_ring.spread()
    for part in range(3):
        swaps[part].finish()
        for group in range(16):
            at = slice(ROWS * group, ROWS * (group + 1))
            qkv[HD * part : HD * (part + 1), at] = true_group(qkv_heads.at[part], group)
    up_ring.start("z")
    up_ring.corners()
    for query_at in range(0, 2048, 512):
        attend_block(qkv, start, o_true, lse, query_at, 512, 512)
    for at in range(16):
        put_stored(o_send, at, o_true)
    swap = Swap(here, post, local, o_send, o_all)
    down_ring.last()
    out_ring.last()
    up_ring.spread()
    out_ring.finish()
    swap.finish()

    sums = [
        GroupSum(here, post, near_send.at[n], near_in.at[n], far_send.at[n], far_in.at[n], terms)
        for n in range(4)
    ]
    wo_flat = wo_all[...].reshape(256, WIDTH)

    def half_lanes(low):
        return pl.ds(pl.multiple_of(256 * low, 256), 256)

    def out_half(low):
        heads = [o_all[group, :, half_lanes(low)] for group in range(4)]
        return dot(jnp.concatenate(heads, 0), wo_flat, 0, 0)

    sums[0].give(0, out_half(1 - here.low))
    sums[0].give(1, out_half(here.low))
    sums[0].cross()
    up_ring.last()
    branch = sums[0].total()
    t_normed, t_inv = norm_parts(branch)
    hres = tok[...].astype(F32) + t_normed * vectors[2:3] + vectors[3:4]
    res[0] = t_normed
    h_normed, h_inv = norm_parts(hres)
    res[1] = h_normed
    res[2] = hres
    c_all[here.member] = (h_normed * vectors[4:5] + vectors[5:6]).astype(BF)
    gather = GroupGather(here, post, c_all)
    gather.near()
    up_ring.finish()
    wu_flat = wu_all[...].reshape(WIDTH, WIDTH)

    def half(held, low):
        return held[pl.ds(2 * low, 2)].reshape(2 * ROWS, WIDTH)

    def up_half(low):
        gl, slope = gelu_and_slope(dot(half(c_all, low), wu_flat, 1, 0))
        gl_all[pl.ds(2 * low, 2)] = gl.astype(BF).reshape(2, ROWS, WIDTH)
        slope_all[pl.ds(2 * low, 2)] = slope.reshape(2, ROWS, WIDTH)

    up_half(here.low)
    for load in load_wd:
        load.wait()
    down_ring.finish()
    wd_flat = wd_all[...].reshape(WIDTH, WIDTH)
    sums[1].give(1, dot(half(gl_all, here.low), wd_flat, 1, 0))
    gather.rest()
    up_half(1 - here.low)
    sums[1].give(0, dot(half(gl_all, 1 - here.low), wd_flat, 1, 0))
    sums[1].cross()
    branch = sums[1].total()
    m_normed, m_inv = norm_parts(branch)
    act[...] = (res[2] + m_normed * vectors[6:7] + vectors[7:8]).astype(BF)
    load_cot.wait()
    upstream = cot[...].astype(F32)
    dm_all[here.member] = norm_pull(m_normed, m_inv, vectors[6:7], upstream).astype(BF)
    gather = GroupGather(here, post, dm_all)
    d_vec[6:7] = jnp.sum(upstream * m_normed, 0, keepdims=True)
    d_vec[7:8] = jnp.sum(upstream, 0, keepdims=True)
    gather.near()

    def du_half(low):
        d_gl = dot(half(dm_all, low), wd_flat, 1, 1)
        slope = slope_all[pl.ds(2 * low, 2)].reshape(2 * ROWS, WIDTH)
        du_all[pl.ds(2 * low, 2)] = (d_gl * slope).astype(BF).reshape(2, ROWS, WIDTH)

    du_half(here.low)
    sums[2].give(1, dot(half(du_all, here.low), wu_flat, 1, 1))
    gather.rest()
    du_half(1 - here.low)
    sums[2].give(0, dot(half(du_all, 1 - here.low), wu_flat, 1, 1))
    sums[2].cross()
    gl_flat = gl_all[...].reshape(512, WIDTH)
    dm_flat = dm_all[...].reshape(512, WIDTH)
    for shard in range(SPOTS):
        term = dot(gl_flat[:, ROWS * shard : ROWS * (shard + 1)], dm_flat, 0, 0)
        down_parts[shard] = term.astype(BF).reshape(2, 64, WIDTH)
    down_sum = CubeSum(here, post, down_parts, row_piece, down_in)
    up_sum = CubeSum(here, post, up_parts, group_piece, up_in)
    out_sum = CubeSum(here, post, out_parts, row_piece, out_in)
    qkv_sums = [
        CubeSum(here, post, qkv_parts.at[part], group_piece, qkv_in.at[part]) for part in range(3)
    ]
    down_sum.hop()
    du_flat = du_all[...].reshape(512, WIDTH)
    c_flat = c_all[...].reshape(512, WIDTH)
    for block in range(SPOTS):
        term = dot(c_flat[:, ROWS * block : ROWS * (block + 1)], du_flat, 0, 0)
        up_parts[block // 2, block % 2] = term.astype(BF).reshape(2, 64, WIDTH)
    up_sum.hop()
    d_c = sums[2].total()
    h_normed = res[1]
    d_h = upstream + norm_pull(h_normed, h_inv, vectors[4:5], d_c)
    t_normed = res[0]
    dt_all[here.member] = norm_pull(t_normed, t_inv, vectors[2:3], d_h).astype(BF)
    gather = GroupGather(here, post, dt_all)
    d_vec[4:5] = jnp.sum(d_c * h_normed, 0, keepdims=True)
    d_vec[5:6] = jnp.sum(d_c, 0, keepdims=True)
    d_vec[2:3] = jnp.sum(d_h * t_normed, 0, keepdims=True)
    d_vec[3:4] = jnp.sum(d_h, 0, keepdims=True)
    res[2] = d_h
    down_sum.hop()
    gather.near()
    gather.rest()
    dt_flat = dt_all[...].reshape(512, WIDTH)
    d_o = dot(wo_flat, dt_flat, 1, 1)
    for head in range(4):
        do_send[head] = d_o[HD * head : HD * (head + 1)].astype(BF)
    swap = Swap(here, post, local, do_send, do_heads)
    o_flat = o_all[...].reshape(256, 512)
    out_parts[...] = dot(o_flat, dt_flat, 1, 0).astype(BF).reshape(SPOTS, 2, 16, WIDTH)
    up_sum.hop()
    out_sum.hop()
    swap.finish()
    down_sum.hop()
    for group in range(16):
        d_out[:, ROWS * group : ROWS * (group + 1)] = true_group(do_heads, group)
    grads[HD:] = jnp.zeros((2 * HD, 2048), F32)
    for query_at in range(0, 2048, 256):
        attend_back_block(qkv, start, o_true, lse, d_out, grads, query_at, 256)
        if query_at == 1536:
            out_sum.hop()
    for at in range(16):
        put_stored(d_send.at[2], at, grads[2 * HD :])
    swaps = [Swap(here, post, local, d_send.at[2], d_in.at[2])]
    position = lax.broadcasted_iota(jnp.int32, (1, 2048), 1) - start[...]
    cos_t, sin_t = turn_tables(position.astype(F32))
    for part in (1, 0):
        first = grads[HD * part : HD * part + HD // 2]
        second = grads[HD * part + HD // 2 : HD * (part + 1)]
        turned = jnp.concatenate([first * cos_t + second * sin_t, second * cos_t - first * sin_t], 0)
        for at in range(16):
            put_stored(d_send.at[part], at, turned)
        swaps.append(Swap(here, post, local, d_send.at[part], d_in.at[part]))
    up_sum.hop()
    low_half, high_half = down_sum.total()
    g_down[0:64] = low_half
    g_down[64:128] = high_half
    out_sum.hop()
    for number, part in enumerate((2, 1, 0)):
        swaps[number].finish()
        d_all[256 * part : 256 * (part + 1)] = d_in[part].reshape(256, 512)
        for block in range(SPOTS):
            term = dot(
                a_t[ROWS * block : ROWS * (block + 1)], d_all[256 * part : 256 * (part + 1)], 1, 1
            )
            qkv_parts[part, block // 2, block % 2] = term.astype(BF).reshape(2, 64, 256)
        qkv_sums[part].hop()
    wqkv_flat = [wqkv[part].reshape(WIDTH, 256) for part in range(3)]

    def in_half(low):
        terms = [
            dot(d_all[256 * part : 256 * (part + 1), half_lanes(low)], wqkv_flat[part], 0, 1)
            for part in range(3)
        ]
        return terms[0] + terms[1] + terms[2]

    sums[3].give(0, in_half(1 - here.low))
    sums[3].give(1, in_half(here.low))
    sums[3].cross()
    for part in (2, 1, 0):
        qkv_sums[part].hop()
    low_half, high_half = up_sum.total()
    for member in range(GROUP):
        halved = low_half if member < 2 else high_half
        up_send[member] = halved[32 * (member % 2) : 32 * (member % 2) + 32].astype(BF)
    up_got[here.member] = up_send[here.member]
    ends = []
    for member, place in here.mates():
        ends.append((post.send(up_send.at[member], up_got.at[here.member], place), up_got.at[member]))
    low_half, high_half = out_sum.total()
    out_end[0:16] = low_half.astype(BF)
    out_end[16:32] = high_half.astype(BF)
    out_copy = pltpu.make_async_remote_copy(
        src_ref=out_end, dst_ref=out_got, send_sem=self_sems.at[3], recv_sem=self_sems.at[4],
        device_id=here.place(*out_from), device_id_type=MESH_ID,
    )
    pl.when(out_moves)(out_copy.start)

    @pl.when(out_stays)
    def _():
        out_got[...] = out_end[...]

    d_a = sums[3].total()
    normed, inv_std = norm_parts(tok[...].astype(F32))
    in_grad[...] = res[2] + norm_pull(normed, inv_std, vectors[0:1], d_a)
    d_vec[0:1] = jnp.sum(d_a * normed, 0, keepdims=True)
    d_vec[1:2] = jnp.sum(d_a, 0, keepdims=True)
    for shard in range(SPOTS):
        at = 256 * (shard // 2) + 64 * (shard % 2)
        vec_send[shard] = jnp.concatenate(
            [d_vec[:, at : at + 64], d_vec[:, at + ROWS : at + ROWS + 64]], 1
        )
    vec_in[here.shard] = vec_send[here.shard]
    vec_sent = []
    for step in range(1, SPOTS):
        shard, place = here.plane(step)
        came = lax.rem(here.shard + SPOTS - step, SPOTS)
        vec_sent.append((post.send(vec_send.at[shard], vec_in.at[here.shard], place), vec_in.at[came]))
    for part in (2, 1, 0):
        qkv_sums[part].hop()
    for sent, landing in vec_sent:
        post.arrived(sent, landing)
    total = vec_in[0]
    for shard in range(1, SPOTS):
        total = total + vec_in[shard]
    vec_group[here.member] = total
    vec_sent = []
    for member, place in here.mates():
        mine = vec_group.at[here.member]
        vec_sent.append((post.send(mine, mine, place), vec_group.at[member]))
    for sent, landing in ends:
        post.arrived(sent, landing)

    @pl.when(out_moves)
    def _():
        out_copy.wait_recv()
        out_copy.wait_send()

    for sent, landing in vec_sent:
        post.arrived(sent, landing)
    total = vec_group[0] + vec_group[1] + vec_group[2] + vec_group[3]
    mine = total[:, 0:32]
    for member in range(1, GROUP):
        mine = jnp.where(here.member == member, total[:, 32 * member : 32 * (member + 1)], mine)
    g_vec[...] = mine
    ends = []
    for part in (2, 1, 0):
        low_half, high_half = qkv_sums[part].total()
        for member in range(GROUP):
            halved = low_half if member < 2 else high_half
            qkv_end[part, member] = halved[32 * (member % 2) : 32 * (member % 2) + 32].astype(BF)
        qkv_got[part, here.member] = qkv_end[part, here.member]
        for member, place in here.mates():
            sent = post.send(qkv_end.at[part, member], qkv_got.at[part, here.member], place)
            ends.append((sent, qkv_got.at[part, member]))
    for sent, landing in ends:
        post.arrived(sent, landing)
    post.finish()


def call_layer(*args):
    vmem = pl.BlockSpec(memory_space=pltpu.VMEM)
    anywhere = pl.BlockSpec(memory_space=pl.ANY)
    shape = jax.ShapeDtypeStruct
    dma = pltpu.SemaphoreType.DMA

    def held(*dims, kind=BF):
        return pltpu.VMEM(dims, kind)

    rows = (GROUP, ROWS, WIDTH)
    return pl.pallas_call(
        layer_kernel,
        out_shape=[
            shape((ROWS, WIDTH), BF),
            shape((ROWS, WIDTH), F32),
            shape((ROWS, WIDTH), F32),
            shape((GROUP, 32, WIDTH), BF),
            shape((3, GROUP, 32, 256), BF),
            shape((32, WIDTH), BF),
            shape((8, 32), F32),
        ],
        in_specs=[anywhere] * 17,
        out_specs=[vmem] * 7,
        scratch_shapes=[
            held(ROWS, WIDTH), held(ROWS, WIDTH), held(3, 32, WIDTH), held(32, 4 * WIDTH),
            held(1, ROWS, kind=jnp.int32), held(8, 1, 32),
            held(*rows), held(3, 4, 2, 2, 64, 256), held(3, GROUP, 32, 256), held(GROUP, 32, WIDTH),
            held(GROUP, 16, ROWS, kind=F32), held(SPOTS, 16, ROWS, kind=F32),
            held(32, WIDTH), held(SPOTS, 2, 16, WIDTH), held(4, 2, 2, 64, WIDTH), held(SPOTS, 2, 64, WIDTH),
            held(8, WIDTH, kind=F32), held(16, ROWS, kind=F32), held(1, 2048, kind=jnp.int32),
            held(WIDTH, 512), held(3, 4, HD, 512), held(3, 4, HD, 512), held(192, 2048),
            held(HD, 2048, kind=F32), held(1, 2048, kind=F32), held(4, HD, 512), held(4, HD, 512),
            held(*rows), held(*rows), held(*rows), held(*rows), held(*rows, kind=F32), held(*rows),
            held(3, ROWS, WIDTH, kind=F32),
            held(4, 2, ROWS, WIDTH), held(4, 2, ROWS, WIDTH), held(4, ROWS, WIDTH), held(4, ROWS, WIDTH),
            held(2, 2, ROWS, WIDTH, kind=F32),
            held(4, HD, 512), held(4, HD, 512), held(HD, 2048), held(192, 2048, kind=F32),
            held(3, 4, HD, 512), held(3, 4, HD, 512), held(768, 512),
            held(SPOTS, 2, 64, WIDTH), held(14, 64, WIDTH),
            held(4, 2, 2, 64, WIDTH), held(14, 64, WIDTH),
            held(SPOTS, 2, 16, WIDTH), held(14, 16, WIDTH),
            held(3, 4, 2, 2, 64, 256), held(3, 14, 64, 256),
            held(SPOTS, 8, ROWS, kind=F32), held(SPOTS, 8, ROWS, kind=F32), held(GROUP, 8, ROWS, kind=F32),
            held(8, WIDTH, kind=F32), held(GROUP, 32, WIDTH), held(3, GROUP, 32, 256), held(32, WIDTH),
            dma((300,)), dma((300,)), dma((40,)), dma((5,)),
        ],
        compiler_params=pltpu.CompilerParams(
            collective_id=0, has_side_effects=True, vmem_limit_bytes=VMEM_BYTES
        ),
        name="layer",
    )(*args)


def finish_kernel(
    act_in, grad_in, down_in, up_got, qkv_got, out_got, vec,
    act, in_grad, g_q, g_k, g_v, g_out, g_up, g_down, *g_norms
):
    act[...] = act_in[...]
    in_grad[...] = grad_in[...]
    g_down[...] = down_in[...]
    g_out[...] = out_got[...].astype(F32)
    for member in range(GROUP):
        for shard in range(SPOTS):
            at = ROWS * device_of(shard, member)
            g_up[:, at : at + 128] = up_got[member, :, 128 * shard : 128 * (shard + 1)].astype(F32)
        base = 256 * member
        for slot, out in enumerate((g_q, g_k, g_v)):
            out[:, base : base + 256] = qkv_got[slot, member].astype(F32)
    for row, out in enumerate(g_norms):
        out[...] = vec[row : row + 1]


def call_finish(*args):
    vmem = pl.BlockSpec(memory_space=pltpu.VMEM)
    shape = jax.ShapeDtypeStruct
    narrow = shape((32, WIDTH), F32)
    return pl.pallas_call(
        finish_kernel,
        out_shape=[
            shape((ROWS, WIDTH), BF), shape((ROWS, WIDTH), F32), narrow, narrow, narrow, narrow,
            shape((32, 4 * WIDTH), F32), shape((ROWS, WIDTH), F32),
        ] + [shape((1, 32), F32)] * 8,
        in_specs=[vmem] * 7,
        out_specs=[vmem] * 16,
        compiler_params=pltpu.CompilerParams(vmem_limit_bytes=VMEM_BYTES),
        name="finish",
    )(*args)


def on_device_grouped(tokens, segments, cotangent, *params):
    weights, norms = params[:6], params[6:]
    results = call_layer(
        tokens[0], segments, cotangent[0], *weights, *[vector[None] for vector in norms]
    )
    outs = call_finish(*results)
    act, in_grad, *rest = outs
    return (act[None], in_grad[None], *rest[:6]) + tuple(vector[0] for vector in rest[6:])


def solution(mesh):
    in_specs = (
        P("dp", "ctx", None),
        P("dp", "ctx"),
        P("dp", "ctx", None),
        P(("dp", "ctx"), None),
        P(("dp", "ctx"), None),
        P(("dp", "ctx"), None),
        P(("dp", "ctx"), None),
        P(("dp", "ctx"), None),
        P(("dp", "ctx"), None),
        P(("dp", "ctx")),
        P(("dp", "ctx")),
        P(("dp", "ctx")),
        P(("dp", "ctx")),
        P(("dp", "ctx")),
        P(("dp", "ctx")),
        P(("dp", "ctx")),
        P(("dp", "ctx")),
    )
    out_specs = (
        P("dp", "ctx", None),
        P("dp", "ctx", None),
        P(("dp", "ctx"), None),
        P(("dp", "ctx"), None),
        P(("dp", "ctx"), None),
        P(("dp", "ctx"), None),
        P(("dp", "ctx"), None),
        P(("dp", "ctx"), None),
        P(("dp", "ctx")),
        P(("dp", "ctx")),
        P(("dp", "ctx")),
        P(("dp", "ctx")),
        P(("dp", "ctx")),
        P(("dp", "ctx")),
        P(("dp", "ctx")),
        P(("dp", "ctx")),
    )
    grouped = mesh.shape["dp"] == 2 and mesh.shape["ctx"] == 16
    return jax.shard_map(
        on_device_grouped if grouped else on_device, mesh=mesh, in_specs=in_specs, out_specs=out_specs, check_vma=False
    )
```

```python
import math

import jax
import jax.numpy as jnp
from jax import lax
from jax.experimental import pallas as pl
from jax.experimental.pallas import tpu as pltpu
from jax.sharding import PartitionSpec as P

HEADS = 16
HD = 64


norm_eps = 1e-05
masked_value = -1e30


def layer_norm(value, gain, bias):
    row_mean = jnp.mean(value, -1, keepdims=True)
    centred = value - row_mean
    scaled = centred * lax.rsqrt(jnp.mean(centred * centred, -1, keepdims=True) + norm_eps)
    return scaled * gain + bias


def norm_back(value, gain, upstream):
    row_mean = jnp.mean(value, -1, keepdims=True)
    centred = value - row_mean
    inv_std = lax.rsqrt(jnp.mean(centred * centred, -1, keepdims=True) + norm_eps)
    normed = centred * inv_std
    d_normed = upstream * gain
    d_value = inv_std * (
        d_normed
        - jnp.mean(d_normed, -1, keepdims=True)
        - normed * jnp.mean(d_normed * normed, -1, keepdims=True)
    )
    return (d_value, jnp.sum(upstream * normed, 0), jnp.sum(upstream, 0))


def rope_tables(offsets, head_dim):
    freq = 10000.0 ** (-jnp.arange(head_dim // 2, dtype=jnp.float32) / (head_dim // 2))
    angle = offsets.astype(jnp.float32)[..., None] * freq
    return (jnp.cos(angle)[..., None, :], jnp.sin(angle)[..., None, :])


def rotate(values, cos_t, sin_t):
    half_dim = values.shape[-1] // 2
    first = values[..., :half_dim]
    second = values[..., half_dim:]
    return jnp.concatenate([first * cos_t - second * sin_t, second * cos_t + first * sin_t], -1)


def unrotate(grads, cos_t, sin_t):
    half_dim = grads.shape[-1] // 2
    first = grads[..., :half_dim]
    second = grads[..., half_dim:]
    return jnp.concatenate([first * cos_t + second * sin_t, second * cos_t - first * sin_t], -1)


def true_position(flat_index, row_count, ctx_size):
    device_of = flat_index // row_count
    offset_in = flat_index % row_count
    half_rows = row_count // 2
    return jnp.where(
        offset_in < half_rows,
        device_of * half_rows + offset_in,
        (2 * ctx_size - 1 - device_of) * half_rows + offset_in - half_rows,
    )


def split_blocks(array, block_rows):
    return array.reshape((array.shape[0] // block_rows, block_rows) + array.shape[1:])


def score_block(queries, keys, query_pos, query_seg, key_pos, key_seg):
    scores = jnp.einsum(
        "qhd,khd->hqk", queries, keys, preferred_element_type=jnp.float32
    ) * queries.shape[-1] ** (-0.5)
    allowed = (query_seg[:, None] == key_seg[None, :]) & (key_pos[None, :] <= query_pos[:, None])
    return (scores, allowed[None])


def grad_block(queries, d_attn, lse, delta, keys, values, query_pos, query_seg, key_pos, key_seg):
    scores, allowed = score_block(queries, keys, query_pos, query_seg, key_pos, key_seg)
    attn_probs = jnp.where(allowed, jnp.exp(scores - lse[:, :, None]), 0.0)
    d_probs = jnp.einsum("qhd,khd->hqk", d_attn, values, preferred_element_type=jnp.float32)
    d_scores = (attn_probs * (d_probs - delta[:, :, None])).astype(jnp.bfloat16)
    return (attn_probs, d_scores)


def key_terms(
    query_rows,
    dattn_rows,
    lse_rows,
    delta_rows,
    query_pos,
    query_seg,
    key_block,
    value_block,
    key_pos,
    key_seg,
):
    attn_probs, d_scores = grad_block(
        query_rows,
        dattn_rows,
        lse_rows,
        delta_rows,
        key_block,
        value_block,
        query_pos,
        query_seg,
        key_pos,
        key_seg,
    )
    d_keys = jnp.einsum(
        "hqk,qhd->khd", d_scores, query_rows, preferred_element_type=jnp.float32
    ) * query_rows.shape[-1] ** (-0.5)
    d_values = jnp.einsum(
        "hqk,qhd->khd",
        attn_probs.astype(jnp.bfloat16),
        dattn_rows,
        preferred_element_type=jnp.float32,
    )
    return (d_keys, d_values)


def on_device(
    tokens,
    segments,
    cotangent,
    w_query,
    w_key,
    w_value,
    w_out,
    w_up,
    w_down,
    gain_attn_in,
    bias_attn_in,
    gain_attn_out,
    bias_attn_out,
    gain_mlp_in,
    bias_mlp_in,
    gain_mlp_out,
    bias_mlp_out,
):
    whole = (
        lax.all_gather(w_query, ("dp", "ctx"), axis=0, tiled=True),
        lax.all_gather(w_key, ("dp", "ctx"), axis=0, tiled=True),
        lax.all_gather(w_value, ("dp", "ctx"), axis=0, tiled=True),
        lax.all_gather(w_out, ("dp", "ctx"), axis=0, tiled=True),
        lax.all_gather(w_up, ("dp", "ctx"), axis=0, tiled=True),
        lax.all_gather(w_down, ("dp", "ctx"), axis=0, tiled=True),
        lax.all_gather(gain_attn_in, ("dp", "ctx"), axis=0, tiled=True),
        lax.all_gather(bias_attn_in, ("dp", "ctx"), axis=0, tiled=True),
        lax.all_gather(gain_attn_out, ("dp", "ctx"), axis=0, tiled=True),
        lax.all_gather(bias_attn_out, ("dp", "ctx"), axis=0, tiled=True),
        lax.all_gather(gain_mlp_in, ("dp", "ctx"), axis=0, tiled=True),
        lax.all_gather(bias_mlp_in, ("dp", "ctx"), axis=0, tiled=True),
        lax.all_gather(gain_mlp_out, ("dp", "ctx"), axis=0, tiled=True),
        lax.all_gather(bias_mlp_out, ("dp", "ctx"), axis=0, tiled=True),
    )
    query_w, key_w, value_w, out_w, up_w, down_w = whole[:6]
    gain_ai, bias_ai, gain_ao, bias_ao, gain_mi, bias_mi, gain_mo, bias_mo = [
        entry.astype(jnp.float32) for entry in whole[6:]
    ]
    row_count = tokens.shape[1]
    model_width = tokens.shape[2]
    ctx_size = lax.axis_size("ctx")
    seq_length = row_count * ctx_size
    score_scale = HD ** (-0.5)
    seg_all = lax.all_gather(segments, "ctx", axis=1, tiled=True)[0]
    my_seg = segments[0]
    all_pos = true_position(jnp.arange(seq_length, dtype=jnp.int32), row_count, ctx_size)
    my_pos = true_position(
        lax.axis_index("ctx") * row_count + jnp.arange(row_count, dtype=jnp.int32),
        row_count,
        ctx_size,
    )
    doc_first = jnp.min(
        jnp.where(seg_all[None, :] == my_seg[:, None], all_pos[None, :], seq_length), axis=1
    )
    cos_t, sin_t = rope_tables(my_pos - doc_first, HD)
    inputs = tokens[0].astype(jnp.float32)
    attn_in = layer_norm(inputs, gain_ai, bias_ai).astype(jnp.bfloat16)
    query_pre = jnp.dot(attn_in, query_w, preferred_element_type=jnp.float32).reshape(
        row_count, HEADS, HD
    )
    key_pre = jnp.dot(attn_in, key_w, preferred_element_type=jnp.float32).reshape(
        row_count, HEADS, HD
    )
    queries = rotate(query_pre, cos_t, sin_t).astype(jnp.bfloat16)
    keys_rot = rotate(key_pre, cos_t, sin_t).astype(jnp.bfloat16)
    values_flat = jnp.dot(attn_in, value_w, preferred_element_type=jnp.float32).astype(jnp.bfloat16)
    values_heads = values_flat.reshape(row_count, HEADS, HD)
    keys_flat = keys_rot.reshape(row_count, model_width)
    start_state = (
        jnp.full((HEADS, row_count), masked_value, jnp.float32),
        jnp.zeros((HEADS, row_count), jnp.float32),
        jnp.zeros((row_count, HEADS, HD), jnp.float32),
    )
    key_rows = lax.all_gather(keys_flat, "ctx", axis=0, tiled=True)
    value_rows = lax.all_gather(values_flat, "ctx", axis=0, tiled=True)
    span = key_rows.shape[0]
    block_rows = math.gcd(span, 1024)
    key_pos = true_position(jnp.arange(span, dtype=jnp.int32), row_count, ctx_size)
    key_seg = seg_all

    def visit(state_now, parts):
        row_top, row_total, weighted = state_now
        key_block = parts[0].reshape(block_rows, HEADS, HD)
        value_block = parts[1].reshape(block_rows, HEADS, HD)
        scores, allowed = score_block(queries, key_block, my_pos, my_seg, parts[2], parts[3])
        top_new = jnp.maximum(row_top, jnp.max(jnp.where(allowed, scores, masked_value), -1))
        fade = jnp.exp(row_top - top_new)
        attn_probs = jnp.where(allowed, jnp.exp(scores - top_new[:, :, None]), 0.0)
        row_total = row_total * fade + jnp.sum(attn_probs, -1)
        weighted = weighted * fade.T[:, :, None] + jnp.einsum(
            "hqk,khd->qhd",
            attn_probs.astype(jnp.bfloat16),
            value_block,
            preferred_element_type=jnp.float32,
        )
        return ((top_new, row_total, weighted), None)

    blocks = (
        split_blocks(key_rows, block_rows),
        split_blocks(value_rows, block_rows),
        split_blocks(key_pos, block_rows),
        split_blocks(key_seg, block_rows),
    )
    row_top, row_total, weighted = lax.scan(visit, start_state, blocks)[0]
    lse = row_top + jnp.log(row_total)
    attn_f = weighted / row_total.T[:, :, None]
    attn_b = attn_f.reshape(row_count, model_width).astype(jnp.bfloat16)
    branch = jnp.dot(attn_b, out_w, preferred_element_type=jnp.float32)
    resid = inputs + layer_norm(branch, gain_ao, bias_ao)
    mlp_in = layer_norm(resid, gain_mi, bias_mi).astype(jnp.bfloat16)
    hidden_pre = jnp.dot(mlp_in, up_w, preferred_element_type=jnp.float32)
    hidden = jax.nn.gelu(hidden_pre, approximate=True).astype(jnp.bfloat16)
    mlp_out = jnp.dot(hidden, down_w, preferred_element_type=jnp.float32)
    result = resid + layer_norm(mlp_out, gain_mo, bias_mo)
    upstream = cotangent[0].astype(jnp.float32)
    d_mlp_out, dgain_mo, dbias_mo = norm_back(mlp_out, gain_mo, upstream)
    d_mlp_b = d_mlp_out.astype(jnp.bfloat16)
    grad_down = jnp.dot(hidden.T, d_mlp_b, preferred_element_type=jnp.float32)
    d_hidden = jnp.dot(d_mlp_b, down_w.T, preferred_element_type=jnp.float32)
    gelu_back = jax.vjp(lambda pre: jax.nn.gelu(pre, approximate=True), hidden_pre)[1]
    d_pre = gelu_back(d_hidden)[0].astype(jnp.bfloat16)
    grad_up = jnp.dot(mlp_in.T, d_pre, preferred_element_type=jnp.float32)
    d_mlp_in = jnp.dot(d_pre, up_w.T, preferred_element_type=jnp.float32)
    d_resid_n, dgain_mi, dbias_mi = norm_back(resid, gain_mi, d_mlp_in)
    d_resid = upstream + d_resid_n
    d_branch, dgain_ao, dbias_ao = norm_back(branch, gain_ao, d_resid)
    d_branch_b = d_branch.astype(jnp.bfloat16)
    grad_out = jnp.dot(attn_b.T, d_branch_b, preferred_element_type=jnp.float32)
    d_attn_flat = jnp.dot(d_branch_b, out_w.T, preferred_element_type=jnp.float32).astype(
        jnp.bfloat16
    )
    d_attn = d_attn_flat.reshape(row_count, HEADS, HD)
    delta = jnp.sum(d_attn.astype(jnp.float32) * attn_f, -1).T
    zero_heads = jnp.zeros((row_count, HEADS, HD), jnp.float32)

    def query_grad(dq_now, key_rows, value_rows, key_pos, key_seg):
        block_rows = math.gcd(key_rows.shape[0], 1024)

        def visit(dq_run, parts):
            key_block = parts[0].reshape(block_rows, HEADS, HD)
            value_block = parts[1].reshape(block_rows, HEADS, HD)
            d_scores = grad_block(
                queries,
                d_attn,
                lse,
                delta,
                key_block,
                value_block,
                my_pos,
                my_seg,
                parts[2],
                parts[3],
            )[1]
            return (
                dq_run
                + jnp.einsum(
                    "hqk,khd->qhd", d_scores, key_block, preferred_element_type=jnp.float32
                )
                * score_scale,
                None,
            )

        blocks = (
            split_blocks(key_rows, block_rows),
            split_blocks(value_rows, block_rows),
            split_blocks(key_pos, block_rows),
            split_blocks(key_seg, block_rows),
        )
        return lax.scan(visit, dq_now, blocks)[0]

    lse_all, delta_all = (
        lax.all_gather(lse.T, "ctx", axis=0, tiled=True),
        lax.all_gather(delta.T, "ctx", axis=0, tiled=True),
    )
    query_rows = lax.all_gather(queries.reshape(row_count, model_width), "ctx", axis=0, tiled=True)
    dattn_rows = lax.all_gather(d_attn_flat, "ctx", axis=0, tiled=True)
    span = query_rows.shape[0]
    query_block_rows = math.gcd(span, 1024)
    query_pos = true_position(jnp.arange(span, dtype=jnp.int32), row_count, ctx_size)

    def visit(sums, parts):
        d_keys, d_values = key_terms(
            parts[0].reshape(query_block_rows, HEADS, HD),
            parts[1].reshape(query_block_rows, HEADS, HD),
            parts[2].T,
            parts[3].T,
            parts[4],
            parts[5],
            keys_rot,
            values_heads,
            my_pos,
            my_seg,
        )
        return ((sums[0] + d_keys, sums[1] + d_values), None)

    blocks = (
        split_blocks(query_rows, query_block_rows),
        split_blocks(dattn_rows, query_block_rows),
        split_blocks(lse_all, query_block_rows),
        split_blocks(delta_all, query_block_rows),
        split_blocks(query_pos, query_block_rows),
        split_blocks(seg_all, query_block_rows),
    )
    dk_rot, dv_sum = lax.scan(visit, (zero_heads, zero_heads), blocks)[0]
    pieces = (
        lax.all_gather(keys_flat, "ctx", axis=0, tiled=True),
        lax.all_gather(values_flat, "ctx", axis=0, tiled=True),
    )
    span = pieces[0].shape[0]
    key_pos = true_position(jnp.arange(span, dtype=jnp.int32), row_count, ctx_size)
    key_seg = seg_all
    dq_rot = query_grad(zero_heads, pieces[0], pieces[1], key_pos, key_seg)
    d_query = unrotate(dq_rot, cos_t, sin_t).reshape(row_count, model_width).astype(jnp.bfloat16)
    d_key = unrotate(dk_rot, cos_t, sin_t).reshape(row_count, model_width).astype(jnp.bfloat16)
    d_value = dv_sum.reshape(row_count, model_width).astype(jnp.bfloat16)
    grad_query = jnp.dot(attn_in.T, d_query, preferred_element_type=jnp.float32)
    grad_key = jnp.dot(attn_in.T, d_key, preferred_element_type=jnp.float32)
    grad_value = jnp.dot(attn_in.T, d_value, preferred_element_type=jnp.float32)
    d_attn_in = (
        jnp.dot(d_query, query_w.T, preferred_element_type=jnp.float32)
        + jnp.dot(d_key, key_w.T, preferred_element_type=jnp.float32)
        + jnp.dot(d_value, value_w.T, preferred_element_type=jnp.float32)
    )
    d_inputs_n, dgain_ai, dbias_ai = norm_back(inputs, gain_ai, d_attn_in)
    input_grad = (d_resid + d_inputs_n)[None]
    shares = (
        lax.psum_scatter(grad_query, ("dp", "ctx"), scatter_dimension=0, tiled=True),
        lax.psum_scatter(grad_key, ("dp", "ctx"), scatter_dimension=0, tiled=True),
        lax.psum_scatter(grad_value, ("dp", "ctx"), scatter_dimension=0, tiled=True),
        lax.psum_scatter(grad_out, ("dp", "ctx"), scatter_dimension=0, tiled=True),
        lax.psum_scatter(grad_up, ("dp", "ctx"), scatter_dimension=0, tiled=True),
        lax.psum_scatter(grad_down, ("dp", "ctx"), scatter_dimension=0, tiled=True),
        lax.psum_scatter(dgain_ai, ("dp", "ctx"), scatter_dimension=0, tiled=True),
        lax.psum_scatter(dbias_ai, ("dp", "ctx"), scatter_dimension=0, tiled=True),
        lax.psum_scatter(dgain_ao, ("dp", "ctx"), scatter_dimension=0, tiled=True),
        lax.psum_scatter(dbias_ao, ("dp", "ctx"), scatter_dimension=0, tiled=True),
        lax.psum_scatter(dgain_mi, ("dp", "ctx"), scatter_dimension=0, tiled=True),
        lax.psum_scatter(dbias_mi, ("dp", "ctx"), scatter_dimension=0, tiled=True),
        lax.psum_scatter(dgain_mo, ("dp", "ctx"), scatter_dimension=0, tiled=True),
        lax.psum_scatter(dbias_mo, ("dp", "ctx"), scatter_dimension=0, tiled=True),
    )
    return (result.astype(jnp.bfloat16)[None], input_grad) + tuple(shares)


BF = jnp.bfloat16
F32 = jnp.float32
MESH_ID = pl.DeviceIdType.MESH
GROUP = 4
SPOTS = 8
ROWS = 128
WIDTH = 1024
VMEM_BYTES = 60 << 20


def dot(left, right, left_dim, right_dim):
    return lax.dot_general(
        left, right, (((left_dim,), (right_dim,)), ((), ())), preferred_element_type=F32
    )


class Here:
    def __init__(self):
        self.x = lax.axis_index("dp")
        at = lax.axis_index("ctx")
        self.high, self.low, self.y, self.c = at // 8, (at // 4) % 2, (at // 2) % 2, at % 2
        self.member = 2 * self.low + self.c
        self.tokens = 2 * self.high + self.y
        self.shard = 4 * self.x + self.tokens
        self.core_mate = self.place(self.x, self.high, self.low, self.y, 1 - self.c)
        self.link_mate = self.place(self.x, self.high, 1 - self.low, self.y, self.c)
        self.far_mate = self.place(self.x, self.high, 1 - self.low, self.y, 1 - self.c)
        self.core_member = 2 * self.low + (1 - self.c)
        self.link_member = 2 * (1 - self.low) + self.c
        self.far_member = 2 * (1 - self.low) + (1 - self.c)

    @staticmethod
    def place(x, high, low, y, c):
        return (x, 8 * high + 4 * low + 2 * y + c)

    def across(self, axes):
        x = 1 - self.x if "x" in axes else self.x
        y = 1 - self.y if "y" in axes else self.y
        high = 1 - self.high if "z" in axes else self.high
        return 4 * x + 2 * high + y, self.place(x, high, self.low, y, self.c)

    def plane(self, step):
        shard = lax.rem(self.shard + step, SPOTS)
        return shard, self.place(shard // 4, (shard // 2) % 2, self.low, shard % 2, self.c)

    def in_sequence(self, step):
        group = lax.rem(self.tokens + step, 4)
        return group, self.place(self.x, group // 2, self.low, group % 2, self.c)

    def mates(self):
        return (
            (self.core_member, self.core_mate),
            (self.link_member, self.link_mate),
            (self.far_member, self.far_mate),
        )


def device_of(shard, member):
    return 8 * (shard // 2) + 4 * (member // 2) + 2 * (shard % 2) + member % 2


def row_piece(held, shard, half):
    return held.at[shard, half]


def group_piece(held, shard, half):
    return held.at[shard // 2, half, shard % 2]


class Post:
    def __init__(self, send_sems, recv_sems):
        self.send_sems, self.recv_sems = send_sems, recv_sems
        self.count = 0
        self.started = []

    def send(self, src, dst, to):
        copy = pltpu.make_async_remote_copy(
            src_ref=src,
            dst_ref=dst,
            send_sem=self.send_sems.at[self.count],
            recv_sem=self.recv_sems.at[self.count],
            device_id=to,
            device_id_type=MESH_ID,
        )
        copy.start()
        self.started.append(copy)
        self.count += 1
        assert self.count <= self.send_sems.shape[0]
        return self.count - 1, to

    def arrived(self, sent, landing):
        number, to = sent
        pltpu.make_async_remote_copy(
            src_ref=landing,
            dst_ref=landing,
            send_sem=self.send_sems.at[number],
            recv_sem=self.recv_sems.at[number],
            device_id=to,
            device_id_type=MESH_ID,
        ).wait_recv()

    def finish(self):
        for copy in self.started:
            copy.wait_send()


class Local:
    def __init__(self, sems):
        self.sems = sems
        self.started = []

    def copy(self, src, dst):
        copy = pltpu.make_async_copy(src, dst, self.sems.at[len(self.started)])
        copy.start()
        self.started.append(copy)
        return copy


OTHER = {"x": "y", "y": "x"}


class CubeGather:
    def __init__(self, here, post, held, piece, own=None, corner_ways="yx"):
        self.here, self.post, self.held, self.piece, self.own = here, post, held, piece, own
        self.corner_ways = corner_ways
        self.waiting = {}

    def move(self, axes, half, way):
        here = self.here
        mine = self.piece(self.held, here.across(axes)[0], half)
        src = mine if axes or self.own is None else self.own(half)
        sent = self.post.send(src, mine, here.across(way)[1])
        axes = "".join(sorted(set(axes) ^ set(way)))
        self.waiting[axes, half] = (sent, self.piece(self.held, here.across(axes)[0], half))

    def take(self, axes, half):
        self.post.arrived(*self.waiting.pop((axes, half)))

    def start(self, ways="zxy", halves=(0, 1)):
        for way in ways:
            for half in halves:
                self.move("", half, way)

    def corners(self):
        for half, way in enumerate(self.corner_ways):
            self.take(OTHER[way], half)
            self.move(OTHER[way], half, way)

    def spread(self):
        for half in (0, 1):
            self.take("z", half)
            self.move("z", half, "x")
            self.move("z", half, "y")

    def last(self):
        for half, way in enumerate(self.corner_ways):
            self.take(OTHER[way] + "z", half)
            self.move(OTHER[way] + "z", half, way)

    def finish(self):
        for key in list(self.waiting):
            self.take(*key)


class CubeSum:
    def __init__(self, here, post, parts, piece, landing, corner_ways="yx"):
        self.here, self.post, self.parts, self.piece, self.landing = here, post, parts, piece, landing
        self.corner_ways = corner_ways
        self.waiting = {}
        self.slots = 0
        self.hops = 0

    def part(self, axes, half):
        return self.piece(self.parts, self.here.across(axes)[0], half)

    def move(self, axes, half, way):
        src = self.part(axes, half)
        came = self.waiting.pop((axes, half), [])
        if came:
            value = src[...].astype(F32)
            for sent, slot in came:
                self.post.arrived(sent, slot)
                value = value + slot[...].astype(F32)
            src = came[0][1]
            src[...] = value.astype(src.dtype)
        slot = self.landing.at[self.slots]
        self.slots += 1
        sent = self.post.send(src, slot, self.here.across(way)[1])
        axes = "".join(sorted(set(axes) ^ set(way)))
        self.waiting.setdefault((axes, half), []).append((sent, slot))

    def hop(self):
        self.hops += 1
        if self.hops == 1:
            for axes in ("xyz", "xy"):
                for half, way in enumerate(self.corner_ways):
                    self.move(axes, half, way)
            for axes in ("z", ""):
                for half, way in enumerate(self.corner_ways):
                    self.move(way + axes, half, way)
        if self.hops == 2:
            for axes in ("z", ""):
                for half, way in enumerate(self.corner_ways):
                    self.move(OTHER[way] + axes, half, OTHER[way])
        if self.hops == 3:
            self.move("z", 0, "z")
            self.move("z", 1, "z")

    def total(self):
        halves = []
        for half in (0, 1):
            value = self.part("", half)[...].astype(F32)
            for sent, slot in self.waiting.pop(("", half)):
                self.post.arrived(sent, slot)
                value = value + slot[...].astype(F32)
            halves.append(value)
        return halves


HALVES = (slice(0, 64), slice(64, 128))


class GroupGather:
    def __init__(self, here, post, held):
        self.here, self.post, self.held = here, post, held
        self.over, self.core, self.passed = [], [], []

    def put(self, half):
        mine = self.piece(self.here.member, half)
        self.over.append(self.post.send(mine, mine, self.here.link_mate))
        self.core.append(self.post.send(mine, mine, self.here.core_mate))

    def piece(self, member, half):
        return self.held.at[member, HALVES[half]]

    def near(self):
        for half in (0, 1):
            self.post.arrived(self.core[half], self.piece(self.here.core_member, half))

    def rest(self, half):
        here = self.here
        linked = self.piece(here.link_member, half)
        self.post.arrived(self.over[half], linked)
        passed = self.post.send(linked, linked, here.core_mate)
        self.post.arrived(passed, self.piece(here.far_member, half))


class GroupSum:
    def __init__(self, here, post, near_send, near_in, far_send, far_in, terms):
        self.here, self.post = here, post
        self.near_send, self.near_in = near_send, near_in
        self.far_send, self.far_in = far_send, far_in
        self.terms = terms
        self.near, self.far = {}, {}

    def give(self, slot, half, value):
        here = self.here
        self.terms[slot, :, HALVES[half]] = value.reshape(2, 64, WIDTH)
        self.near_send[slot, half] = self.terms[slot, 1 - here.c, HALVES[half]].astype(BF)
        self.near[slot, half] = self.post.send(
            self.near_send.at[slot, half], self.near_in.at[slot, half], here.core_mate
        )

    def give_all(self, slot, value):
        value = value.reshape(2, ROWS, WIDTH)
        for half in (0, 1):
            self.give(slot, half, value[:, HALVES[half]])

    def cross(self, half):
        here = self.here
        self.post.arrived(self.near[0, half], self.near_in.at[0, half])
        value = self.terms[0, here.c, HALVES[half]] + self.near_in[0, half].astype(F32)
        self.far_send[half] = value.astype(BF)
        self.far[half] = self.post.send(self.far_send.at[half], self.far_in.at[half], here.link_mate)

    def total(self, half):
        self.post.arrived(self.near[1, half], self.near_in.at[1, half])
        value = self.terms[1, self.here.c, HALVES[half]] + self.near_in[1, half].astype(F32)
        self.post.arrived(self.far[half], self.far_in.at[half])
        return value + self.far_in[half].astype(F32)


class Swap:
    def __init__(self, here, post, local, src, dst):
        self.post = post
        self.sent = []
        for step in (2, 1, 3):
            group, place = here.in_sequence(step)
            came = lax.rem(here.tokens + 4 - step, 4)
            self.sent.append((post.send(src.at[group], dst.at[here.tokens], place), dst.at[came]))
        self.own = local.copy(src.at[here.tokens], dst.at[here.tokens])

    def finish(self):
        self.own.wait()
        for sent, landing in self.sent:
            self.post.arrived(sent, landing)


def out_rows_target(here):
    return here.low, here.y, here.x, here.c, here.high


def out_rows_source(here):
    return here.low, here.c, here.x, here.high, here.y


def same_place(here, spot):
    x, high, low, y, c = spot
    return (x == here.x) & (high == here.high) & (low == here.low) & (y == here.y) & (c == here.c)


def turn_tables(rot):
    index = lax.broadcasted_iota(jnp.int32, (HD // 2, 1), 0).astype(F32)
    angle = rot * jnp.exp(index * (-math.log(10000.0) / (HD // 2)))
    return jnp.cos(angle), jnp.sin(angle)


def norm_parts(value):
    centred = value - jnp.mean(value, -1, keepdims=True)
    inv_std = lax.rsqrt(jnp.mean(centred * centred, -1, keepdims=True) + norm_eps)
    return centred * inv_std, inv_std


def norm_pull(normed, inv_std, gain, upstream):
    d_normed = upstream * gain
    return inv_std * (
        d_normed
        - jnp.mean(d_normed, -1, keepdims=True)
        - normed * jnp.mean(d_normed * normed, -1, keepdims=True)
    )


def stored_at(at):
    return 2 * (at // 8) + (at // 2) % 2, 2 * ((at // 4) % 2) + at % 2


def true_group(ref, group):
    def chunk(at, late):
        tokens, member = stored_at(at)
        tile = ref[tokens, :, ROWS * member : ROWS * (member + 1)]
        return tile[:, 64:] if late else tile[:, :64]

    if group < 8:
        return jnp.concatenate([chunk(2 * group, False), chunk(2 * group + 1, False)], 1)
    return jnp.concatenate([chunk(31 - 2 * group, True), chunk(30 - 2 * group, True)], 1)


def put_stored(ref, at, values):
    def block(number):
        tile = values[:, ROWS * (number // 2) : ROWS * (number // 2) + ROWS]
        return tile[:, 64:] if number % 2 else tile[:, :64]

    tokens, member = stored_at(at)
    ref[tokens, :, ROWS * member : ROWS * (member + 1)] = jnp.concatenate(
        [block(at), block(31 - at)], 1
    ).astype(BF)


def allowed_pairs(key_at, keys, query_at, queries, start):
    key_pos = key_at + lax.broadcasted_iota(jnp.int32, (keys, queries), 0)
    allowed = key_pos >= start
    if key_at + keys > query_at:
        allowed &= key_pos <= query_at + lax.broadcasted_iota(jnp.int32, (keys, queries), 1)
    return allowed


def attend_block(qkv, start, o_true, lse, query_at, queries, keys):
    here = slice(query_at, query_at + queries)
    query, first = qkv[0:HD, here], start[:, here]
    parts, top = [], None
    for key_at in range(0, query_at + queries, keys):
        scores = dot(qkv[HD : 2 * HD, key_at : key_at + keys], query, 0, 0)
        scores = jnp.where(
            allowed_pairs(key_at, keys, query_at, queries, first), scores, masked_value
        )
        peak = jnp.max(scores, 0, keepdims=True)
        top = peak if top is None else jnp.maximum(top, peak)
        parts.append((key_at, scores))
    total, weighted = 0.0, 0.0
    for key_at, scores in parts:
        probs = jnp.exp(scores - top)
        total = total + jnp.sum(probs, 0, keepdims=True)
        weighted = weighted + dot(qkv[2 * HD :, key_at : key_at + keys], probs.astype(BF), 1, 0)
    o_true[:, here] = weighted / total
    lse[:, here] = top + jnp.log(total)


def attend_back_block(qkv, start, o_true, lse, d_out, grads, query_at, queries):
    here = slice(query_at, query_at + queries)
    reach = slice(0, query_at + queries)
    query, d_attn = qkv[0:HD, here], d_out[:, here]
    key = qkv[HD : 2 * HD, reach]
    delta = jnp.sum(d_attn.astype(F32) * o_true[:, here], 0, keepdims=True)
    allowed = allowed_pairs(0, query_at + queries, query_at, queries, start[:, here])
    probs = jnp.where(allowed, jnp.exp(dot(key, query, 0, 0) - lse[:, here]), 0.0)
    d_probs = dot(qkv[2 * HD :, reach], d_attn, 0, 0)
    d_scores = (probs * (d_probs - delta)).astype(BF)
    grads[HD : 2 * HD, reach] += dot(query, d_scores, 1, 1)
    grads[2 * HD :, reach] += dot(d_attn, probs.astype(BF), 1, 1)
    grads[0:HD, here] = dot(key, d_scores, 1, 0) * HD**-0.5


GELU_K = math.sqrt(2.0 / math.pi)


def gelu_and_slope(pre):
    square = pre * pre
    bend = jnp.tanh(GELU_K * pre * (1.0 + 0.044715 * square))
    half = 0.5 * (1.0 + bend)
    slope = half + 0.5 * pre * (1.0 - bend * bend) * GELU_K * (1.0 + 3 * 0.044715 * square)
    return pre * half, slope


def layer_kernel(
    tok_hbm, seg_hbm, cot_hbm, wq, wk, wv, wo, wu, wd, *rest
):
    norms_hbm = rest[:8]
    act, in_grad, g_down, up_got, qkv_got, out_got, g_vec = rest[8:15]
    (
        tok, cot, wqkv_own, wu_own, seg_in, norms_in,
        x_all, wqkv, wqkv_send, wu_send, small_in, small_all, wo_in, wo_all, wu_all, wd_all,
        vectors, starts, start, a_t, qkv_send, qkv_heads, qkv, o_true, lse, o_send, o_all,
        c_all, dm_all, dt_all, gl_all, slope_all, du_all, res,
        near_send, near_in, far_send, far_in, terms,
        do_send, do_heads, d_out, grads, d_send, d_in, d_all,
        down_parts, down_in, up_parts, up_in, out_parts, out_in, qkv_parts, qkv_in,
        vec_send, vec_in, vec_group, d_vec, up_send, qkv_end, out_end,
        send_sems, recv_sems, local_sems, self_sems,
    ) = rest[15:]
    here = Here()
    post = Post(send_sems, recv_sems)
    local = Local(local_sems)
    out_to, out_from = out_rows_target(here), out_rows_source(here)
    out_stays = same_place(here, out_to)
    out_moves = jnp.logical_not(out_stays)
    barrier = pltpu.get_barrier_semaphore()
    partners = [place for _, place in here.mates()] + [here.plane(n)[1] for n in range(1, SPOTS)]
    for place in partners:
        pl.semaphore_signal(barrier, inc=1, device_id=place, device_id_type=MESH_ID)

    @pl.when(out_moves)
    def _():
        for spot in (out_from, out_to):
            pl.semaphore_signal(
                barrier, inc=1, device_id=here.place(*spot), device_id_type=MESH_ID
            )

    loads = [
        local.copy(weight, wqkv_own.at[slot]) for slot, weight in enumerate((wq, wk, wv))
    ]
    load_wu = local.copy(wu, wu_own)
    load_seg = local.copy(seg_hbm, seg_in)
    load_norms = [local.copy(vector, norms_in.at[row]) for row, vector in enumerate(norms_hbm)]
    load_tok = local.copy(tok_hbm, tok)
    load_cot = local.copy(cot_hbm, cot)
    load_wd = [
        local.copy(wd.at[pl.ds(64 * half, 64)], wd_all.at[here.shard, half]) for half in (0, 1)
    ]

    lane = lax.broadcasted_iota(jnp.int32, (1, ROWS), 1)
    for row, load in enumerate(load_norms):
        load.wait()
        value = norms_in[row].astype(F32)
        value = jnp.concatenate([value] * GROUP, 1)
        small_in[here.member, row : row + 1] = jnp.where(lane // 32 == here.member, value, 0.0)
    load_seg.wait()
    small_in[here.member, 8:9] = seg_in[...].astype(F32)
    for load in loads:
        load.wait()
    for member in range(GROUP):
        base = 256 * member
        for part in range(3):
            wqkv_send[part, member] = wqkv_own[part, :, base : base + 256]
    def member_rows(held, member):
        at = pl.ds(pl.multiple_of(32 * (member % 2), 32), 32)
        return held.at[here.shard // 2, member // 2, here.shard % 2, at]

    for part in range(3):
        member_rows(wqkv.at[part], here.member)[...] = wqkv_send[part, here.member]
    load_tok.wait()
    x_all[here.member] = tok[...]

    @pl.when(out_stays)
    def _():
        pl.semaphore_wait(barrier, len(partners))

    @pl.when(out_moves)
    def _():
        pl.semaphore_wait(barrier, len(partners) + 2)

    small_sent, wqkv_sent, wu_sent = [], [], []
    for member, place in here.mates():
        mine = small_in.at[here.member]
        small_sent.append((post.send(mine, mine, place), small_in.at[member]))
    for part in range(3):
        for member, place in here.mates():
            mine, theirs = (member_rows(wqkv.at[part], who) for who in (here.member, member))
            wqkv_sent.append((post.send(wqkv_send.at[part, member], mine, place), theirs))
    down_ring = CubeGather(here, post, wd_all, row_piece, lambda half: wd.at[pl.ds(64 * half, 64)])
    down_ring.start("xy")
    x_gather = GroupGather(here, post, x_all)
    x_gather.put(0)
    x_gather.put(1)
    wo_copy = pltpu.make_async_remote_copy(
        src_ref=wo, dst_ref=wo_in, send_sem=self_sems.at[0], recv_sem=self_sems.at[1],
        device_id=here.place(*out_to), device_id_type=MESH_ID,
    )
    wo_keep = pltpu.make_async_copy(wo, wo_in, self_sems.at[2])
    pl.when(out_moves)(wo_copy.start)
    pl.when(out_stays)(wo_keep.start)
    load_wu.wait()
    for member in range(GROUP):
        for shard in range(SPOTS):
            at = ROWS * device_of(shard, member)
            wu_send[member, :, 128 * shard : 128 * (shard + 1)] = wu_own[:, at : at + 128]
    member_rows(wu_all, here.member)[...] = wu_send[here.member]
    for member, place in here.mates():
        mine, theirs = member_rows(wu_all, here.member), member_rows(wu_all, member)
        wu_sent.append((post.send(wu_send.at[member], mine, place), theirs))

    for sent, landing in small_sent:
        post.arrived(sent, landing)
    small_all[here.shard, 0:8] = (
        small_in[0, 0:8] + small_in[1, 0:8] + small_in[2, 0:8] + small_in[3, 0:8]
    )
    for member in range(GROUP):
        small_all[here.shard, 8 + member : 9 + member] = small_in[member, 8:9]
    plane_sent = []
    for step in range(1, SPOTS):
        _, place = here.plane(step)
        came = lax.rem(here.shard + SPOTS - step, SPOTS)
        mine = small_all.at[here.shard]
        plane_sent.append((post.send(mine, mine, place), small_all.at[came]))

    qkv_rings = []
    for part in range(3):
        for sent, landing in wqkv_sent[3 * part : 3 * part + 3]:
            post.arrived(sent, landing)
        qkv_rings.append(CubeGather(here, post, wqkv.at[part], group_piece))
        qkv_rings[part].start()
    down_ring.start("z")
    x_gather.near()
    for sent, landing in plane_sent:
        post.arrived(sent, landing)
    for block in range(SPOTS):
        first, cut = 2 * (block // 2), slice(64 * (block % 2), 64 * (block % 2) + 64)
        vectors[:, ROWS * block : ROWS * (block + 1)] = jnp.concatenate(
            [small_all[first, 0:8, cut], small_all[first + 1, 0:8, cut]], 1
        )
    gain, bias = vectors[0:1], vectors[1:2]

    def put_a(member):
        normed, _ = norm_parts(x_all[member].astype(F32))
        at = pl.ds(pl.multiple_of(ROWS * member, ROWS), ROWS)
        a_t[:, at] = (normed * gain + bias).astype(BF).T

    put_a(here.member)
    put_a(here.core_member)
    for ring in qkv_rings:
        ring.corners()
    x_gather.rest(0)
    x_gather.rest(1)

    @pl.when(out_moves)
    def _():
        wo_copy.wait_recv()
        wo_copy.wait_send()

    pl.when(out_stays)(wo_keep.wait)
    out_ring = CubeGather(here, post, wo_all, row_piece)
    wo_all[here.shard] = wo_in[...].reshape(2, 16, WIDTH)
    for ring in qkv_rings:
        ring.spread()
    out_ring.start()
    put_a(here.link_member)
    put_a(here.far_member)

    segs = jnp.concatenate([small_all[4 * here.x + group, 8:12] for group in range(4)], 0)
    begin = jnp.zeros_like(segs)
    for doc in range(1, 8):
        size = jnp.sum(
            jnp.sum((segs == doc - 1.0).astype(F32), 1, keepdims=True), 0, keepdims=True
        )
        begin = begin + jnp.where(segs >= doc, size, 0.0)
    starts[...] = begin
    rots = []
    for member in range(GROUP):
        at = 8 * here.high + 4 * (member // 2) + 2 * here.y + member % 2
        position = jnp.where(lane < 64, 64 * at + lane, 64 * (31 - at) + lane - 64)
        rots.append(position.astype(F32) - starts[pl.ds(4 * here.tokens + member, 1)])
    cos_t, sin_t = turn_tables(jnp.concatenate(rots, 1))
    for sent, landing in wu_sent:
        post.arrived(sent, landing)
    up_ring = CubeGather(here, post, wu_all, group_piece)
    for ring in qkv_rings:
        ring.last()
    swaps = []
    for part in range(3):
        qkv_rings[part].finish()
        product = dot(wqkv[part].reshape(WIDTH, 256), a_t[...], 0, 0)
        for head in range(4):
            rows = product[HD * head : HD * (head + 1)]
            if part < 2:
                first, second = rows[: HD // 2], rows[HD // 2 :]
                rows = jnp.concatenate(
                    [first * cos_t - second * sin_t, second * cos_t + first * sin_t], 0
                )
            if part == 0:
                rows = rows * HD**-0.5
            qkv_send[part, head] = rows.astype(BF)
        swaps.append(Swap(here, post, local, qkv_send.at[part], qkv_heads.at[part]))
    up_ring.start("xy")
    for group in range(16):
        a, b, cut = 2 * group, 2 * group + 1, slice(0, 64)
        if group >= 8:
            a, b, cut = 31 - a, 31 - b, slice(64, 128)
        a, b = (4 * tokens + member for tokens, member in (stored_at(a), stored_at(b)))
        start[:, ROWS * group : ROWS * (group + 1)] = jnp.concatenate(
            [starts[a : a + 1, cut], starts[b : b + 1, cut]], 1
        ).astype(jnp.int32)
    down_ring.corners()
    down_ring.spread()
    out_ring.corners()
    out_ring.spread()
    for part in range(3):
        swaps[part].finish()
        for group in range(16):
            at = slice(ROWS * group, ROWS * (group + 1))
            qkv[HD * part : HD * (part + 1), at] = true_group(qkv_heads.at[part], group)
    up_ring.corners()
    for query_at in range(0, 2048, 512):
        attend_block(qkv, start, o_true, lse, query_at, 512, 512)
    for at in range(16):
        put_stored(o_send, at, o_true)
    swap = Swap(here, post, local, o_send, o_all)
    up_ring.start("z")
    down_ring.last()
    out_ring.last()
    out_ring.finish()
    swap.finish()

    sums = [
        GroupSum(here, post, near_send.at[n], near_in.at[n], far_send.at[n], far_in.at[n], terms)
        for n in range(4)
    ]
    wo_flat = wo_all[...].reshape(256, WIDTH)

    def half_lanes(low):
        return pl.ds(pl.multiple_of(256 * low, 256), 256)

    def out_half(low):
        heads = [o_all[group, :, half_lanes(low)] for group in range(4)]
        return dot(jnp.concatenate(heads, 0), wo_flat, 0, 0)

    sums[0].give_all(0, out_half(1 - here.low))
    sums[0].give_all(1, out_half(here.low))
    sums[0].cross(0)
    sums[0].cross(1)
    up_ring.spread()
    up_ring.last()
    t_inv, h_inv = [None, None], [None, None]
    gather = GroupGather(here, post, c_all)
    for part, rows in enumerate(HALVES):
        t_normed, t_inv[part] = norm_parts(sums[0].total(part))
        hres = tok[rows].astype(F32) + t_normed * vectors[2:3] + vectors[3:4]
        res[0, rows] = t_normed
        h_normed, h_inv[part] = norm_parts(hres)
        res[1, rows] = h_normed
        res[2, rows] = hres
        c_all[here.member, rows] = (h_normed * vectors[4:5] + vectors[5:6]).astype(BF)
        gather.put(part)
    gather.near()
    up_ring.finish()
    wu_flat = wu_all[...].reshape(WIDTH, WIDTH)

    def pair(held, low, rows=slice(0, ROWS)):
        value = held[pl.ds(2 * low, 2), rows]
        return value.reshape(-1, WIDTH)

    def set_pair(held, low, rows, value):
        held[pl.ds(2 * low, 2), rows] = value.reshape(2, -1, WIDTH)

    whole = slice(0, ROWS)

    def up_rows(low, rows):
        gl, slope = gelu_and_slope(dot(pair(c_all, low, rows), wu_flat, 1, 0))
        set_pair(gl_all, low, rows, gl.astype(BF))
        set_pair(slope_all, low, rows, slope)

    up_rows(here.low, whole)
    for part, rows in enumerate(HALVES):
        gather.rest(part)
        up_rows(1 - here.low, rows)
        if part == 0:
            for load in load_wd:
                load.wait()
            down_ring.finish()
            wd_flat = wd_all[...].reshape(WIDTH, WIDTH)
        sums[1].give(0, part, dot(pair(gl_all, 1 - here.low, rows), wd_flat, 1, 0))
        sums[1].cross(part)
    sums[1].give_all(1, dot(pair(gl_all, here.low), wd_flat, 1, 0))
    load_cot.wait()
    gather = GroupGather(here, post, dm_all)
    d_gain, d_bias = 0.0, 0.0
    for part, rows in enumerate(HALVES):
        m_normed, m_inv = norm_parts(sums[1].total(part))
        upstream = cot[rows].astype(F32)
        dm_all[here.member, rows] = norm_pull(m_normed, m_inv, vectors[6:7], upstream).astype(BF)
        gather.put(part)
        act[rows] = (res[2, rows] + m_normed * vectors[6:7] + vectors[7:8]).astype(BF)
        d_gain = d_gain + jnp.sum(upstream * m_normed, 0, keepdims=True)
        d_bias = d_bias + jnp.sum(upstream, 0, keepdims=True)
    d_vec[6:7] = d_gain
    d_vec[7:8] = d_bias
    gather.near()

    def du_rows(low, rows):
        d_gl = dot(pair(dm_all, low, rows), wd_flat, 1, 1)
        set_pair(du_all, low, rows, (d_gl * pair(slope_all, low, rows)).astype(BF))

    def put_down(axes):
        shard = here.across(axes)[0]
        gl = gl_all[:, :, pl.ds(pl.multiple_of(ROWS * shard, ROWS), ROWS)].reshape(512, ROWS)
        down_parts[shard] = dot(gl, dm_flat, 0, 0).astype(BF).reshape(2, 64, WIDTH)

    down_sum = CubeSum(here, post, down_parts, row_piece, down_in)
    du_rows(here.low, whole)
    sums[2].give_all(1, dot(pair(du_all, here.low), wu_flat, 1, 1))
    for part, rows in enumerate(HALVES):
        gather.rest(part)
        if part == 1:
            dm_flat = dm_all[...].reshape(512, WIDTH)
            for axes in ("xyz", "xy", "xz", "yz", "x", "y"):
                put_down(axes)
            down_sum.hop()
        du_rows(1 - here.low, rows)
        sums[2].give(0, part, dot(pair(du_all, 1 - here.low, rows), wu_flat, 1, 1))
        if part == 0:
            sums[2].cross(part)
    sums[2].cross(1)
    for axes in ("", "z"):
        put_down(axes)
    up_sum = CubeSum(here, post, up_parts, group_piece, up_in)
    out_sum = CubeSum(here, post, out_parts, row_piece, out_in)
    qkv_sums = [
        CubeSum(here, post, qkv_parts.at[part], group_piece, qkv_in.at[part]) for part in range(3)
    ]
    du_flat = du_all[...].reshape(512, WIDTH)
    c_flat = c_all[...].reshape(512, WIDTH)
    down_sum.hop()
    for block in range(SPOTS):
        term = dot(c_flat[:, ROWS * block : ROWS * (block + 1)], du_flat, 0, 0)
        up_parts[block // 2, block % 2] = term.astype(BF).reshape(2, 64, WIDTH)
    up_sum.hop()
    gather = GroupGather(here, post, dt_all)
    d_mi = [0.0, 0.0]
    d_ao = [0.0, 0.0]
    for part, rows in enumerate(HALVES):
        d_c = sums[2].total(part)
        h_normed, t_normed = res[1, rows], res[0, rows]
        d_h = cot[rows].astype(F32) + norm_pull(h_normed, h_inv[part], vectors[4:5], d_c)
        dt_all[here.member, rows] = norm_pull(t_normed, t_inv[part], vectors[2:3], d_h).astype(BF)
        gather.put(part)
        res[2, rows] = d_h
        d_mi[0] = d_mi[0] + jnp.sum(d_c * h_normed, 0, keepdims=True)
        d_mi[1] = d_mi[1] + jnp.sum(d_c, 0, keepdims=True)
        d_ao[0] = d_ao[0] + jnp.sum(d_h * t_normed, 0, keepdims=True)
        d_ao[1] = d_ao[1] + jnp.sum(d_h, 0, keepdims=True)
    d_vec[4:5], d_vec[5:6] = d_mi
    d_vec[2:3], d_vec[3:4] = d_ao
    down_sum.hop()
    gather.near()
    gather.rest(0)
    gather.rest(1)
    dt_flat = dt_all[...].reshape(512, WIDTH)
    d_o = dot(wo_flat, dt_flat, 1, 1)
    for head in range(4):
        do_send[head] = d_o[HD * head : HD * (head + 1)].astype(BF)
    swap = Swap(here, post, local, do_send, do_heads)
    o_flat = o_all[...].reshape(256, 512)
    out_parts[...] = dot(o_flat, dt_flat, 1, 0).astype(BF).reshape(SPOTS, 2, 16, WIDTH)
    out_sum.hop()
    up_sum.hop()
    swap.finish()
    for group in range(16):
        d_out[:, ROWS * group : ROWS * (group + 1)] = true_group(do_heads, group)
    grads[HD:] = jnp.zeros((2 * HD, 2048), F32)
    for query_at in range(0, 2048, 256):
        attend_back_block(qkv, start, o_true, lse, d_out, grads, query_at, 256)
        if query_at == 1536:
            out_sum.hop()
    for at in range(16):
        put_stored(d_send.at[2], at, grads[2 * HD :])
    swaps = [Swap(here, post, local, d_send.at[2], d_in.at[2])]
    position = lax.broadcasted_iota(jnp.int32, (1, 2048), 1) - start[...]
    cos_t, sin_t = turn_tables(position.astype(F32))
    for part in (1, 0):
        first = grads[HD * part : HD * part + HD // 2]
        second = grads[HD * part + HD // 2 : HD * (part + 1)]
        turned = jnp.concatenate([first * cos_t + second * sin_t, second * cos_t - first * sin_t], 0)
        for at in range(16):
            put_stored(d_send.at[part], at, turned)
        swaps.append(Swap(here, post, local, d_send.at[part], d_in.at[part]))
    low_half, high_half = down_sum.total()
    g_down[0:64] = low_half
    g_down[64:128] = high_half
    for number, part in enumerate((2, 1, 0)):
        swaps[number].finish()
        if number == 2:
            up_sum.hop()
            out_sum.hop()
        d_all[256 * part : 256 * (part + 1)] = d_in[part].reshape(256, 512)
        for block in range(SPOTS):
            term = dot(
                a_t[ROWS * block : ROWS * (block + 1)], d_all[256 * part : 256 * (part + 1)], 1, 1
            )
            qkv_parts[part, block // 2, block % 2] = term.astype(BF).reshape(2, 64, 256)
        qkv_sums[part].hop()
        if number:
            qkv_sums[part + 1].hop()
    qkv_sums[2].hop()
    wqkv_flat = [wqkv[part].reshape(WIDTH, 256) for part in range(3)]

    def in_half(low):
        terms = [
            dot(d_all[256 * part : 256 * (part + 1), half_lanes(low)], wqkv_flat[part], 0, 1)
            for part in range(3)
        ]
        return terms[0] + terms[1] + terms[2]

    sums[3].give_all(0, in_half(1 - here.low))
    sums[3].give_all(1, in_half(here.low))
    sums[3].cross(0)
    sums[3].cross(1)
    qkv_sums[0].hop()
    qkv_sums[1].hop()
    low_half, high_half = up_sum.total()
    for member in range(GROUP):
        halved = low_half if member < 2 else high_half
        up_send[member] = halved[32 * (member % 2) : 32 * (member % 2) + 32].astype(BF)
    up_got[here.member] = up_send[here.member]
    ends = []
    for member, place in here.mates():
        ends.append((post.send(up_send.at[member], up_got.at[here.member], place), up_got.at[member]))
    low_half, high_half = out_sum.total()
    out_end[0:16] = low_half.astype(BF)
    out_end[16:32] = high_half.astype(BF)
    out_copy = pltpu.make_async_remote_copy(
        src_ref=out_end, dst_ref=out_got, send_sem=self_sems.at[3], recv_sem=self_sems.at[4],
        device_id=here.place(*out_from), device_id_type=MESH_ID,
    )
    pl.when(out_moves)(out_copy.start)

    @pl.when(out_stays)
    def _():
        out_got[...] = out_end[...]

    d_gain, d_bias = 0.0, 0.0
    for part, rows in enumerate(HALVES):
        d_a = sums[3].total(part)
        normed, inv_std = norm_parts(tok[rows].astype(F32))
        in_grad[rows] = res[2, rows] + norm_pull(normed, inv_std, vectors[0:1], d_a)
        d_gain = d_gain + jnp.sum(d_a * normed, 0, keepdims=True)
        d_bias = d_bias + jnp.sum(d_a, 0, keepdims=True)
    d_vec[0:1] = d_gain
    d_vec[1:2] = d_bias
    for shard in range(SPOTS):
        at = 256 * (shard // 2) + 64 * (shard % 2)
        vec_send[shard] = jnp.concatenate(
            [d_vec[:, at : at + 64], d_vec[:, at + ROWS : at + ROWS + 64]], 1
        )
    vec_in[here.shard] = vec_send[here.shard]
    vec_sent = []
    for step in range(1, SPOTS):
        shard, place = here.plane(step)
        came = lax.rem(here.shard + SPOTS - step, SPOTS)
        vec_sent.append((post.send(vec_send.at[shard], vec_in.at[here.shard], place), vec_in.at[came]))
    qkv_sums[0].hop()
    for sent, landing in vec_sent:
        post.arrived(sent, landing)
    total = vec_in[0]
    for shard in range(1, SPOTS):
        total = total + vec_in[shard]
    vec_group[here.member] = total
    vec_sent = []
    for member, place in here.mates():
        mine = vec_group.at[here.member]
        vec_sent.append((post.send(mine, mine, place), vec_group.at[member]))
    for sent, landing in ends:
        post.arrived(sent, landing)

    @pl.when(out_moves)
    def _():
        out_copy.wait_recv()
        out_copy.wait_send()

    ends = []
    for part in (2, 1, 0):
        low_half, high_half = qkv_sums[part].total()
        for member in range(GROUP):
            halved = low_half if member < 2 else high_half
            qkv_end[part, member] = halved[32 * (member % 2) : 32 * (member % 2) + 32].astype(BF)
        qkv_got[part, here.member] = qkv_end[part, here.member]
        for member, place in here.mates():
            sent = post.send(qkv_end.at[part, member], qkv_got.at[part, here.member], place)
            ends.append((sent, qkv_got.at[part, member]))
    for sent, landing in vec_sent:
        post.arrived(sent, landing)
    total = vec_group[0] + vec_group[1] + vec_group[2] + vec_group[3]
    mine = total[:, 0:32]
    for member in range(1, GROUP):
        mine = jnp.where(here.member == member, total[:, 32 * member : 32 * (member + 1)], mine)
    g_vec[...] = mine
    for sent, landing in ends:
        post.arrived(sent, landing)
    post.finish()


def call_layer(*args):
    vmem = pl.BlockSpec(memory_space=pltpu.VMEM)
    anywhere = pl.BlockSpec(memory_space=pl.ANY)
    shape = jax.ShapeDtypeStruct
    dma = pltpu.SemaphoreType.DMA

    def held(*dims, kind=BF):
        return pltpu.VMEM(dims, kind)

    rows = (GROUP, ROWS, WIDTH)
    return pl.pallas_call(
        layer_kernel,
        out_shape=[
            shape((ROWS, WIDTH), BF),
            shape((ROWS, WIDTH), F32),
            shape((ROWS, WIDTH), F32),
            shape((GROUP, 32, WIDTH), BF),
            shape((3, GROUP, 32, 256), BF),
            shape((32, WIDTH), BF),
            shape((8, 32), F32),
        ],
        in_specs=[anywhere] * 17,
        out_specs=[vmem] * 7,
        scratch_shapes=[
            held(ROWS, WIDTH), held(ROWS, WIDTH), held(3, 32, WIDTH), held(32, 4 * WIDTH),
            held(1, ROWS, kind=jnp.int32), held(8, 1, 32),
            held(*rows), held(3, 4, 2, 2, 64, 256), held(3, GROUP, 32, 256), held(GROUP, 32, WIDTH),
            held(GROUP, 16, ROWS, kind=F32), held(SPOTS, 16, ROWS, kind=F32),
            held(32, WIDTH), held(SPOTS, 2, 16, WIDTH), held(4, 2, 2, 64, WIDTH), held(SPOTS, 2, 64, WIDTH),
            held(8, WIDTH, kind=F32), held(16, ROWS, kind=F32), held(1, 2048, kind=jnp.int32),
            held(WIDTH, 512), held(3, 4, HD, 512), held(3, 4, HD, 512), held(192, 2048),
            held(HD, 2048, kind=F32), held(1, 2048, kind=F32), held(4, HD, 512), held(4, HD, 512),
            held(*rows), held(*rows), held(*rows), held(*rows), held(*rows, kind=F32), held(*rows),
            held(3, ROWS, WIDTH, kind=F32),
            held(4, 2, 2, 64, WIDTH), held(4, 2, 2, 64, WIDTH), held(4, 2, 64, WIDTH), held(4, 2, 64, WIDTH),
            held(2, 2, ROWS, WIDTH, kind=F32),
            held(4, HD, 512), held(4, HD, 512), held(HD, 2048), held(192, 2048, kind=F32),
            held(3, 4, HD, 512), held(3, 4, HD, 512), held(768, 512),
            held(SPOTS, 2, 64, WIDTH), held(14, 64, WIDTH),
            held(4, 2, 2, 64, WIDTH), held(14, 64, WIDTH),
            held(SPOTS, 2, 16, WIDTH), held(14, 16, WIDTH),
            held(3, 4, 2, 2, 64, 256), held(3, 14, 64, 256),
            held(SPOTS, 8, ROWS, kind=F32), held(SPOTS, 8, ROWS, kind=F32), held(GROUP, 8, ROWS, kind=F32),
            held(8, WIDTH, kind=F32), held(GROUP, 32, WIDTH), held(3, GROUP, 32, 256), held(32, WIDTH),
            dma((300,)), dma((300,)), dma((40,)), dma((5,)),
        ],
        compiler_params=pltpu.CompilerParams(
            collective_id=0, has_side_effects=True, vmem_limit_bytes=VMEM_BYTES
        ),
        name="layer",
    )(*args)


def finish_kernel(
    act_in, grad_in, down_in, up_got, qkv_got, out_got, vec,
    act, in_grad, g_q, g_k, g_v, g_out, g_up, g_down, *g_norms
):
    act[...] = act_in[...]
    in_grad[...] = grad_in[...]
    g_down[...] = down_in[...]
    g_out[...] = out_got[...].astype(F32)
    for member in range(GROUP):
        for shard in range(SPOTS):
            at = ROWS * device_of(shard, member)
            g_up[:, at : at + 128] = up_got[member, :, 128 * shard : 128 * (shard + 1)].astype(F32)
        base = 256 * member
        for slot, out in enumerate((g_q, g_k, g_v)):
            out[:, base : base + 256] = qkv_got[slot, member].astype(F32)
    for row, out in enumerate(g_norms):
        out[...] = vec[row : row + 1]


def call_finish(*args):
    vmem = pl.BlockSpec(memory_space=pltpu.VMEM)
    shape = jax.ShapeDtypeStruct
    narrow = shape((32, WIDTH), F32)
    return pl.pallas_call(
        finish_kernel,
        out_shape=[
            shape((ROWS, WIDTH), BF), shape((ROWS, WIDTH), F32), narrow, narrow, narrow, narrow,
            shape((32, 4 * WIDTH), F32), shape((ROWS, WIDTH), F32),
        ] + [shape((1, 32), F32)] * 8,
        in_specs=[vmem] * 7,
        out_specs=[vmem] * 16,
        compiler_params=pltpu.CompilerParams(vmem_limit_bytes=VMEM_BYTES),
        name="finish",
    )(*args)


def on_device_grouped(tokens, segments, cotangent, *params):
    weights, norms = params[:6], params[6:]
    results = call_layer(
        tokens[0], segments, cotangent[0], *weights, *[vector[None] for vector in norms]
    )
    outs = call_finish(*results)
    act, in_grad, *rest = outs
    return (act[None], in_grad[None], *rest[:6]) + tuple(vector[0] for vector in rest[6:])


def solution(mesh):
    in_specs = (
        P("dp", "ctx", None),
        P("dp", "ctx"),
        P("dp", "ctx", None),
        P(("dp", "ctx"), None),
        P(("dp", "ctx"), None),
        P(("dp", "ctx"), None),
        P(("dp", "ctx"), None),
        P(("dp", "ctx"), None),
        P(("dp", "ctx"), None),
        P(("dp", "ctx")),
        P(("dp", "ctx")),
        P(("dp", "ctx")),
        P(("dp", "ctx")),
        P(("dp", "ctx")),
        P(("dp", "ctx")),
        P(("dp", "ctx")),
        P(("dp", "ctx")),
    )
    out_specs = (
        P("dp", "ctx", None),
        P("dp", "ctx", None),
        P(("dp", "ctx"), None),
        P(("dp", "ctx"), None),
        P(("dp", "ctx"), None),
        P(("dp", "ctx"), None),
        P(("dp", "ctx"), None),
        P(("dp", "ctx"), None),
        P(("dp", "ctx")),
        P(("dp", "ctx")),
        P(("dp", "ctx")),
        P(("dp", "ctx")),
        P(("dp", "ctx")),
        P(("dp", "ctx")),
        P(("dp", "ctx")),
        P(("dp", "ctx")),
    )
    grouped = mesh.shape["dp"] == 2 and mesh.shape["ctx"] == 16
    return jax.shard_map(
        on_device_grouped if grouped else on_device, mesh=mesh, in_specs=in_specs, out_specs=out_specs, check_vma=False
    )
```

```python
import math

import jax
import jax.numpy as jnp
from jax import lax
from jax.experimental import pallas as pl
from jax.experimental.pallas import tpu as pltpu
from jax.sharding import PartitionSpec as P

HEADS = 16
HD = 64


norm_eps = 1e-05
masked_value = -1e30


def layer_norm(value, gain, bias):
    row_mean = jnp.mean(value, -1, keepdims=True)
    centred = value - row_mean
    scaled = centred * lax.rsqrt(jnp.mean(centred * centred, -1, keepdims=True) + norm_eps)
    return scaled * gain + bias


def norm_back(value, gain, upstream):
    row_mean = jnp.mean(value, -1, keepdims=True)
    centred = value - row_mean
    inv_std = lax.rsqrt(jnp.mean(centred * centred, -1, keepdims=True) + norm_eps)
    normed = centred * inv_std
    d_normed = upstream * gain
    d_value = inv_std * (
        d_normed
        - jnp.mean(d_normed, -1, keepdims=True)
        - normed * jnp.mean(d_normed * normed, -1, keepdims=True)
    )
    return (d_value, jnp.sum(upstream * normed, 0), jnp.sum(upstream, 0))


def rope_tables(offsets, head_dim):
    freq = 10000.0 ** (-jnp.arange(head_dim // 2, dtype=jnp.float32) / (head_dim // 2))
    angle = offsets.astype(jnp.float32)[..., None] * freq
    return (jnp.cos(angle)[..., None, :], jnp.sin(angle)[..., None, :])


def rotate(values, cos_t, sin_t):
    half_dim = values.shape[-1] // 2
    first = values[..., :half_dim]
    second = values[..., half_dim:]
    return jnp.concatenate([first * cos_t - second * sin_t, second * cos_t + first * sin_t], -1)


def unrotate(grads, cos_t, sin_t):
    half_dim = grads.shape[-1] // 2
    first = grads[..., :half_dim]
    second = grads[..., half_dim:]
    return jnp.concatenate([first * cos_t + second * sin_t, second * cos_t - first * sin_t], -1)


def true_position(flat_index, row_count, ctx_size):
    device_of = flat_index // row_count
    offset_in = flat_index % row_count
    half_rows = row_count // 2
    return jnp.where(
        offset_in < half_rows,
        device_of * half_rows + offset_in,
        (2 * ctx_size - 1 - device_of) * half_rows + offset_in - half_rows,
    )


def split_blocks(array, block_rows):
    return array.reshape((array.shape[0] // block_rows, block_rows) + array.shape[1:])


def score_block(queries, keys, query_pos, query_seg, key_pos, key_seg):
    scores = jnp.einsum(
        "qhd,khd->hqk", queries, keys, preferred_element_type=jnp.float32
    ) * queries.shape[-1] ** (-0.5)
    allowed = (query_seg[:, None] == key_seg[None, :]) & (key_pos[None, :] <= query_pos[:, None])
    return (scores, allowed[None])


def grad_block(queries, d_attn, lse, delta, keys, values, query_pos, query_seg, key_pos, key_seg):
    scores, allowed = score_block(queries, keys, query_pos, query_seg, key_pos, key_seg)
    attn_probs = jnp.where(allowed, jnp.exp(scores - lse[:, :, None]), 0.0)
    d_probs = jnp.einsum("qhd,khd->hqk", d_attn, values, preferred_element_type=jnp.float32)
    d_scores = (attn_probs * (d_probs - delta[:, :, None])).astype(jnp.bfloat16)
    return (attn_probs, d_scores)


def key_terms(
    query_rows,
    dattn_rows,
    lse_rows,
    delta_rows,
    query_pos,
    query_seg,
    key_block,
    value_block,
    key_pos,
    key_seg,
):
    attn_probs, d_scores = grad_block(
        query_rows,
        dattn_rows,
        lse_rows,
        delta_rows,
        key_block,
        value_block,
        query_pos,
        query_seg,
        key_pos,
        key_seg,
    )
    d_keys = jnp.einsum(
        "hqk,qhd->khd", d_scores, query_rows, preferred_element_type=jnp.float32
    ) * query_rows.shape[-1] ** (-0.5)
    d_values = jnp.einsum(
        "hqk,qhd->khd",
        attn_probs.astype(jnp.bfloat16),
        dattn_rows,
        preferred_element_type=jnp.float32,
    )
    return (d_keys, d_values)


def on_device(
    tokens,
    segments,
    cotangent,
    w_query,
    w_key,
    w_value,
    w_out,
    w_up,
    w_down,
    gain_attn_in,
    bias_attn_in,
    gain_attn_out,
    bias_attn_out,
    gain_mlp_in,
    bias_mlp_in,
    gain_mlp_out,
    bias_mlp_out,
):
    whole = (
        lax.all_gather(w_query, ("dp", "ctx"), axis=0, tiled=True),
        lax.all_gather(w_key, ("dp", "ctx"), axis=0, tiled=True),
        lax.all_gather(w_value, ("dp", "ctx"), axis=0, tiled=True),
        lax.all_gather(w_out, ("dp", "ctx"), axis=0, tiled=True),
        lax.all_gather(w_up, ("dp", "ctx"), axis=0, tiled=True),
        lax.all_gather(w_down, ("dp", "ctx"), axis=0, tiled=True),
        lax.all_gather(gain_attn_in, ("dp", "ctx"), axis=0, tiled=True),
        lax.all_gather(bias_attn_in, ("dp", "ctx"), axis=0, tiled=True),
        lax.all_gather(gain_attn_out, ("dp", "ctx"), axis=0, tiled=True),
        lax.all_gather(bias_attn_out, ("dp", "ctx"), axis=0, tiled=True),
        lax.all_gather(gain_mlp_in, ("dp", "ctx"), axis=0, tiled=True),
        lax.all_gather(bias_mlp_in, ("dp", "ctx"), axis=0, tiled=True),
        lax.all_gather(gain_mlp_out, ("dp", "ctx"), axis=0, tiled=True),
        lax.all_gather(bias_mlp_out, ("dp", "ctx"), axis=0, tiled=True),
    )
    query_w, key_w, value_w, out_w, up_w, down_w = whole[:6]
    gain_ai, bias_ai, gain_ao, bias_ao, gain_mi, bias_mi, gain_mo, bias_mo = [
        entry.astype(jnp.float32) for entry in whole[6:]
    ]
    row_count = tokens.shape[1]
    model_width = tokens.shape[2]
    ctx_size = lax.axis_size("ctx")
    seq_length = row_count * ctx_size
    score_scale = HD ** (-0.5)
    seg_all = lax.all_gather(segments, "ctx", axis=1, tiled=True)[0]
    my_seg = segments[0]
    all_pos = true_position(jnp.arange(seq_length, dtype=jnp.int32), row_count, ctx_size)
    my_pos = true_position(
        lax.axis_index("ctx") * row_count + jnp.arange(row_count, dtype=jnp.int32),
        row_count,
        ctx_size,
    )
    doc_first = jnp.min(
        jnp.where(seg_all[None, :] == my_seg[:, None], all_pos[None, :], seq_length), axis=1
    )
    cos_t, sin_t = rope_tables(my_pos - doc_first, HD)
    inputs = tokens[0].astype(jnp.float32)
    attn_in = layer_norm(inputs, gain_ai, bias_ai).astype(jnp.bfloat16)
    query_pre = jnp.dot(attn_in, query_w, preferred_element_type=jnp.float32).reshape(
        row_count, HEADS, HD
    )
    key_pre = jnp.dot(attn_in, key_w, preferred_element_type=jnp.float32).reshape(
        row_count, HEADS, HD
    )
    queries = rotate(query_pre, cos_t, sin_t).astype(jnp.bfloat16)
    keys_rot = rotate(key_pre, cos_t, sin_t).astype(jnp.bfloat16)
    values_flat = jnp.dot(attn_in, value_w, preferred_element_type=jnp.float32).astype(jnp.bfloat16)
    values_heads = values_flat.reshape(row_count, HEADS, HD)
    keys_flat = keys_rot.reshape(row_count, model_width)
    start_state = (
        jnp.full((HEADS, row_count), masked_value, jnp.float32),
        jnp.zeros((HEADS, row_count), jnp.float32),
        jnp.zeros((row_count, HEADS, HD), jnp.float32),
    )
    key_rows = lax.all_gather(keys_flat, "ctx", axis=0, tiled=True)
    value_rows = lax.all_gather(values_flat, "ctx", axis=0, tiled=True)
    span = key_rows.shape[0]
    block_rows = math.gcd(span, 1024)
    key_pos = true_position(jnp.arange(span, dtype=jnp.int32), row_count, ctx_size)
    key_seg = seg_all

    def visit(state_now, parts):
        row_top, row_total, weighted = state_now
        key_block = parts[0].reshape(block_rows, HEADS, HD)
        value_block = parts[1].reshape(block_rows, HEADS, HD)
        scores, allowed = score_block(queries, key_block, my_pos, my_seg, parts[2], parts[3])
        top_new = jnp.maximum(row_top, jnp.max(jnp.where(allowed, scores, masked_value), -1))
        fade = jnp.exp(row_top - top_new)
        attn_probs = jnp.where(allowed, jnp.exp(scores - top_new[:, :, None]), 0.0)
        row_total = row_total * fade + jnp.sum(attn_probs, -1)
        weighted = weighted * fade.T[:, :, None] + jnp.einsum(
            "hqk,khd->qhd",
            attn_probs.astype(jnp.bfloat16),
            value_block,
            preferred_element_type=jnp.float32,
        )
        return ((top_new, row_total, weighted), None)

    blocks = (
        split_blocks(key_rows, block_rows),
        split_blocks(value_rows, block_rows),
        split_blocks(key_pos, block_rows),
        split_blocks(key_seg, block_rows),
    )
    row_top, row_total, weighted = lax.scan(visit, start_state, blocks)[0]
    lse = row_top + jnp.log(row_total)
    attn_f = weighted / row_total.T[:, :, None]
    attn_b = attn_f.reshape(row_count, model_width).astype(jnp.bfloat16)
    branch = jnp.dot(attn_b, out_w, preferred_element_type=jnp.float32)
    resid = inputs + layer_norm(branch, gain_ao, bias_ao)
    mlp_in = layer_norm(resid, gain_mi, bias_mi).astype(jnp.bfloat16)
    hidden_pre = jnp.dot(mlp_in, up_w, preferred_element_type=jnp.float32)
    hidden = jax.nn.gelu(hidden_pre, approximate=True).astype(jnp.bfloat16)
    mlp_out = jnp.dot(hidden, down_w, preferred_element_type=jnp.float32)
    result = resid + layer_norm(mlp_out, gain_mo, bias_mo)
    upstream = cotangent[0].astype(jnp.float32)
    d_mlp_out, dgain_mo, dbias_mo = norm_back(mlp_out, gain_mo, upstream)
    d_mlp_b = d_mlp_out.astype(jnp.bfloat16)
    grad_down = jnp.dot(hidden.T, d_mlp_b, preferred_element_type=jnp.float32)
    d_hidden = jnp.dot(d_mlp_b, down_w.T, preferred_element_type=jnp.float32)
    gelu_back = jax.vjp(lambda pre: jax.nn.gelu(pre, approximate=True), hidden_pre)[1]
    d_pre = gelu_back(d_hidden)[0].astype(jnp.bfloat16)
    grad_up = jnp.dot(mlp_in.T, d_pre, preferred_element_type=jnp.float32)
    d_mlp_in = jnp.dot(d_pre, up_w.T, preferred_element_type=jnp.float32)
    d_resid_n, dgain_mi, dbias_mi = norm_back(resid, gain_mi, d_mlp_in)
    d_resid = upstream + d_resid_n
    d_branch, dgain_ao, dbias_ao = norm_back(branch, gain_ao, d_resid)
    d_branch_b = d_branch.astype(jnp.bfloat16)
    grad_out = jnp.dot(attn_b.T, d_branch_b, preferred_element_type=jnp.float32)
    d_attn_flat = jnp.dot(d_branch_b, out_w.T, preferred_element_type=jnp.float32).astype(
        jnp.bfloat16
    )
    d_attn = d_attn_flat.reshape(row_count, HEADS, HD)
    delta = jnp.sum(d_attn.astype(jnp.float32) * attn_f, -1).T
    zero_heads = jnp.zeros((row_count, HEADS, HD), jnp.float32)

    def query_grad(dq_now, key_rows, value_rows, key_pos, key_seg):
        block_rows = math.gcd(key_rows.shape[0], 1024)

        def visit(dq_run, parts):
            key_block = parts[0].reshape(block_rows, HEADS, HD)
            value_block = parts[1].reshape(block_rows, HEADS, HD)
            d_scores = grad_block(
                queries,
                d_attn,
                lse,
                delta,
                key_block,
                value_block,
                my_pos,
                my_seg,
                parts[2],
                parts[3],
            )[1]
            return (
                dq_run
                + jnp.einsum(
                    "hqk,khd->qhd", d_scores, key_block, preferred_element_type=jnp.float32
                )
                * score_scale,
                None,
            )

        blocks = (
            split_blocks(key_rows, block_rows),
            split_blocks(value_rows, block_rows),
            split_blocks(key_pos, block_rows),
            split_blocks(key_seg, block_rows),
        )
        return lax.scan(visit, dq_now, blocks)[0]

    lse_all, delta_all = (
        lax.all_gather(lse.T, "ctx", axis=0, tiled=True),
        lax.all_gather(delta.T, "ctx", axis=0, tiled=True),
    )
    query_rows = lax.all_gather(queries.reshape(row_count, model_width), "ctx", axis=0, tiled=True)
    dattn_rows = lax.all_gather(d_attn_flat, "ctx", axis=0, tiled=True)
    span = query_rows.shape[0]
    query_block_rows = math.gcd(span, 1024)
    query_pos = true_position(jnp.arange(span, dtype=jnp.int32), row_count, ctx_size)

    def visit(sums, parts):
        d_keys, d_values = key_terms(
            parts[0].reshape(query_block_rows, HEADS, HD),
            parts[1].reshape(query_block_rows, HEADS, HD),
            parts[2].T,
            parts[3].T,
            parts[4],
            parts[5],
            keys_rot,
            values_heads,
            my_pos,
            my_seg,
        )
        return ((sums[0] + d_keys, sums[1] + d_values), None)

    blocks = (
        split_blocks(query_rows, query_block_rows),
        split_blocks(dattn_rows, query_block_rows),
        split_blocks(lse_all, query_block_rows),
        split_blocks(delta_all, query_block_rows),
        split_blocks(query_pos, query_block_rows),
        split_blocks(seg_all, query_block_rows),
    )
    dk_rot, dv_sum = lax.scan(visit, (zero_heads, zero_heads), blocks)[0]
    pieces = (
        lax.all_gather(keys_flat, "ctx", axis=0, tiled=True),
        lax.all_gather(values_flat, "ctx", axis=0, tiled=True),
    )
    span = pieces[0].shape[0]
    key_pos = true_position(jnp.arange(span, dtype=jnp.int32), row_count, ctx_size)
    key_seg = seg_all
    dq_rot = query_grad(zero_heads, pieces[0], pieces[1], key_pos, key_seg)
    d_query = unrotate(dq_rot, cos_t, sin_t).reshape(row_count, model_width).astype(jnp.bfloat16)
    d_key = unrotate(dk_rot, cos_t, sin_t).reshape(row_count, model_width).astype(jnp.bfloat16)
    d_value = dv_sum.reshape(row_count, model_width).astype(jnp.bfloat16)
    grad_query = jnp.dot(attn_in.T, d_query, preferred_element_type=jnp.float32)
    grad_key = jnp.dot(attn_in.T, d_key, preferred_element_type=jnp.float32)
    grad_value = jnp.dot(attn_in.T, d_value, preferred_element_type=jnp.float32)
    d_attn_in = (
        jnp.dot(d_query, query_w.T, preferred_element_type=jnp.float32)
        + jnp.dot(d_key, key_w.T, preferred_element_type=jnp.float32)
        + jnp.dot(d_value, value_w.T, preferred_element_type=jnp.float32)
    )
    d_inputs_n, dgain_ai, dbias_ai = norm_back(inputs, gain_ai, d_attn_in)
    input_grad = (d_resid + d_inputs_n)[None]
    shares = (
        lax.psum_scatter(grad_query, ("dp", "ctx"), scatter_dimension=0, tiled=True),
        lax.psum_scatter(grad_key, ("dp", "ctx"), scatter_dimension=0, tiled=True),
        lax.psum_scatter(grad_value, ("dp", "ctx"), scatter_dimension=0, tiled=True),
        lax.psum_scatter(grad_out, ("dp", "ctx"), scatter_dimension=0, tiled=True),
        lax.psum_scatter(grad_up, ("dp", "ctx"), scatter_dimension=0, tiled=True),
        lax.psum_scatter(grad_down, ("dp", "ctx"), scatter_dimension=0, tiled=True),
        lax.psum_scatter(dgain_ai, ("dp", "ctx"), scatter_dimension=0, tiled=True),
        lax.psum_scatter(dbias_ai, ("dp", "ctx"), scatter_dimension=0, tiled=True),
        lax.psum_scatter(dgain_ao, ("dp", "ctx"), scatter_dimension=0, tiled=True),
        lax.psum_scatter(dbias_ao, ("dp", "ctx"), scatter_dimension=0, tiled=True),
        lax.psum_scatter(dgain_mi, ("dp", "ctx"), scatter_dimension=0, tiled=True),
        lax.psum_scatter(dbias_mi, ("dp", "ctx"), scatter_dimension=0, tiled=True),
        lax.psum_scatter(dgain_mo, ("dp", "ctx"), scatter_dimension=0, tiled=True),
        lax.psum_scatter(dbias_mo, ("dp", "ctx"), scatter_dimension=0, tiled=True),
    )
    return (result.astype(jnp.bfloat16)[None], input_grad) + tuple(shares)


BF = jnp.bfloat16
F32 = jnp.float32
MESH_ID = pl.DeviceIdType.MESH
GROUP = 4
SPOTS = 8
ROWS = 128
WIDTH = 1024
VMEM_BYTES = 60 << 20


def dot(left, right, left_dim, right_dim):
    return lax.dot_general(
        left, right, (((left_dim,), (right_dim,)), ((), ())), preferred_element_type=F32
    )


class Here:
    def __init__(self):
        self.x = lax.axis_index("dp")
        at = lax.axis_index("ctx")
        self.high, self.low, self.y, self.c = at // 8, (at // 4) % 2, (at // 2) % 2, at % 2
        self.member = 2 * self.low + self.c
        self.tokens = 2 * self.high + self.y
        self.shard = 4 * self.x + self.tokens
        self.core_mate = self.place(self.x, self.high, self.low, self.y, 1 - self.c)
        self.link_mate = self.place(self.x, self.high, 1 - self.low, self.y, self.c)
        self.far_mate = self.place(self.x, self.high, 1 - self.low, self.y, 1 - self.c)
        self.core_member = 2 * self.low + (1 - self.c)
        self.link_member = 2 * (1 - self.low) + self.c
        self.far_member = 2 * (1 - self.low) + (1 - self.c)

    @staticmethod
    def place(x, high, low, y, c):
        return (x, 8 * high + 4 * low + 2 * y + c)

    def across(self, axes):
        x = 1 - self.x if "x" in axes else self.x
        y = 1 - self.y if "y" in axes else self.y
        high = 1 - self.high if "z" in axes else self.high
        return 4 * x + 2 * high + y, self.place(x, high, self.low, y, self.c)

    def plane(self, step):
        shard = lax.rem(self.shard + step, SPOTS)
        return shard, self.place(shard // 4, (shard // 2) % 2, self.low, shard % 2, self.c)

    def in_sequence(self, step):
        group = lax.rem(self.tokens + step, 4)
        return group, self.place(self.x, group // 2, self.low, group % 2, self.c)

    def mates(self):
        return (
            (self.core_member, self.core_mate),
            (self.link_member, self.link_mate),
            (self.far_member, self.far_mate),
        )


def device_of(shard, member):
    return 8 * (shard // 2) + 4 * (member // 2) + 2 * (shard % 2) + member % 2


def row_piece(held, shard, half):
    return held.at[shard, half]


def group_piece(held, shard, half):
    return held.at[shard // 2, half, shard % 2]


class Post:
    def __init__(self, send_sems, recv_sems):
        self.send_sems, self.recv_sems = send_sems, recv_sems
        self.count = 0
        self.started = []

    def send(self, src, dst, to):
        copy = pltpu.make_async_remote_copy(
            src_ref=src,
            dst_ref=dst,
            send_sem=self.send_sems.at[self.count],
            recv_sem=self.recv_sems.at[self.count],
            device_id=to,
            device_id_type=MESH_ID,
        )
        copy.start()
        self.started.append(copy)
        self.count += 1
        assert self.count <= self.send_sems.shape[0]
        return self.count - 1, to

    def arrived(self, sent, landing):
        number, to = sent
        pltpu.make_async_remote_copy(
            src_ref=landing,
            dst_ref=landing,
            send_sem=self.send_sems.at[number],
            recv_sem=self.recv_sems.at[number],
            device_id=to,
            device_id_type=MESH_ID,
        ).wait_recv()

    def finish(self):
        for copy in self.started:
            copy.wait_send()


class Local:
    def __init__(self, sems):
        self.sems = sems
        self.started = []

    def copy(self, src, dst):
        copy = pltpu.make_async_copy(src, dst, self.sems.at[len(self.started)])
        copy.start()
        self.started.append(copy)
        return copy


OTHER = {"x": "y", "y": "x"}


class CubeGather:
    def __init__(self, here, post, held, piece, own=None, corner_ways="yx"):
        self.here, self.post, self.held, self.piece, self.own = here, post, held, piece, own
        self.corner_ways = corner_ways
        self.waiting = {}

    def move(self, axes, half, way):
        here = self.here
        mine = self.piece(self.held, here.across(axes)[0], half)
        src = mine if axes or self.own is None else self.own(half)
        sent = self.post.send(src, mine, here.across(way)[1])
        axes = "".join(sorted(set(axes) ^ set(way)))
        self.waiting[axes, half] = (sent, self.piece(self.held, here.across(axes)[0], half))

    def take(self, axes, half):
        self.post.arrived(*self.waiting.pop((axes, half)))

    def start(self, ways="zxy", halves=(0, 1)):
        for way in ways:
            for half in halves:
                self.move("", half, way)

    def corners(self):
        for half, way in enumerate(self.corner_ways):
            self.take(OTHER[way], half)
            self.move(OTHER[way], half, way)

    def spread(self):
        for half in (0, 1):
            self.take("z", half)
            self.move("z", half, "x")
            self.move("z", half, "y")

    def last(self):
        for half, way in enumerate(self.corner_ways):
            self.take(OTHER[way] + "z", half)
            self.move(OTHER[way] + "z", half, way)

    def finish(self):
        for key in list(self.waiting):
            self.take(*key)


class CubeSum:
    def __init__(self, here, post, parts, piece, landing, corner_ways="yx"):
        self.here, self.post, self.parts, self.piece, self.landing = here, post, parts, piece, landing
        self.corner_ways = corner_ways
        self.waiting = {}
        self.slots = 0
        self.hops = 0

    def part(self, axes, half):
        return self.piece(self.parts, self.here.across(axes)[0], half)

    def move(self, axes, half, way):
        src = self.part(axes, half)
        came = self.waiting.pop((axes, half), [])
        if came:
            value = src[...].astype(F32)
            for sent, slot in came:
                self.post.arrived(sent, slot)
                value = value + slot[...].astype(F32)
            src = came[0][1]
            src[...] = value.astype(src.dtype)
        slot = self.landing.at[self.slots]
        self.slots += 1
        sent = self.post.send(src, slot, self.here.across(way)[1])
        axes = "".join(sorted(set(axes) ^ set(way)))
        self.waiting.setdefault((axes, half), []).append((sent, slot))

    def hop(self):
        self.hops += 1
        if self.hops == 1:
            for axes in ("xyz", "xy"):
                for half, way in enumerate(self.corner_ways):
                    self.move(axes, half, way)
            for axes in ("z", ""):
                for half, way in enumerate(self.corner_ways):
                    self.move(way + axes, half, way)
        if self.hops == 2:
            for axes in ("z", ""):
                for half, way in enumerate(self.corner_ways):
                    self.move(OTHER[way] + axes, half, OTHER[way])
        if self.hops == 3:
            self.move("z", 0, "z")
            self.move("z", 1, "z")

    def total(self):
        halves = []
        for half in (0, 1):
            value = self.part("", half)[...].astype(F32)
            for sent, slot in self.waiting.pop(("", half)):
                self.post.arrived(sent, slot)
                value = value + slot[...].astype(F32)
            halves.append(value)
        return halves


HALVES = (slice(0, 64), slice(64, 128))


class GroupGather:
    def __init__(self, here, post, held):
        self.here, self.post, self.held = here, post, held
        self.over, self.core, self.passed = [], [], []

    def put(self, half):
        mine = self.piece(self.here.member, half)
        self.over.append(self.post.send(mine, mine, self.here.link_mate))
        self.core.append(self.post.send(mine, mine, self.here.core_mate))

    def piece(self, member, half):
        return self.held.at[member, HALVES[half]]

    def near(self):
        for half in (0, 1):
            self.post.arrived(self.core[half], self.piece(self.here.core_member, half))

    def rest(self, half):
        here = self.here
        linked = self.piece(here.link_member, half)
        self.post.arrived(self.over[half], linked)
        passed = self.post.send(linked, linked, here.core_mate)
        self.post.arrived(passed, self.piece(here.far_member, half))


class GroupSum:
    def __init__(self, here, post, near_send, near_in, far_send, far_in, terms):
        self.here, self.post = here, post
        self.near_send, self.near_in = near_send, near_in
        self.far_send, self.far_in = far_send, far_in
        self.terms = terms
        self.near, self.far = {}, {}

    def give(self, slot, half, value):
        here = self.here
        self.terms[slot, :, HALVES[half]] = value.reshape(2, 64, WIDTH)
        self.near_send[slot, half] = self.terms[slot, 1 - here.c, HALVES[half]].astype(BF)
        self.near[slot, half] = self.post.send(
            self.near_send.at[slot, half], self.near_in.at[slot, half], here.core_mate
        )

    def give_all(self, slot, value):
        value = value.reshape(2, ROWS, WIDTH)
        for half in (0, 1):
            self.give(slot, half, value[:, HALVES[half]])

    def cross(self, half):
        here = self.here
        self.post.arrived(self.near[0, half], self.near_in.at[0, half])
        value = self.terms[0, here.c, HALVES[half]] + self.near_in[0, half].astype(F32)
        self.far_send[half] = value.astype(BF)
        self.far[half] = self.post.send(self.far_send.at[half], self.far_in.at[half], here.link_mate)

    def total(self, half):
        self.post.arrived(self.near[1, half], self.near_in.at[1, half])
        value = self.terms[1, self.here.c, HALVES[half]] + self.near_in[1, half].astype(F32)
        self.post.arrived(self.far[half], self.far_in.at[half])
        return value + self.far_in[half].astype(F32)


class Swap:
    def __init__(self, here, post, local, src, dst):
        self.post = post
        self.sent = []
        for step in (2, 1, 3):
            group, place = here.in_sequence(step)
            came = lax.rem(here.tokens + 4 - step, 4)
            self.sent.append((post.send(src.at[group], dst.at[here.tokens], place), dst.at[came]))
        self.own = local.copy(src.at[here.tokens], dst.at[here.tokens])

    def finish(self):
        self.own.wait()
        for sent, landing in self.sent:
            self.post.arrived(sent, landing)


def out_rows_target(here):
    return here.low, here.y, here.x, here.c, here.high


def out_rows_source(here):
    return here.low, here.c, here.x, here.high, here.y


def same_place(here, spot):
    x, high, low, y, c = spot
    return (x == here.x) & (high == here.high) & (low == here.low) & (y == here.y) & (c == here.c)


def turn_tables(rot):
    index = lax.broadcasted_iota(jnp.int32, (HD // 2, 1), 0).astype(F32)
    angle = rot * jnp.exp(index * (-math.log(10000.0) / (HD // 2)))
    return jnp.cos(angle), jnp.sin(angle)


def norm_parts(value):
    centred = value - jnp.mean(value, -1, keepdims=True)
    inv_std = lax.rsqrt(jnp.mean(centred * centred, -1, keepdims=True) + norm_eps)
    return centred * inv_std, inv_std


def norm_pull(normed, inv_std, gain, upstream):
    d_normed = upstream * gain
    return inv_std * (
        d_normed
        - jnp.mean(d_normed, -1, keepdims=True)
        - normed * jnp.mean(d_normed * normed, -1, keepdims=True)
    )


def stored_at(at):
    return 2 * (at // 8) + (at // 2) % 2, 2 * ((at // 4) % 2) + at % 2


def true_group(ref, group):
    def chunk(at, late):
        tokens, member = stored_at(at)
        tile = ref[tokens, :, ROWS * member : ROWS * (member + 1)]
        return tile[:, 64:] if late else tile[:, :64]

    if group < 8:
        return jnp.concatenate([chunk(2 * group, False), chunk(2 * group + 1, False)], 1)
    return jnp.concatenate([chunk(31 - 2 * group, True), chunk(30 - 2 * group, True)], 1)


def put_stored(ref, at, values):
    def block(number):
        tile = values[:, ROWS * (number // 2) : ROWS * (number // 2) + ROWS]
        return tile[:, 64:] if number % 2 else tile[:, :64]

    tokens, member = stored_at(at)
    ref[tokens, :, ROWS * member : ROWS * (member + 1)] = jnp.concatenate(
        [block(at), block(31 - at)], 1
    ).astype(BF)


def allowed_pairs(key_at, keys, query_at, queries, start):
    key_pos = key_at + lax.broadcasted_iota(jnp.int32, (keys, queries), 0)
    allowed = key_pos >= start
    if key_at + keys > query_at:
        allowed &= key_pos <= query_at + lax.broadcasted_iota(jnp.int32, (keys, queries), 1)
    return allowed


def attend_block(qkv, start, o_true, lse, query_at, queries, keys):
    here = slice(query_at, query_at + queries)
    query, first = qkv[0:HD, here], start[:, here]
    parts, top = [], None
    for key_at in range(0, query_at + queries, keys):
        scores = dot(qkv[HD : 2 * HD, key_at : key_at + keys], query, 0, 0)
        scores = jnp.where(
            allowed_pairs(key_at, keys, query_at, queries, first), scores, masked_value
        )
        peak = jnp.max(scores, 0, keepdims=True)
        top = peak if top is None else jnp.maximum(top, peak)
        parts.append((key_at, scores))
    total, weighted = 0.0, 0.0
    for key_at, scores in parts:
        probs = jnp.exp(scores - top)
        total = total + jnp.sum(probs, 0, keepdims=True)
        weighted = weighted + dot(qkv[2 * HD :, key_at : key_at + keys], probs.astype(BF), 1, 0)
    o_true[:, here] = weighted / total
    lse[:, here] = top + jnp.log(total)


def attend_back_block(qkv, start, o_true, lse, d_out, grads, query_at, queries):
    here = slice(query_at, query_at + queries)
    reach = slice(0, query_at + queries)
    query, d_attn = qkv[0:HD, here], d_out[:, here]
    key = qkv[HD : 2 * HD, reach]
    delta = jnp.sum(d_attn.astype(F32) * o_true[:, here], 0, keepdims=True)
    allowed = allowed_pairs(0, query_at + queries, query_at, queries, start[:, here])
    probs = jnp.where(allowed, jnp.exp(dot(key, query, 0, 0) - lse[:, here]), 0.0)
    d_probs = dot(qkv[2 * HD :, reach], d_attn, 0, 0)
    d_scores = (probs * (d_probs - delta)).astype(BF)
    grads[HD : 2 * HD, reach] += dot(query, d_scores, 1, 1)
    grads[2 * HD :, reach] += dot(d_attn, probs.astype(BF), 1, 1)
    grads[0:HD, here] = dot(key, d_scores, 1, 0) * HD**-0.5


GELU_K = math.sqrt(2.0 / math.pi)


def gelu_and_slope(pre):
    square = pre * pre
    bend = jnp.tanh(GELU_K * pre * (1.0 + 0.044715 * square))
    half = 0.5 * (1.0 + bend)
    slope = half + 0.5 * pre * (1.0 - bend * bend) * GELU_K * (1.0 + 3 * 0.044715 * square)
    return pre * half, slope


def layer_kernel(
    tok_hbm, seg_hbm, cot_hbm, wq, wk, wv, wo, wu, wd, *rest
):
    norms_hbm = rest[:8]
    act_hbm, in_grad_hbm, g_down_hbm, up_got, qkv_got, out_got, g_vec = rest[8:15]
    (
        in_grad, g_down, act,
        tok, cot, wqkv_own, wu_own, seg_in, norms_in,
        x_all, wqkv, wqkv_send, wu_send, small_in, small_all, wo_in, wo_all, wu_all, wd_all,
        vectors, starts, start, a_t, qkv_send, qkv_heads, qkv, o_true, lse, o_send, o_all,
        c_all, dm_all, dt_all, gl_all, slope_all, du_all, res,
        near_send, near_in, far_send, far_in, terms,
        do_send, do_heads, d_out, grads, d_send, d_in, d_all,
        down_parts, down_in, up_parts, up_in, out_parts, out_in, qkv_parts, qkv_in,
        vec_send, vec_in, vec_group, d_vec, up_send, qkv_end, out_end,
        send_sems, recv_sems, local_sems, self_sems,
    ) = rest[15:]
    here = Here()
    post = Post(send_sems, recv_sems)
    local = Local(local_sems)
    out_to, out_from = out_rows_target(here), out_rows_source(here)
    out_stays = same_place(here, out_to)
    out_moves = jnp.logical_not(out_stays)
    barrier = pltpu.get_barrier_semaphore()
    partners = [place for _, place in here.mates()] + [here.plane(n)[1] for n in range(1, SPOTS)]
    for place in partners:
        pl.semaphore_signal(barrier, inc=1, device_id=place, device_id_type=MESH_ID)

    @pl.when(out_moves)
    def _():
        for spot in (out_from, out_to):
            pl.semaphore_signal(
                barrier, inc=1, device_id=here.place(*spot), device_id_type=MESH_ID
            )

    loads = [
        local.copy(weight, wqkv_own.at[slot]) for slot, weight in enumerate((wq, wk, wv))
    ]
    load_wu = local.copy(wu, wu_own)
    load_seg = local.copy(seg_hbm, seg_in)
    load_norms = [local.copy(vector, norms_in.at[row]) for row, vector in enumerate(norms_hbm)]
    load_tok = local.copy(tok_hbm, tok)
    load_cot = local.copy(cot_hbm, cot)
    load_wd = [
        local.copy(wd.at[pl.ds(64 * half, 64)], wd_all.at[here.shard, half]) for half in (0, 1)
    ]

    lane = lax.broadcasted_iota(jnp.int32, (1, ROWS), 1)
    for row, load in enumerate(load_norms):
        load.wait()
        value = norms_in[row].astype(F32)
        value = jnp.concatenate([value] * GROUP, 1)
        small_in[here.member, row : row + 1] = jnp.where(lane // 32 == here.member, value, 0.0)
    load_seg.wait()
    small_in[here.member, 8:9] = seg_in[...].astype(F32)
    for load in loads:
        load.wait()
    for member in range(GROUP):
        base = 256 * member
        for part in range(3):
            wqkv_send[part, member] = wqkv_own[part, :, base : base + 256]
    def member_rows(held, member):
        at = pl.ds(pl.multiple_of(32 * (member % 2), 32), 32)
        return held.at[here.shard // 2, member // 2, here.shard % 2, at]

    for part in range(3):
        member_rows(wqkv.at[part], here.member)[...] = wqkv_send[part, here.member]
    load_tok.wait()
    x_all[here.member] = tok[...]

    @pl.when(out_stays)
    def _():
        pl.semaphore_wait(barrier, len(partners))

    @pl.when(out_moves)
    def _():
        pl.semaphore_wait(barrier, len(partners) + 2)

    small_sent, wqkv_sent, wu_sent = [], [], []
    for member, place in here.mates():
        mine = small_in.at[here.member]
        small_sent.append((post.send(mine, mine, place), small_in.at[member]))
    for part in range(3):
        for member, place in here.mates():
            mine, theirs = (member_rows(wqkv.at[part], who) for who in (here.member, member))
            wqkv_sent.append((post.send(wqkv_send.at[part, member], mine, place), theirs))
    down_ring = CubeGather(here, post, wd_all, row_piece, lambda half: wd.at[pl.ds(64 * half, 64)])
    down_ring.start("xy")
    x_gather = GroupGather(here, post, x_all)
    x_gather.put(0)
    x_gather.put(1)
    wo_copy = pltpu.make_async_remote_copy(
        src_ref=wo, dst_ref=wo_in, send_sem=self_sems.at[0], recv_sem=self_sems.at[1],
        device_id=here.place(*out_to), device_id_type=MESH_ID,
    )
    wo_keep = pltpu.make_async_copy(wo, wo_in, self_sems.at[2])
    pl.when(out_moves)(wo_copy.start)
    pl.when(out_stays)(wo_keep.start)
    load_wu.wait()
    for member in range(GROUP):
        for shard in range(SPOTS):
            at = ROWS * device_of(shard, member)
            wu_send[member, :, 128 * shard : 128 * (shard + 1)] = wu_own[:, at : at + 128]
    member_rows(wu_all, here.member)[...] = wu_send[here.member]
    for member, place in here.mates():
        mine, theirs = member_rows(wu_all, here.member), member_rows(wu_all, member)
        wu_sent.append((post.send(wu_send.at[member], mine, place), theirs))

    for sent, landing in small_sent:
        post.arrived(sent, landing)
    small_all[here.shard, 0:8] = (
        small_in[0, 0:8] + small_in[1, 0:8] + small_in[2, 0:8] + small_in[3, 0:8]
    )
    for member in range(GROUP):
        small_all[here.shard, 8 + member : 9 + member] = small_in[member, 8:9]
    plane_sent = []
    for step in range(1, SPOTS):
        _, place = here.plane(step)
        came = lax.rem(here.shard + SPOTS - step, SPOTS)
        mine = small_all.at[here.shard]
        plane_sent.append((post.send(mine, mine, place), small_all.at[came]))

    qkv_rings = []
    for part in range(3):
        for sent, landing in wqkv_sent[3 * part : 3 * part + 3]:
            post.arrived(sent, landing)
        qkv_rings.append(CubeGather(here, post, wqkv.at[part], group_piece))
        qkv_rings[part].start()
    down_ring.start("z")
    x_gather.near()
    for sent, landing in plane_sent:
        post.arrived(sent, landing)
    for block in range(SPOTS):
        first, cut = 2 * (block // 2), slice(64 * (block % 2), 64 * (block % 2) + 64)
        vectors[:, ROWS * block : ROWS * (block + 1)] = jnp.concatenate(
            [small_all[first, 0:8, cut], small_all[first + 1, 0:8, cut]], 1
        )
    gain, bias = vectors[0:1], vectors[1:2]

    def put_a(member):
        normed, _ = norm_parts(x_all[member].astype(F32))
        at = pl.ds(pl.multiple_of(ROWS * member, ROWS), ROWS)
        a_t[:, at] = (normed * gain + bias).astype(BF).T

    put_a(here.member)
    put_a(here.core_member)
    for ring in qkv_rings:
        ring.corners()
    x_gather.rest(0)
    x_gather.rest(1)

    @pl.when(out_moves)
    def _():
        wo_copy.wait_recv()
        wo_copy.wait_send()

    pl.when(out_stays)(wo_keep.wait)
    out_ring = CubeGather(here, post, wo_all, row_piece)
    wo_all[here.shard] = wo_in[...].reshape(2, 16, WIDTH)
    for ring in qkv_rings:
        ring.spread()
    out_ring.start()
    put_a(here.link_member)
    put_a(here.far_member)

    segs = jnp.concatenate([small_all[4 * here.x + group, 8:12] for group in range(4)], 0)
    begin = jnp.zeros_like(segs)
    for doc in range(1, 8):
        size = jnp.sum(
            jnp.sum((segs == doc - 1.0).astype(F32), 1, keepdims=True), 0, keepdims=True
        )
        begin = begin + jnp.where(segs >= doc, size, 0.0)
    starts[...] = begin
    rots = []
    for member in range(GROUP):
        at = 8 * here.high + 4 * (member // 2) + 2 * here.y + member % 2
        position = jnp.where(lane < 64, 64 * at + lane, 64 * (31 - at) + lane - 64)
        rots.append(position.astype(F32) - starts[pl.ds(4 * here.tokens + member, 1)])
    cos_t, sin_t = turn_tables(jnp.concatenate(rots, 1))
    for sent, landing in wu_sent:
        post.arrived(sent, landing)
    up_ring = CubeGather(here, post, wu_all, group_piece)
    for ring in qkv_rings:
        ring.last()
    swaps = []
    for part in range(3):
        qkv_rings[part].finish()
        product = dot(wqkv[part].reshape(WIDTH, 256), a_t[...], 0, 0)
        for head in range(4):
            rows = product[HD * head : HD * (head + 1)]
            if part < 2:
                first, second = rows[: HD // 2], rows[HD // 2 :]
                rows = jnp.concatenate(
                    [first * cos_t - second * sin_t, second * cos_t + first * sin_t], 0
                )
            if part == 0:
                rows = rows * HD**-0.5
            qkv_send[part, head] = rows.astype(BF)
        swaps.append(Swap(here, post, local, qkv_send.at[part], qkv_heads.at[part]))
    up_ring.start("xy")
    for group in range(16):
        a, b, cut = 2 * group, 2 * group + 1, slice(0, 64)
        if group >= 8:
            a, b, cut = 31 - a, 31 - b, slice(64, 128)
        a, b = (4 * tokens + member for tokens, member in (stored_at(a), stored_at(b)))
        start[:, ROWS * group : ROWS * (group + 1)] = jnp.concatenate(
            [starts[a : a + 1, cut], starts[b : b + 1, cut]], 1
        ).astype(jnp.int32)
    down_ring.corners()
    down_ring.spread()
    out_ring.corners()
    out_ring.spread()
    for part in range(3):
        swaps[part].finish()
        for group in range(16):
            at = slice(ROWS * group, ROWS * (group + 1))
            qkv[HD * part : HD * (part + 1), at] = true_group(qkv_heads.at[part], group)
    up_ring.corners()
    for query_at in range(0, 2048, 512):
        attend_block(qkv, start, o_true, lse, query_at, 512, 512)
    for at in range(16):
        put_stored(o_send, at, o_true)
    swap = Swap(here, post, local, o_send, o_all)
    up_ring.start("z")
    down_ring.last()
    out_ring.last()
    out_ring.finish()
    swap.finish()

    sums = [
        GroupSum(here, post, near_send.at[n], near_in.at[n], far_send.at[n], far_in.at[n], terms)
        for n in range(4)
    ]
    wo_flat = wo_all[...].reshape(256, WIDTH)

    def half_lanes(low):
        return pl.ds(pl.multiple_of(256 * low, 256), 256)

    def out_half(low):
        heads = [o_all[group, :, half_lanes(low)] for group in range(4)]
        return dot(jnp.concatenate(heads, 0), wo_flat, 0, 0)

    sums[0].give_all(0, out_half(1 - here.low))
    sums[0].give_all(1, out_half(here.low))
    sums[0].cross(0)
    sums[0].cross(1)
    up_ring.spread()
    up_ring.last()
    t_inv, h_inv = [None, None], [None, None]
    gather = GroupGather(here, post, c_all)
    for part, rows in enumerate(HALVES):
        t_normed, t_inv[part] = norm_parts(sums[0].total(part))
        hres = tok[rows].astype(F32) + t_normed * vectors[2:3] + vectors[3:4]
        res[0, rows] = t_normed
        h_normed, h_inv[part] = norm_parts(hres)
        res[1, rows] = h_normed
        res[2, rows] = hres
        c_all[here.member, rows] = (h_normed * vectors[4:5] + vectors[5:6]).astype(BF)
        gather.put(part)
    gather.near()
    up_ring.finish()
    wu_flat = wu_all[...].reshape(WIDTH, WIDTH)

    def pair(held, low, rows=slice(0, ROWS)):
        value = held[pl.ds(2 * low, 2), rows]
        return value.reshape(-1, WIDTH)

    def set_pair(held, low, rows, value):
        held[pl.ds(2 * low, 2), rows] = value.reshape(2, -1, WIDTH)

    whole = slice(0, ROWS)

    def up_rows(low, rows):
        gl, slope = gelu_and_slope(dot(pair(c_all, low, rows), wu_flat, 1, 0))
        set_pair(gl_all, low, rows, gl.astype(BF))
        set_pair(slope_all, low, rows, slope)

    up_rows(here.low, whole)
    for part, rows in enumerate(HALVES):
        gather.rest(part)
        up_rows(1 - here.low, rows)
        if part == 0:
            for load in load_wd:
                load.wait()
            down_ring.finish()
            wd_flat = wd_all[...].reshape(WIDTH, WIDTH)
        sums[1].give(0, part, dot(pair(gl_all, 1 - here.low, rows), wd_flat, 1, 0))
        sums[1].cross(part)
    sums[1].give_all(1, dot(pair(gl_all, here.low), wd_flat, 1, 0))
    load_cot.wait()
    gather = GroupGather(here, post, dm_all)
    d_gain, d_bias = 0.0, 0.0
    for part, rows in enumerate(HALVES):
        m_normed, m_inv = norm_parts(sums[1].total(part))
        upstream = cot[rows].astype(F32)
        dm_all[here.member, rows] = norm_pull(m_normed, m_inv, vectors[6:7], upstream).astype(BF)
        gather.put(part)
        act[rows] = (res[2, rows] + m_normed * vectors[6:7] + vectors[7:8]).astype(BF)
        d_gain = d_gain + jnp.sum(upstream * m_normed, 0, keepdims=True)
        d_bias = d_bias + jnp.sum(upstream, 0, keepdims=True)
    writes = [local.copy(act, act_hbm)]
    d_vec[6:7] = d_gain
    d_vec[7:8] = d_bias
    gather.near()

    def du_rows(low, rows):
        d_gl = dot(pair(dm_all, low, rows), wd_flat, 1, 1)
        set_pair(du_all, low, rows, (d_gl * pair(slope_all, low, rows)).astype(BF))

    def put_down(axes):
        shard = here.across(axes)[0]
        gl = gl_all[:, :, pl.ds(pl.multiple_of(ROWS * shard, ROWS), ROWS)].reshape(512, ROWS)
        down_parts[shard] = dot(gl, dm_flat, 0, 0).astype(BF).reshape(2, 64, WIDTH)

    down_sum = CubeSum(here, post, down_parts, row_piece, down_in)
    du_rows(here.low, whole)
    sums[2].give_all(1, dot(pair(du_all, here.low), wu_flat, 1, 1))
    for part, rows in enumerate(HALVES):
        gather.rest(part)
        if part == 1:
            dm_flat = dm_all[...].reshape(512, WIDTH)
            for axes in ("xyz", "xy", "xz", "yz", "x", "y"):
                put_down(axes)
            down_sum.hop()
        du_rows(1 - here.low, rows)
        sums[2].give(0, part, dot(pair(du_all, 1 - here.low, rows), wu_flat, 1, 1))
        if part == 0:
            sums[2].cross(part)
    sums[2].cross(1)
    for axes in ("", "z"):
        put_down(axes)
    up_sum = CubeSum(here, post, up_parts, group_piece, up_in)
    out_sum = CubeSum(here, post, out_parts, row_piece, out_in)
    qkv_sums = [
        CubeSum(here, post, qkv_parts.at[part], group_piece, qkv_in.at[part]) for part in range(3)
    ]
    du_flat = du_all[...].reshape(512, WIDTH)
    c_flat = c_all[...].reshape(512, WIDTH)
    down_sum.hop()
    for block in range(SPOTS):
        term = dot(c_flat[:, ROWS * block : ROWS * (block + 1)], du_flat, 0, 0)
        up_parts[block // 2, block % 2] = term.astype(BF).reshape(2, 64, WIDTH)
    gather = GroupGather(here, post, dt_all)
    d_mi = [0.0, 0.0]
    d_ao = [0.0, 0.0]
    for part, rows in enumerate(HALVES):
        d_c = sums[2].total(part)
        h_normed, t_normed = res[1, rows], res[0, rows]
        d_h = cot[rows].astype(F32) + norm_pull(h_normed, h_inv[part], vectors[4:5], d_c)
        dt_all[here.member, rows] = norm_pull(t_normed, t_inv[part], vectors[2:3], d_h).astype(BF)
        gather.put(part)
        res[2, rows] = d_h
        d_mi[0] = d_mi[0] + jnp.sum(d_c * h_normed, 0, keepdims=True)
        d_mi[1] = d_mi[1] + jnp.sum(d_c, 0, keepdims=True)
        d_ao[0] = d_ao[0] + jnp.sum(d_h * t_normed, 0, keepdims=True)
        d_ao[1] = d_ao[1] + jnp.sum(d_h, 0, keepdims=True)
    d_vec[4:5], d_vec[5:6] = d_mi
    d_vec[2:3], d_vec[3:4] = d_ao
    gather.near()
    gather.rest(0)
    gather.rest(1)
    dt_flat = dt_all[...].reshape(512, WIDTH)
    d_o = dot(wo_flat, dt_flat, 1, 1)
    for head in range(4):
        do_send[head] = d_o[HD * head : HD * (head + 1)].astype(BF)
    swap = Swap(here, post, local, do_send, do_heads)
    down_sum.hop()
    o_flat = o_all[...].reshape(256, 512)
    out_parts[...] = dot(o_flat, dt_flat, 1, 0).astype(BF).reshape(SPOTS, 2, 16, WIDTH)
    up_sum.hop()
    out_sum.hop()
    swap.finish()
    for group in range(16):
        d_out[:, ROWS * group : ROWS * (group + 1)] = true_group(do_heads, group)
    grads[HD:] = jnp.zeros((2 * HD, 2048), F32)
    for query_at in range(0, 2048, 256):
        attend_back_block(qkv, start, o_true, lse, d_out, grads, query_at, 256)
        if query_at == 1024:
            up_sum.hop()
        if query_at == 1536:
            out_sum.hop()
    for at in range(16):
        put_stored(d_send.at[2], at, grads[2 * HD :])
    swaps = [Swap(here, post, local, d_send.at[2], d_in.at[2])]
    position = lax.broadcasted_iota(jnp.int32, (1, 2048), 1) - start[...]
    cos_t, sin_t = turn_tables(position.astype(F32))
    for part in (1, 0):
        first = grads[HD * part : HD * part + HD // 2]
        second = grads[HD * part + HD // 2 : HD * (part + 1)]
        turned = jnp.concatenate([first * cos_t + second * sin_t, second * cos_t - first * sin_t], 0)
        for at in range(16):
            put_stored(d_send.at[part], at, turned)
        swaps.append(Swap(here, post, local, d_send.at[part], d_in.at[part]))
    low_half, high_half = down_sum.total()
    g_down[0:64] = low_half
    g_down[64:128] = high_half
    writes.append(local.copy(g_down, g_down_hbm))
    for number, part in enumerate((2, 1, 0)):
        swaps[number].finish()
        if number == 2:
            up_sum.hop()
            out_sum.hop()
        d_all[256 * part : 256 * (part + 1)] = d_in[part].reshape(256, 512)
        for block in range(SPOTS):
            term = dot(
                a_t[ROWS * block : ROWS * (block + 1)], d_all[256 * part : 256 * (part + 1)], 1, 1
            )
            qkv_parts[part, block // 2, block % 2] = term.astype(BF).reshape(2, 64, 256)
        qkv_sums[part].hop()
        if number:
            qkv_sums[part + 1].hop()
    qkv_sums[2].hop()
    wqkv_flat = [wqkv[part].reshape(WIDTH, 256) for part in range(3)]

    def in_half(low):
        terms = [
            dot(d_all[256 * part : 256 * (part + 1), half_lanes(low)], wqkv_flat[part], 0, 1)
            for part in range(3)
        ]
        return terms[0] + terms[1] + terms[2]

    sums[3].give_all(0, in_half(1 - here.low))
    sums[3].give_all(1, in_half(here.low))
    sums[3].cross(0)
    sums[3].cross(1)
    qkv_sums[0].hop()
    qkv_sums[1].hop()
    d_gain, d_bias = 0.0, 0.0
    for part, rows in enumerate(HALVES):
        d_a = sums[3].total(part)
        normed, inv_std = norm_parts(tok[rows].astype(F32))
        in_grad[rows] = res[2, rows] + norm_pull(normed, inv_std, vectors[0:1], d_a)
        d_gain = d_gain + jnp.sum(d_a * normed, 0, keepdims=True)
        d_bias = d_bias + jnp.sum(d_a, 0, keepdims=True)
    writes.append(local.copy(in_grad, in_grad_hbm))
    d_vec[0:1] = d_gain
    d_vec[1:2] = d_bias
    for shard in range(SPOTS):
        at = 256 * (shard // 2) + 64 * (shard % 2)
        vec_send[shard] = jnp.concatenate(
            [d_vec[:, at : at + 64], d_vec[:, at + ROWS : at + ROWS + 64]], 1
        )
    vec_in[here.shard] = vec_send[here.shard]
    vec_sent = []
    for step in range(1, SPOTS):
        shard, place = here.plane(step)
        came = lax.rem(here.shard + SPOTS - step, SPOTS)
        vec_sent.append((post.send(vec_send.at[shard], vec_in.at[here.shard], place), vec_in.at[came]))
    qkv_sums[0].hop()
    for sent, landing in vec_sent:
        post.arrived(sent, landing)
    total = vec_in[0]
    for shard in range(1, SPOTS):
        total = total + vec_in[shard]
    vec_group[here.member] = total
    vec_sent = []
    for member, place in here.mates():
        mine = vec_group.at[here.member]
        vec_sent.append((post.send(mine, mine, place), vec_group.at[member]))
    low_half, high_half = up_sum.total()
    for member in range(GROUP):
        halved = low_half if member < 2 else high_half
        up_send[member] = halved[32 * (member % 2) : 32 * (member % 2) + 32].astype(BF)
    up_got[here.member] = up_send[here.member]
    ends = []
    for member, place in here.mates():
        ends.append((post.send(up_send.at[member], up_got.at[here.member], place), up_got.at[member]))
    low_half, high_half = out_sum.total()
    out_end[0:16] = low_half.astype(BF)
    out_end[16:32] = high_half.astype(BF)
    out_copy = pltpu.make_async_remote_copy(
        src_ref=out_end, dst_ref=out_got, send_sem=self_sems.at[3], recv_sem=self_sems.at[4],
        device_id=here.place(*out_from), device_id_type=MESH_ID,
    )
    pl.when(out_moves)(out_copy.start)

    @pl.when(out_stays)
    def _():
        out_got[...] = out_end[...]

    for part in (2, 1, 0):
        low_half, high_half = qkv_sums[part].total()
        for member in range(GROUP):
            halved = low_half if member < 2 else high_half
            qkv_end[part, member] = halved[32 * (member % 2) : 32 * (member % 2) + 32].astype(BF)
        qkv_got[part, here.member] = qkv_end[part, here.member]
        for member, place in here.mates():
            sent = post.send(qkv_end.at[part, member], qkv_got.at[part, here.member], place)
            ends.append((sent, qkv_got.at[part, member]))
    for sent, landing in vec_sent:
        post.arrived(sent, landing)
    total = vec_group[0] + vec_group[1] + vec_group[2] + vec_group[3]
    mine = total[:, 0:32]
    for member in range(1, GROUP):
        mine = jnp.where(here.member == member, total[:, 32 * member : 32 * (member + 1)], mine)
    g_vec[...] = mine

    @pl.when(out_moves)
    def _():
        out_copy.wait_recv()
        out_copy.wait_send()

    for sent, landing in ends:
        post.arrived(sent, landing)
    for write in writes:
        write.wait()
    post.finish()


def call_layer(*args):
    vmem = pl.BlockSpec(memory_space=pltpu.VMEM)
    anywhere = pl.BlockSpec(memory_space=pl.ANY)
    shape = jax.ShapeDtypeStruct
    dma = pltpu.SemaphoreType.DMA

    def held(*dims, kind=BF):
        return pltpu.VMEM(dims, kind)

    rows = (GROUP, ROWS, WIDTH)
    return pl.pallas_call(
        layer_kernel,
        out_shape=[
            shape((ROWS, WIDTH), BF),
            shape((ROWS, WIDTH), F32),
            shape((ROWS, WIDTH), F32),
            shape((GROUP, 32, WIDTH), BF),
            shape((3, GROUP, 32, 256), BF),
            shape((32, WIDTH), BF),
            shape((8, 32), F32),
        ],
        in_specs=[anywhere] * 17,
        out_specs=[anywhere] * 3 + [vmem] * 4,
        scratch_shapes=[
            held(ROWS, WIDTH, kind=F32), held(ROWS, WIDTH, kind=F32), held(ROWS, WIDTH),
            held(ROWS, WIDTH), held(ROWS, WIDTH), held(3, 32, WIDTH), held(32, 4 * WIDTH),
            held(1, ROWS, kind=jnp.int32), held(8, 1, 32),
            held(*rows), held(3, 4, 2, 2, 64, 256), held(3, GROUP, 32, 256), held(GROUP, 32, WIDTH),
            held(GROUP, 16, ROWS, kind=F32), held(SPOTS, 16, ROWS, kind=F32),
            held(32, WIDTH), held(SPOTS, 2, 16, WIDTH), held(4, 2, 2, 64, WIDTH), held(SPOTS, 2, 64, WIDTH),
            held(8, WIDTH, kind=F32), held(16, ROWS, kind=F32), held(1, 2048, kind=jnp.int32),
            held(WIDTH, 512), held(3, 4, HD, 512), held(3, 4, HD, 512), held(192, 2048),
            held(HD, 2048, kind=F32), held(1, 2048, kind=F32), held(4, HD, 512), held(4, HD, 512),
            held(*rows), held(*rows), held(*rows), held(*rows), held(*rows, kind=F32), held(*rows),
            held(3, ROWS, WIDTH, kind=F32),
            held(4, 2, 2, 64, WIDTH), held(4, 2, 2, 64, WIDTH), held(4, 2, 64, WIDTH), held(4, 2, 64, WIDTH),
            held(2, 2, ROWS, WIDTH, kind=F32),
            held(4, HD, 512), held(4, HD, 512), held(HD, 2048), held(192, 2048, kind=F32),
            held(3, 4, HD, 512), held(3, 4, HD, 512), held(768, 512),
            held(SPOTS, 2, 64, WIDTH), held(14, 64, WIDTH),
            held(4, 2, 2, 64, WIDTH), held(14, 64, WIDTH),
            held(SPOTS, 2, 16, WIDTH), held(14, 16, WIDTH),
            held(3, 4, 2, 2, 64, 256), held(3, 14, 64, 256),
            held(SPOTS, 8, ROWS, kind=F32), held(SPOTS, 8, ROWS, kind=F32), held(GROUP, 8, ROWS, kind=F32),
            held(8, WIDTH, kind=F32), held(GROUP, 32, WIDTH), held(3, GROUP, 32, 256), held(32, WIDTH),
            dma((300,)), dma((300,)), dma((40,)), dma((5,)),
        ],
        compiler_params=pltpu.CompilerParams(
            collective_id=0, has_side_effects=True, vmem_limit_bytes=VMEM_BYTES
        ),
        name="layer",
    )(*args)


def finish_kernel(
    act_in, grad_in, down_in, up_got, qkv_got, out_got, vec,
    act, in_grad, g_q, g_k, g_v, g_out, g_up, g_down, *g_norms
):
    act[...] = act_in[...]
    in_grad[...] = grad_in[...]
    g_down[...] = down_in[...]
    g_out[...] = out_got[...].astype(F32)
    for member in range(GROUP):
        for shard in range(SPOTS):
            at = ROWS * device_of(shard, member)
            g_up[:, at : at + 128] = up_got[member, :, 128 * shard : 128 * (shard + 1)].astype(F32)
        base = 256 * member
        for slot, out in enumerate((g_q, g_k, g_v)):
            out[:, base : base + 256] = qkv_got[slot, member].astype(F32)
    for row, out in enumerate(g_norms):
        out[...] = vec[row : row + 1]


def call_finish(*args):
    vmem = pl.BlockSpec(memory_space=pltpu.VMEM)
    shape = jax.ShapeDtypeStruct
    narrow = shape((32, WIDTH), F32)
    return pl.pallas_call(
        finish_kernel,
        out_shape=[
            shape((ROWS, WIDTH), BF), shape((ROWS, WIDTH), F32), narrow, narrow, narrow, narrow,
            shape((32, 4 * WIDTH), F32), shape((ROWS, WIDTH), F32),
        ] + [shape((1, 32), F32)] * 8,
        in_specs=[vmem] * 7,
        out_specs=[vmem] * 16,
        compiler_params=pltpu.CompilerParams(vmem_limit_bytes=VMEM_BYTES),
        name="finish",
    )(*args)


def on_device_grouped(tokens, segments, cotangent, *params):
    weights, norms = params[:6], params[6:]
    results = call_layer(
        tokens[0], segments, cotangent[0], *weights, *[vector[None] for vector in norms]
    )
    outs = call_finish(*results)
    act, in_grad, *rest = outs
    return (act[None], in_grad[None], *rest[:6]) + tuple(vector[0] for vector in rest[6:])


def solution(mesh):
    in_specs = (
        P("dp", "ctx", None),
        P("dp", "ctx"),
        P("dp", "ctx", None),
        P(("dp", "ctx"), None),
        P(("dp", "ctx"), None),
        P(("dp", "ctx"), None),
        P(("dp", "ctx"), None),
        P(("dp", "ctx"), None),
        P(("dp", "ctx"), None),
        P(("dp", "ctx")),
        P(("dp", "ctx")),
        P(("dp", "ctx")),
        P(("dp", "ctx")),
        P(("dp", "ctx")),
        P(("dp", "ctx")),
        P(("dp", "ctx")),
        P(("dp", "ctx")),
    )
    out_specs = (
        P("dp", "ctx", None),
        P("dp", "ctx", None),
        P(("dp", "ctx"), None),
        P(("dp", "ctx"), None),
        P(("dp", "ctx"), None),
        P(("dp", "ctx"), None),
        P(("dp", "ctx"), None),
        P(("dp", "ctx"), None),
        P(("dp", "ctx")),
        P(("dp", "ctx")),
        P(("dp", "ctx")),
        P(("dp", "ctx")),
        P(("dp", "ctx")),
        P(("dp", "ctx")),
        P(("dp", "ctx")),
        P(("dp", "ctx")),
    )
    grouped = mesh.shape["dp"] == 2 and mesh.shape["ctx"] == 16
    return jax.shard_map(
        on_device_grouped if grouped else on_device, mesh=mesh, in_specs=in_specs, out_specs=out_specs, check_vma=False
    )
```

```python
import math

import jax
import jax.numpy as jnp
from jax import lax
from jax.experimental import pallas as pl
from jax.experimental.pallas import tpu as pltpu
from jax.sharding import PartitionSpec as P

HEADS = 16
HD = 64


norm_eps = 1e-05
masked_value = -1e30


def layer_norm(value, gain, bias):
    row_mean = jnp.mean(value, -1, keepdims=True)
    centred = value - row_mean
    scaled = centred * lax.rsqrt(jnp.mean(centred * centred, -1, keepdims=True) + norm_eps)
    return scaled * gain + bias


def norm_back(value, gain, upstream):
    row_mean = jnp.mean(value, -1, keepdims=True)
    centred = value - row_mean
    inv_std = lax.rsqrt(jnp.mean(centred * centred, -1, keepdims=True) + norm_eps)
    normed = centred * inv_std
    d_normed = upstream * gain
    d_value = inv_std * (
        d_normed
        - jnp.mean(d_normed, -1, keepdims=True)
        - normed * jnp.mean(d_normed * normed, -1, keepdims=True)
    )
    return (d_value, jnp.sum(upstream * normed, 0), jnp.sum(upstream, 0))


def rope_tables(offsets, head_dim):
    freq = 10000.0 ** (-jnp.arange(head_dim // 2, dtype=jnp.float32) / (head_dim // 2))
    angle = offsets.astype(jnp.float32)[..., None] * freq
    return (jnp.cos(angle)[..., None, :], jnp.sin(angle)[..., None, :])


def rotate(values, cos_t, sin_t):
    half_dim = values.shape[-1] // 2
    first = values[..., :half_dim]
    second = values[..., half_dim:]
    return jnp.concatenate([first * cos_t - second * sin_t, second * cos_t + first * sin_t], -1)


def unrotate(grads, cos_t, sin_t):
    half_dim = grads.shape[-1] // 2
    first = grads[..., :half_dim]
    second = grads[..., half_dim:]
    return jnp.concatenate([first * cos_t + second * sin_t, second * cos_t - first * sin_t], -1)


def true_position(flat_index, row_count, ctx_size):
    device_of = flat_index // row_count
    offset_in = flat_index % row_count
    half_rows = row_count // 2
    return jnp.where(
        offset_in < half_rows,
        device_of * half_rows + offset_in,
        (2 * ctx_size - 1 - device_of) * half_rows + offset_in - half_rows,
    )


def split_blocks(array, block_rows):
    return array.reshape((array.shape[0] // block_rows, block_rows) + array.shape[1:])


def score_block(queries, keys, query_pos, query_seg, key_pos, key_seg):
    scores = jnp.einsum(
        "qhd,khd->hqk", queries, keys, preferred_element_type=jnp.float32
    ) * queries.shape[-1] ** (-0.5)
    allowed = (query_seg[:, None] == key_seg[None, :]) & (key_pos[None, :] <= query_pos[:, None])
    return (scores, allowed[None])


def grad_block(queries, d_attn, lse, delta, keys, values, query_pos, query_seg, key_pos, key_seg):
    scores, allowed = score_block(queries, keys, query_pos, query_seg, key_pos, key_seg)
    attn_probs = jnp.where(allowed, jnp.exp(scores - lse[:, :, None]), 0.0)
    d_probs = jnp.einsum("qhd,khd->hqk", d_attn, values, preferred_element_type=jnp.float32)
    d_scores = (attn_probs * (d_probs - delta[:, :, None])).astype(jnp.bfloat16)
    return (attn_probs, d_scores)


def key_terms(
    query_rows,
    dattn_rows,
    lse_rows,
    delta_rows,
    query_pos,
    query_seg,
    key_block,
    value_block,
    key_pos,
    key_seg,
):
    attn_probs, d_scores = grad_block(
        query_rows,
        dattn_rows,
        lse_rows,
        delta_rows,
        key_block,
        value_block,
        query_pos,
        query_seg,
        key_pos,
        key_seg,
    )
    d_keys = jnp.einsum(
        "hqk,qhd->khd", d_scores, query_rows, preferred_element_type=jnp.float32
    ) * query_rows.shape[-1] ** (-0.5)
    d_values = jnp.einsum(
        "hqk,qhd->khd",
        attn_probs.astype(jnp.bfloat16),
        dattn_rows,
        preferred_element_type=jnp.float32,
    )
    return (d_keys, d_values)


def on_device(
    tokens,
    segments,
    cotangent,
    w_query,
    w_key,
    w_value,
    w_out,
    w_up,
    w_down,
    gain_attn_in,
    bias_attn_in,
    gain_attn_out,
    bias_attn_out,
    gain_mlp_in,
    bias_mlp_in,
    gain_mlp_out,
    bias_mlp_out,
):
    whole = (
        lax.all_gather(w_query, ("dp", "ctx"), axis=0, tiled=True),
        lax.all_gather(w_key, ("dp", "ctx"), axis=0, tiled=True),
        lax.all_gather(w_value, ("dp", "ctx"), axis=0, tiled=True),
        lax.all_gather(w_out, ("dp", "ctx"), axis=0, tiled=True),
        lax.all_gather(w_up, ("dp", "ctx"), axis=0, tiled=True),
        lax.all_gather(w_down, ("dp", "ctx"), axis=0, tiled=True),
        lax.all_gather(gain_attn_in, ("dp", "ctx"), axis=0, tiled=True),
        lax.all_gather(bias_attn_in, ("dp", "ctx"), axis=0, tiled=True),
        lax.all_gather(gain_attn_out, ("dp", "ctx"), axis=0, tiled=True),
        lax.all_gather(bias_attn_out, ("dp", "ctx"), axis=0, tiled=True),
        lax.all_gather(gain_mlp_in, ("dp", "ctx"), axis=0, tiled=True),
        lax.all_gather(bias_mlp_in, ("dp", "ctx"), axis=0, tiled=True),
        lax.all_gather(gain_mlp_out, ("dp", "ctx"), axis=0, tiled=True),
        lax.all_gather(bias_mlp_out, ("dp", "ctx"), axis=0, tiled=True),
    )
    query_w, key_w, value_w, out_w, up_w, down_w = whole[:6]
    gain_ai, bias_ai, gain_ao, bias_ao, gain_mi, bias_mi, gain_mo, bias_mo = [
        entry.astype(jnp.float32) for entry in whole[6:]
    ]
    row_count = tokens.shape[1]
    model_width = tokens.shape[2]
    ctx_size = lax.axis_size("ctx")
    seq_length = row_count * ctx_size
    score_scale = HD ** (-0.5)
    seg_all = lax.all_gather(segments, "ctx", axis=1, tiled=True)[0]
    my_seg = segments[0]
    all_pos = true_position(jnp.arange(seq_length, dtype=jnp.int32), row_count, ctx_size)
    my_pos = true_position(
        lax.axis_index("ctx") * row_count + jnp.arange(row_count, dtype=jnp.int32),
        row_count,
        ctx_size,
    )
    doc_first = jnp.min(
        jnp.where(seg_all[None, :] == my_seg[:, None], all_pos[None, :], seq_length), axis=1
    )
    cos_t, sin_t = rope_tables(my_pos - doc_first, HD)
    inputs = tokens[0].astype(jnp.float32)
    attn_in = layer_norm(inputs, gain_ai, bias_ai).astype(jnp.bfloat16)
    query_pre = jnp.dot(attn_in, query_w, preferred_element_type=jnp.float32).reshape(
        row_count, HEADS, HD
    )
    key_pre = jnp.dot(attn_in, key_w, preferred_element_type=jnp.float32).reshape(
        row_count, HEADS, HD
    )
    queries = rotate(query_pre, cos_t, sin_t).astype(jnp.bfloat16)
    keys_rot = rotate(key_pre, cos_t, sin_t).astype(jnp.bfloat16)
    values_flat = jnp.dot(attn_in, value_w, preferred_element_type=jnp.float32).astype(jnp.bfloat16)
    values_heads = values_flat.reshape(row_count, HEADS, HD)
    keys_flat = keys_rot.reshape(row_count, model_width)
    start_state = (
        jnp.full((HEADS, row_count), masked_value, jnp.float32),
        jnp.zeros((HEADS, row_count), jnp.float32),
        jnp.zeros((row_count, HEADS, HD), jnp.float32),
    )
    key_rows = lax.all_gather(keys_flat, "ctx", axis=0, tiled=True)
    value_rows = lax.all_gather(values_flat, "ctx", axis=0, tiled=True)
    span = key_rows.shape[0]
    block_rows = math.gcd(span, 1024)
    key_pos = true_position(jnp.arange(span, dtype=jnp.int32), row_count, ctx_size)
    key_seg = seg_all

    def visit(state_now, parts):
        row_top, row_total, weighted = state_now
        key_block = parts[0].reshape(block_rows, HEADS, HD)
        value_block = parts[1].reshape(block_rows, HEADS, HD)
        scores, allowed = score_block(queries, key_block, my_pos, my_seg, parts[2], parts[3])
        top_new = jnp.maximum(row_top, jnp.max(jnp.where(allowed, scores, masked_value), -1))
        fade = jnp.exp(row_top - top_new)
        attn_probs = jnp.where(allowed, jnp.exp(scores - top_new[:, :, None]), 0.0)
        row_total = row_total * fade + jnp.sum(attn_probs, -1)
        weighted = weighted * fade.T[:, :, None] + jnp.einsum(
            "hqk,khd->qhd",
            attn_probs.astype(jnp.bfloat16),
            value_block,
            preferred_element_type=jnp.float32,
        )
        return ((top_new, row_total, weighted), None)

    blocks = (
        split_blocks(key_rows, block_rows),
        split_blocks(value_rows, block_rows),
        split_blocks(key_pos, block_rows),
        split_blocks(key_seg, block_rows),
    )
    row_top, row_total, weighted = lax.scan(visit, start_state, blocks)[0]
    lse = row_top + jnp.log(row_total)
    attn_f = weighted / row_total.T[:, :, None]
    attn_b = attn_f.reshape(row_count, model_width).astype(jnp.bfloat16)
    branch = jnp.dot(attn_b, out_w, preferred_element_type=jnp.float32)
    resid = inputs + layer_norm(branch, gain_ao, bias_ao)
    mlp_in = layer_norm(resid, gain_mi, bias_mi).astype(jnp.bfloat16)
    hidden_pre = jnp.dot(mlp_in, up_w, preferred_element_type=jnp.float32)
    hidden = jax.nn.gelu(hidden_pre, approximate=True).astype(jnp.bfloat16)
    mlp_out = jnp.dot(hidden, down_w, preferred_element_type=jnp.float32)
    result = resid + layer_norm(mlp_out, gain_mo, bias_mo)
    upstream = cotangent[0].astype(jnp.float32)
    d_mlp_out, dgain_mo, dbias_mo = norm_back(mlp_out, gain_mo, upstream)
    d_mlp_b = d_mlp_out.astype(jnp.bfloat16)
    grad_down = jnp.dot(hidden.T, d_mlp_b, preferred_element_type=jnp.float32)
    d_hidden = jnp.dot(d_mlp_b, down_w.T, preferred_element_type=jnp.float32)
    gelu_back = jax.vjp(lambda pre: jax.nn.gelu(pre, approximate=True), hidden_pre)[1]
    d_pre = gelu_back(d_hidden)[0].astype(jnp.bfloat16)
    grad_up = jnp.dot(mlp_in.T, d_pre, preferred_element_type=jnp.float32)
    d_mlp_in = jnp.dot(d_pre, up_w.T, preferred_element_type=jnp.float32)
    d_resid_n, dgain_mi, dbias_mi = norm_back(resid, gain_mi, d_mlp_in)
    d_resid = upstream + d_resid_n
    d_branch, dgain_ao, dbias_ao = norm_back(branch, gain_ao, d_resid)
    d_branch_b = d_branch.astype(jnp.bfloat16)
    grad_out = jnp.dot(attn_b.T, d_branch_b, preferred_element_type=jnp.float32)
    d_attn_flat = jnp.dot(d_branch_b, out_w.T, preferred_element_type=jnp.float32).astype(
        jnp.bfloat16
    )
    d_attn = d_attn_flat.reshape(row_count, HEADS, HD)
    delta = jnp.sum(d_attn.astype(jnp.float32) * attn_f, -1).T
    zero_heads = jnp.zeros((row_count, HEADS, HD), jnp.float32)

    def query_grad(dq_now, key_rows, value_rows, key_pos, key_seg):
        block_rows = math.gcd(key_rows.shape[0], 1024)

        def visit(dq_run, parts):
            key_block = parts[0].reshape(block_rows, HEADS, HD)
            value_block = parts[1].reshape(block_rows, HEADS, HD)
            d_scores = grad_block(
                queries,
                d_attn,
                lse,
                delta,
                key_block,
                value_block,
                my_pos,
                my_seg,
                parts[2],
                parts[3],
            )[1]
            return (
                dq_run
                + jnp.einsum(
                    "hqk,khd->qhd", d_scores, key_block, preferred_element_type=jnp.float32
                )
                * score_scale,
                None,
            )

        blocks = (
            split_blocks(key_rows, block_rows),
            split_blocks(value_rows, block_rows),
            split_blocks(key_pos, block_rows),
            split_blocks(key_seg, block_rows),
        )
        return lax.scan(visit, dq_now, blocks)[0]

    lse_all, delta_all = (
        lax.all_gather(lse.T, "ctx", axis=0, tiled=True),
        lax.all_gather(delta.T, "ctx", axis=0, tiled=True),
    )
    query_rows = lax.all_gather(queries.reshape(row_count, model_width), "ctx", axis=0, tiled=True)
    dattn_rows = lax.all_gather(d_attn_flat, "ctx", axis=0, tiled=True)
    span = query_rows.shape[0]
    query_block_rows = math.gcd(span, 1024)
    query_pos = true_position(jnp.arange(span, dtype=jnp.int32), row_count, ctx_size)

    def visit(sums, parts):
        d_keys, d_values = key_terms(
            parts[0].reshape(query_block_rows, HEADS, HD),
            parts[1].reshape(query_block_rows, HEADS, HD),
            parts[2].T,
            parts[3].T,
            parts[4],
            parts[5],
            keys_rot,
            values_heads,
            my_pos,
            my_seg,
        )
        return ((sums[0] + d_keys, sums[1] + d_values), None)

    blocks = (
        split_blocks(query_rows, query_block_rows),
        split_blocks(dattn_rows, query_block_rows),
        split_blocks(lse_all, query_block_rows),
        split_blocks(delta_all, query_block_rows),
        split_blocks(query_pos, query_block_rows),
        split_blocks(seg_all, query_block_rows),
    )
    dk_rot, dv_sum = lax.scan(visit, (zero_heads, zero_heads), blocks)[0]
    pieces = (
        lax.all_gather(keys_flat, "ctx", axis=0, tiled=True),
        lax.all_gather(values_flat, "ctx", axis=0, tiled=True),
    )
    span = pieces[0].shape[0]
    key_pos = true_position(jnp.arange(span, dtype=jnp.int32), row_count, ctx_size)
    key_seg = seg_all
    dq_rot = query_grad(zero_heads, pieces[0], pieces[1], key_pos, key_seg)
    d_query = unrotate(dq_rot, cos_t, sin_t).reshape(row_count, model_width).astype(jnp.bfloat16)
    d_key = unrotate(dk_rot, cos_t, sin_t).reshape(row_count, model_width).astype(jnp.bfloat16)
    d_value = dv_sum.reshape(row_count, model_width).astype(jnp.bfloat16)
    grad_query = jnp.dot(attn_in.T, d_query, preferred_element_type=jnp.float32)
    grad_key = jnp.dot(attn_in.T, d_key, preferred_element_type=jnp.float32)
    grad_value = jnp.dot(attn_in.T, d_value, preferred_element_type=jnp.float32)
    d_attn_in = (
        jnp.dot(d_query, query_w.T, preferred_element_type=jnp.float32)
        + jnp.dot(d_key, key_w.T, preferred_element_type=jnp.float32)
        + jnp.dot(d_value, value_w.T, preferred_element_type=jnp.float32)
    )
    d_inputs_n, dgain_ai, dbias_ai = norm_back(inputs, gain_ai, d_attn_in)
    input_grad = (d_resid + d_inputs_n)[None]
    shares = (
        lax.psum_scatter(grad_query, ("dp", "ctx"), scatter_dimension=0, tiled=True),
        lax.psum_scatter(grad_key, ("dp", "ctx"), scatter_dimension=0, tiled=True),
        lax.psum_scatter(grad_value, ("dp", "ctx"), scatter_dimension=0, tiled=True),
        lax.psum_scatter(grad_out, ("dp", "ctx"), scatter_dimension=0, tiled=True),
        lax.psum_scatter(grad_up, ("dp", "ctx"), scatter_dimension=0, tiled=True),
        lax.psum_scatter(grad_down, ("dp", "ctx"), scatter_dimension=0, tiled=True),
        lax.psum_scatter(dgain_ai, ("dp", "ctx"), scatter_dimension=0, tiled=True),
        lax.psum_scatter(dbias_ai, ("dp", "ctx"), scatter_dimension=0, tiled=True),
        lax.psum_scatter(dgain_ao, ("dp", "ctx"), scatter_dimension=0, tiled=True),
        lax.psum_scatter(dbias_ao, ("dp", "ctx"), scatter_dimension=0, tiled=True),
        lax.psum_scatter(dgain_mi, ("dp", "ctx"), scatter_dimension=0, tiled=True),
        lax.psum_scatter(dbias_mi, ("dp", "ctx"), scatter_dimension=0, tiled=True),
        lax.psum_scatter(dgain_mo, ("dp", "ctx"), scatter_dimension=0, tiled=True),
        lax.psum_scatter(dbias_mo, ("dp", "ctx"), scatter_dimension=0, tiled=True),
    )
    return (result.astype(jnp.bfloat16)[None], input_grad) + tuple(shares)


BF = jnp.bfloat16
F32 = jnp.float32
MESH_ID = pl.DeviceIdType.MESH
GROUP = 4
SPOTS = 8
ROWS = 128
WIDTH = 1024
VMEM_BYTES = 60 << 20


def dot(left, right, left_dim, right_dim):
    return lax.dot_general(
        left, right, (((left_dim,), (right_dim,)), ((), ())), preferred_element_type=F32
    )


class Here:
    def __init__(self):
        self.x = lax.axis_index("dp")
        at = lax.axis_index("ctx")
        self.high, self.low, self.y, self.c = at // 8, (at // 4) % 2, (at // 2) % 2, at % 2
        self.member = 2 * self.low + self.c
        self.tokens = 2 * self.high + self.y
        self.shard = 4 * self.x + self.tokens
        self.core_mate = self.place(self.x, self.high, self.low, self.y, 1 - self.c)
        self.link_mate = self.place(self.x, self.high, 1 - self.low, self.y, self.c)
        self.far_mate = self.place(self.x, self.high, 1 - self.low, self.y, 1 - self.c)
        self.core_member = 2 * self.low + (1 - self.c)
        self.link_member = 2 * (1 - self.low) + self.c
        self.far_member = 2 * (1 - self.low) + (1 - self.c)

    @staticmethod
    def place(x, high, low, y, c):
        return (x, 8 * high + 4 * low + 2 * y + c)

    def across(self, axes):
        x = 1 - self.x if "x" in axes else self.x
        y = 1 - self.y if "y" in axes else self.y
        high = 1 - self.high if "z" in axes else self.high
        return 4 * x + 2 * high + y, self.place(x, high, self.low, y, self.c)

    def plane(self, step):
        shard = lax.rem(self.shard + step, SPOTS)
        return shard, self.place(shard // 4, (shard // 2) % 2, self.low, shard % 2, self.c)

    def in_sequence(self, step):
        group = lax.rem(self.tokens + step, 4)
        return group, self.place(self.x, group // 2, self.low, group % 2, self.c)

    def mates(self):
        return (
            (self.core_member, self.core_mate),
            (self.link_member, self.link_mate),
            (self.far_member, self.far_mate),
        )


def device_of(shard, member):
    return 8 * (shard // 2) + 4 * (member // 2) + 2 * (shard % 2) + member % 2


def row_piece(held, shard, half):
    return held.at[shard, half]


def group_piece(held, shard, half):
    return held.at[shard // 2, half, shard % 2]


class Post:
    def __init__(self, send_sems, recv_sems):
        self.send_sems, self.recv_sems = send_sems, recv_sems
        self.count = 0
        self.started = []

    def send(self, src, dst, to):
        copy = pltpu.make_async_remote_copy(
            src_ref=src,
            dst_ref=dst,
            send_sem=self.send_sems.at[self.count],
            recv_sem=self.recv_sems.at[self.count],
            device_id=to,
            device_id_type=MESH_ID,
        )
        copy.start()
        self.started.append(copy)
        self.count += 1
        assert self.count <= self.send_sems.shape[0]
        return self.count - 1, to

    def arrived(self, sent, landing):
        number, to = sent
        pltpu.make_async_remote_copy(
            src_ref=landing,
            dst_ref=landing,
            send_sem=self.send_sems.at[number],
            recv_sem=self.recv_sems.at[number],
            device_id=to,
            device_id_type=MESH_ID,
        ).wait_recv()

    def finish(self):
        for copy in self.started:
            copy.wait_send()


class Local:
    def __init__(self, sems):
        self.sems = sems
        self.started = []

    def copy(self, src, dst):
        copy = pltpu.make_async_copy(src, dst, self.sems.at[len(self.started)])
        copy.start()
        self.started.append(copy)
        return copy


OTHER = {"x": "y", "y": "x"}


class CubeGather:
    def __init__(self, here, post, held, piece, own=None, corner_ways="yx"):
        self.here, self.post, self.held, self.piece, self.own = here, post, held, piece, own
        self.corner_ways = corner_ways
        self.waiting = {}

    def move(self, axes, half, way):
        here = self.here
        mine = self.piece(self.held, here.across(axes)[0], half)
        src = mine if axes or self.own is None else self.own(half)
        sent = self.post.send(src, mine, here.across(way)[1])
        axes = "".join(sorted(set(axes) ^ set(way)))
        self.waiting[axes, half] = (sent, self.piece(self.held, here.across(axes)[0], half))

    def take(self, axes, half):
        self.post.arrived(*self.waiting.pop((axes, half)))

    def start(self, ways="zxy", halves=(0, 1)):
        for way in ways:
            for half in halves:
                self.move("", half, way)

    def corners(self):
        for half, way in enumerate(self.corner_ways):
            self.take(OTHER[way], half)
            self.move(OTHER[way], half, way)

    def spread(self):
        for half in (0, 1):
            self.take("z", half)
            self.move("z", half, "x")
            self.move("z", half, "y")

    def last(self):
        for half, way in enumerate(self.corner_ways):
            self.take(OTHER[way] + "z", half)
            self.move(OTHER[way] + "z", half, way)

    def finish(self):
        for key in list(self.waiting):
            self.take(*key)


class CubeSum:
    def __init__(self, here, post, parts, piece, landing, corner_ways="yx"):
        self.here, self.post, self.parts, self.piece, self.landing = here, post, parts, piece, landing
        self.corner_ways = corner_ways
        self.waiting = {}
        self.slots = 0
        self.hops = 0

    def part(self, axes, half):
        return self.piece(self.parts, self.here.across(axes)[0], half)

    def move(self, axes, half, way):
        src = self.part(axes, half)
        came = self.waiting.pop((axes, half), [])
        if came:
            value = src[...].astype(F32)
            for sent, slot in came:
                self.post.arrived(sent, slot)
                value = value + slot[...].astype(F32)
            src = came[0][1]
            src[...] = value.astype(src.dtype)
        slot = self.landing.at[self.slots]
        self.slots += 1
        sent = self.post.send(src, slot, self.here.across(way)[1])
        axes = "".join(sorted(set(axes) ^ set(way)))
        self.waiting.setdefault((axes, half), []).append((sent, slot))

    def hop(self):
        self.hops += 1
        if self.hops == 1:
            for axes in ("xyz", "xy"):
                for half, way in enumerate(self.corner_ways):
                    self.move(axes, half, way)
            for axes in ("z", ""):
                for half, way in enumerate(self.corner_ways):
                    self.move(way + axes, half, way)
        if self.hops == 2:
            for axes in ("z", ""):
                for half, way in enumerate(self.corner_ways):
                    self.move(OTHER[way] + axes, half, OTHER[way])
        if self.hops == 3:
            self.move("z", 0, "z")
            self.move("z", 1, "z")

    def total(self):
        halves = []
        for half in (0, 1):
            value = self.part("", half)[...].astype(F32)
            for sent, slot in self.waiting.pop(("", half)):
                self.post.arrived(sent, slot)
                value = value + slot[...].astype(F32)
            halves.append(value)
        return halves


HALVES = (slice(0, 64), slice(64, 128))


class GroupGather:
    def __init__(self, here, post, held):
        self.here, self.post, self.held = here, post, held
        self.over, self.core, self.passed = [], [], []

    def put(self, half):
        mine = self.piece(self.here.member, half)
        self.over.append(self.post.send(mine, mine, self.here.link_mate))
        self.core.append(self.post.send(mine, mine, self.here.core_mate))

    def piece(self, member, half):
        return self.held.at[member, HALVES[half]]

    def near(self):
        for half in (0, 1):
            self.post.arrived(self.core[half], self.piece(self.here.core_member, half))

    def rest(self, half):
        here = self.here
        linked = self.piece(here.link_member, half)
        self.post.arrived(self.over[half], linked)
        passed = self.post.send(linked, linked, here.core_mate)
        self.post.arrived(passed, self.piece(here.far_member, half))


class GroupSum:
    def __init__(self, here, post, near_send, near_in, far_send, far_in, terms):
        self.here, self.post = here, post
        self.near_send, self.near_in = near_send, near_in
        self.far_send, self.far_in = far_send, far_in
        self.terms = terms
        self.near, self.far = {}, {}

    def give(self, slot, half, value):
        here = self.here
        self.terms[slot, :, HALVES[half]] = value.reshape(2, 64, WIDTH)
        self.near_send[slot, half] = self.terms[slot, 1 - here.c, HALVES[half]].astype(BF)
        self.near[slot, half] = self.post.send(
            self.near_send.at[slot, half], self.near_in.at[slot, half], here.core_mate
        )

    def give_all(self, slot, value):
        value = value.reshape(2, ROWS, WIDTH)
        for half in (0, 1):
            self.give(slot, half, value[:, HALVES[half]])

    def cross(self, half):
        here = self.here
        self.post.arrived(self.near[0, half], self.near_in.at[0, half])
        value = self.terms[0, here.c, HALVES[half]] + self.near_in[0, half].astype(F32)
        self.far_send[half] = value.astype(BF)
        self.far[half] = self.post.send(self.far_send.at[half], self.far_in.at[half], here.link_mate)

    def total(self, half):
        self.post.arrived(self.near[1, half], self.near_in.at[1, half])
        value = self.terms[1, self.here.c, HALVES[half]] + self.near_in[1, half].astype(F32)
        self.post.arrived(self.far[half], self.far_in.at[half])
        return value + self.far_in[half].astype(F32)


class Swap:
    def __init__(self, here, post, local, src, dst):
        self.post = post
        self.sent = []
        for step in (2, 1, 3):
            group, place = here.in_sequence(step)
            came = lax.rem(here.tokens + 4 - step, 4)
            self.sent.append((post.send(src.at[group], dst.at[here.tokens], place), dst.at[came]))
        self.own = local.copy(src.at[here.tokens], dst.at[here.tokens])

    def finish(self):
        self.own.wait()
        for sent, landing in self.sent:
            self.post.arrived(sent, landing)


def out_rows_target(here):
    return here.low, here.y, here.x, here.c, here.high


def out_rows_source(here):
    return here.low, here.c, here.x, here.high, here.y


def same_place(here, spot):
    x, high, low, y, c = spot
    return (x == here.x) & (high == here.high) & (low == here.low) & (y == here.y) & (c == here.c)


def turn_tables(rot):
    index = lax.broadcasted_iota(jnp.int32, (HD // 2, 1), 0).astype(F32)
    angle = rot * jnp.exp(index * (-math.log(10000.0) / (HD // 2)))
    return jnp.cos(angle), jnp.sin(angle)


def norm_parts(value):
    centred = value - jnp.mean(value, -1, keepdims=True)
    inv_std = lax.rsqrt(jnp.mean(centred * centred, -1, keepdims=True) + norm_eps)
    return centred * inv_std, inv_std


def norm_pull(normed, inv_std, gain, upstream):
    d_normed = upstream * gain
    return inv_std * (
        d_normed
        - jnp.mean(d_normed, -1, keepdims=True)
        - normed * jnp.mean(d_normed * normed, -1, keepdims=True)
    )


def stored_at(at):
    return 2 * (at // 8) + (at // 2) % 2, 2 * ((at // 4) % 2) + at % 2


def true_group(ref, group):
    def chunk(at, late):
        tokens, member = stored_at(at)
        tile = ref[tokens, :, ROWS * member : ROWS * (member + 1)]
        return tile[:, 64:] if late else tile[:, :64]

    if group < 8:
        return jnp.concatenate([chunk(2 * group, False), chunk(2 * group + 1, False)], 1)
    return jnp.concatenate([chunk(31 - 2 * group, True), chunk(30 - 2 * group, True)], 1)


def put_stored(ref, at, values):
    def block(number):
        tile = values[:, ROWS * (number // 2) : ROWS * (number // 2) + ROWS]
        return tile[:, 64:] if number % 2 else tile[:, :64]

    tokens, member = stored_at(at)
    ref[tokens, :, ROWS * member : ROWS * (member + 1)] = jnp.concatenate(
        [block(at), block(31 - at)], 1
    ).astype(BF)


def allowed_pairs(key_at, keys, query_at, queries, start):
    key_pos = key_at + lax.broadcasted_iota(jnp.int32, (keys, queries), 0)
    allowed = key_pos >= start
    if key_at + keys > query_at:
        allowed &= key_pos <= query_at + lax.broadcasted_iota(jnp.int32, (keys, queries), 1)
    return allowed


def attend_block(qkv, start, o_true, lse, query_at, queries, keys):
    here = slice(query_at, query_at + queries)
    query, first = qkv[0:HD, here], start[:, here]
    parts, top = [], None
    for key_at in range(0, query_at + queries, keys):
        scores = dot(qkv[HD : 2 * HD, key_at : key_at + keys], query, 0, 0)
        scores = jnp.where(
            allowed_pairs(key_at, keys, query_at, queries, first), scores, masked_value
        )
        peak = jnp.max(scores, 0, keepdims=True)
        top = peak if top is None else jnp.maximum(top, peak)
        parts.append((key_at, scores))
    total, weighted = 0.0, 0.0
    for key_at, scores in parts:
        probs = jnp.exp(scores - top)
        total = total + jnp.sum(probs, 0, keepdims=True)
        weighted = weighted + dot(qkv[2 * HD :, key_at : key_at + keys], probs.astype(BF), 1, 0)
    o_true[:, here] = weighted / total
    lse[:, here] = top + jnp.log(total)


def attend_back_block(qkv, start, o_true, lse, d_out, grads, query_at, queries):
    here = slice(query_at, query_at + queries)
    reach = slice(0, query_at + queries)
    query, d_attn = qkv[0:HD, here], d_out[:, here]
    key = qkv[HD : 2 * HD, reach]
    delta = jnp.sum(d_attn.astype(F32) * o_true[:, here], 0, keepdims=True)
    allowed = allowed_pairs(0, query_at + queries, query_at, queries, start[:, here])
    probs = jnp.where(allowed, jnp.exp(dot(key, query, 0, 0) - lse[:, here]), 0.0)
    d_probs = dot(qkv[2 * HD :, reach], d_attn, 0, 0)
    d_scores = (probs * (d_probs - delta)).astype(BF)
    grads[HD : 2 * HD, reach] += dot(query, d_scores, 1, 1)
    grads[2 * HD :, reach] += dot(d_attn, probs.astype(BF), 1, 1)
    grads[0:HD, here] = dot(key, d_scores, 1, 0) * HD**-0.5


GELU_K = math.sqrt(2.0 / math.pi)


def gelu_and_slope(pre):
    square = pre * pre
    bend = jnp.tanh(GELU_K * pre * (1.0 + 0.044715 * square))
    half = 0.5 * (1.0 + bend)
    slope = half + 0.5 * pre * (1.0 - bend * bend) * GELU_K * (1.0 + 3 * 0.044715 * square)
    return pre * half, slope


def layer_kernel(
    tok_hbm, seg_hbm, cot_hbm, wq, wk, wv, wo, wu, wd, *rest
):
    norms_hbm = rest[:8]
    act_hbm, in_grad_hbm, g_down_hbm, up_got, qkv_got, out_got, g_vec = rest[8:15]
    (
        in_grad, g_down, act,
        tok, cot, wqkv_own, wu_own, seg_in, norms_in,
        x_all, wqkv, wqkv_send, wu_send, small_in, small_all, wo_in, wo_all, wu_all, wd_all,
        vectors, starts, start, a_t, qkv_send, qkv_heads, qkv, o_true, lse, o_send, o_all,
        c_all, dm_all, dt_all, gl_all, slope_all, du_all, res,
        near_send, near_in, far_send, far_in, terms,
        do_send, do_heads, d_out, grads, d_send, d_in, d_all,
        down_parts, down_in, up_parts, up_in, out_parts, out_in, qkv_parts, qkv_in,
        vec_send, vec_in, vec_group, d_vec, up_send, qkv_end, out_end,
        send_sems, recv_sems, local_sems, self_sems,
    ) = rest[15:]
    here = Here()
    post = Post(send_sems, recv_sems)
    local = Local(local_sems)
    out_to, out_from = out_rows_target(here), out_rows_source(here)
    out_stays = same_place(here, out_to)
    out_moves = jnp.logical_not(out_stays)
    barrier = pltpu.get_barrier_semaphore()
    partners = [place for _, place in here.mates()] + [here.plane(n)[1] for n in range(1, SPOTS)]
    for place in partners:
        pl.semaphore_signal(barrier, inc=1, device_id=place, device_id_type=MESH_ID)

    @pl.when(out_moves)
    def _():
        for spot in (out_from, out_to):
            pl.semaphore_signal(
                barrier, inc=1, device_id=here.place(*spot), device_id_type=MESH_ID
            )

    loads = [
        local.copy(weight, wqkv_own.at[slot]) for slot, weight in enumerate((wq, wk, wv))
    ]
    load_wu = local.copy(wu, wu_own)
    load_seg = local.copy(seg_hbm, seg_in)
    load_norms = [local.copy(vector, norms_in.at[row]) for row, vector in enumerate(norms_hbm)]
    load_tok = local.copy(tok_hbm, tok)
    load_cot = local.copy(cot_hbm, cot)
    load_wd = [
        local.copy(wd.at[pl.ds(64 * half, 64)], wd_all.at[here.shard, half]) for half in (0, 1)
    ]

    lane = lax.broadcasted_iota(jnp.int32, (1, ROWS), 1)
    for row, load in enumerate(load_norms):
        load.wait()
        value = norms_in[row].astype(F32)
        value = jnp.concatenate([value] * GROUP, 1)
        small_in[here.member, row : row + 1] = jnp.where(lane // 32 == here.member, value, 0.0)
    load_seg.wait()
    small_in[here.member, 8:9] = seg_in[...].astype(F32)
    for load in loads:
        load.wait()
    for member in range(GROUP):
        base = 256 * member
        for part in range(3):
            wqkv_send[part, member] = wqkv_own[part, :, base : base + 256]
    def member_rows(held, member):
        at = pl.ds(pl.multiple_of(32 * (member % 2), 32), 32)
        return held.at[here.shard // 2, member // 2, here.shard % 2, at]

    for part in range(3):
        member_rows(wqkv.at[part], here.member)[...] = wqkv_send[part, here.member]
    load_tok.wait()
    x_all[here.member] = tok[...]

    @pl.when(out_stays)
    def _():
        pl.semaphore_wait(barrier, len(partners))

    @pl.when(out_moves)
    def _():
        pl.semaphore_wait(barrier, len(partners) + 2)

    small_sent, wqkv_sent, wu_sent = [], [], []
    for member, place in here.mates():
        mine = small_in.at[here.member]
        small_sent.append((post.send(mine, mine, place), small_in.at[member]))
    for part in range(3):
        for member, place in here.mates():
            mine, theirs = (member_rows(wqkv.at[part], who) for who in (here.member, member))
            wqkv_sent.append((post.send(wqkv_send.at[part, member], mine, place), theirs))
    down_ring = CubeGather(here, post, wd_all, row_piece, lambda half: wd.at[pl.ds(64 * half, 64)])
    down_ring.start("xy")
    x_gather = GroupGather(here, post, x_all)
    x_gather.put(0)
    x_gather.put(1)
    wo_copy = pltpu.make_async_remote_copy(
        src_ref=wo, dst_ref=wo_in, send_sem=self_sems.at[0], recv_sem=self_sems.at[1],
        device_id=here.place(*out_to), device_id_type=MESH_ID,
    )
    wo_keep = pltpu.make_async_copy(wo, wo_in, self_sems.at[2])
    pl.when(out_moves)(wo_copy.start)
    pl.when(out_stays)(wo_keep.start)
    load_wu.wait()
    for member in range(GROUP):
        for shard in range(SPOTS):
            at = ROWS * device_of(shard, member)
            wu_send[member, :, 128 * shard : 128 * (shard + 1)] = wu_own[:, at : at + 128]
    member_rows(wu_all, here.member)[...] = wu_send[here.member]
    for member, place in here.mates():
        mine, theirs = member_rows(wu_all, here.member), member_rows(wu_all, member)
        wu_sent.append((post.send(wu_send.at[member], mine, place), theirs))

    for sent, landing in small_sent:
        post.arrived(sent, landing)
    small_all[here.shard, 0:8] = (
        small_in[0, 0:8] + small_in[1, 0:8] + small_in[2, 0:8] + small_in[3, 0:8]
    )
    for member in range(GROUP):
        small_all[here.shard, 8 + member : 9 + member] = small_in[member, 8:9]
    plane_sent = []
    for step in range(1, SPOTS):
        _, place = here.plane(step)
        came = lax.rem(here.shard + SPOTS - step, SPOTS)
        mine = small_all.at[here.shard]
        plane_sent.append((post.send(mine, mine, place), small_all.at[came]))

    qkv_rings = []
    for part in range(3):
        for sent, landing in wqkv_sent[3 * part : 3 * part + 3]:
            post.arrived(sent, landing)
        qkv_rings.append(CubeGather(here, post, wqkv.at[part], group_piece))
        qkv_rings[part].start()
    down_ring.start("z")
    x_gather.near()
    for sent, landing in plane_sent:
        post.arrived(sent, landing)
    for block in range(SPOTS):
        first, cut = 2 * (block // 2), slice(64 * (block % 2), 64 * (block % 2) + 64)
        vectors[:, ROWS * block : ROWS * (block + 1)] = jnp.concatenate(
            [small_all[first, 0:8, cut], small_all[first + 1, 0:8, cut]], 1
        )
    gain, bias = vectors[0:1], vectors[1:2]

    def put_a(member):
        normed, _ = norm_parts(x_all[member].astype(F32))
        at = pl.ds(pl.multiple_of(ROWS * member, ROWS), ROWS)
        a_t[:, at] = (normed * gain + bias).astype(BF).T

    put_a(here.member)
    put_a(here.core_member)
    for ring in qkv_rings:
        ring.corners()
    x_gather.rest(0)
    x_gather.rest(1)

    @pl.when(out_moves)
    def _():
        wo_copy.wait_recv()
        wo_copy.wait_send()

    pl.when(out_stays)(wo_keep.wait)
    out_ring = CubeGather(here, post, wo_all, row_piece)
    wo_all[here.shard] = wo_in[...].reshape(2, 16, WIDTH)
    for ring in qkv_rings:
        ring.spread()
    out_ring.start()
    put_a(here.link_member)
    put_a(here.far_member)

    segs = jnp.concatenate([small_all[4 * here.x + group, 8:12] for group in range(4)], 0)
    begin = jnp.zeros_like(segs)
    for doc in range(1, 8):
        size = jnp.sum(
            jnp.sum((segs == doc - 1.0).astype(F32), 1, keepdims=True), 0, keepdims=True
        )
        begin = begin + jnp.where(segs >= doc, size, 0.0)
    starts[...] = begin
    rots = []
    for member in range(GROUP):
        at = 8 * here.high + 4 * (member // 2) + 2 * here.y + member % 2
        position = jnp.where(lane < 64, 64 * at + lane, 64 * (31 - at) + lane - 64)
        rots.append(position.astype(F32) - starts[pl.ds(4 * here.tokens + member, 1)])
    cos_t, sin_t = turn_tables(jnp.concatenate(rots, 1))
    for sent, landing in wu_sent:
        post.arrived(sent, landing)
    up_ring = CubeGather(here, post, wu_all, group_piece)
    for ring in qkv_rings:
        ring.last()
    up_ring.start("x")
    swaps = []
    for part in range(3):
        qkv_rings[part].finish()
        product = dot(wqkv[part].reshape(WIDTH, 256), a_t[...], 0, 0)
        for head in range(4):
            rows = product[HD * head : HD * (head + 1)]
            if part < 2:
                first, second = rows[: HD // 2], rows[HD // 2 :]
                rows = jnp.concatenate(
                    [first * cos_t - second * sin_t, second * cos_t + first * sin_t], 0
                )
            if part == 0:
                rows = rows * HD**-0.5
            qkv_send[part, head] = rows.astype(BF)
        swaps.append(Swap(here, post, local, qkv_send.at[part], qkv_heads.at[part]))
    up_ring.start("y")
    for group in range(16):
        a, b, cut = 2 * group, 2 * group + 1, slice(0, 64)
        if group >= 8:
            a, b, cut = 31 - a, 31 - b, slice(64, 128)
        a, b = (4 * tokens + member for tokens, member in (stored_at(a), stored_at(b)))
        start[:, ROWS * group : ROWS * (group + 1)] = jnp.concatenate(
            [starts[a : a + 1, cut], starts[b : b + 1, cut]], 1
        ).astype(jnp.int32)
    down_ring.corners()
    down_ring.spread()
    out_ring.corners()
    out_ring.spread()
    for part in range(3):
        swaps[part].finish()
        for group in range(16):
            at = slice(ROWS * group, ROWS * (group + 1))
            qkv[HD * part : HD * (part + 1), at] = true_group(qkv_heads.at[part], group)
    up_ring.corners()
    for query_at in range(0, 2048, 512):
        attend_block(qkv, start, o_true, lse, query_at, 512, 512)
    for at in range(16):
        put_stored(o_send, at, o_true)
    swap = Swap(here, post, local, o_send, o_all)
    up_ring.start("z")
    down_ring.last()
    out_ring.last()
    out_ring.finish()
    swap.finish()

    sums = [
        GroupSum(here, post, near_send.at[n], near_in.at[n], far_send.at[n], far_in.at[n], terms)
        for n in range(4)
    ]
    wo_flat = wo_all[...].reshape(256, WIDTH)

    def half_lanes(low):
        return pl.ds(pl.multiple_of(256 * low, 256), 256)

    def out_half(low):
        heads = [o_all[group, :, half_lanes(low)] for group in range(4)]
        return dot(jnp.concatenate(heads, 0), wo_flat, 0, 0)

    sums[0].give_all(0, out_half(1 - here.low))
    sums[0].give_all(1, out_half(here.low))
    sums[0].cross(0)
    sums[0].cross(1)
    up_ring.spread()
    up_ring.last()
    t_inv, h_inv = [None, None], [None, None]
    gather = GroupGather(here, post, c_all)
    for part, rows in enumerate(HALVES):
        t_normed, t_inv[part] = norm_parts(sums[0].total(part))
        hres = tok[rows].astype(F32) + t_normed * vectors[2:3] + vectors[3:4]
        res[0, rows] = t_normed
        h_normed, h_inv[part] = norm_parts(hres)
        res[1, rows] = h_normed
        res[2, rows] = hres
        c_all[here.member, rows] = (h_normed * vectors[4:5] + vectors[5:6]).astype(BF)
        gather.put(part)
    gather.near()
    up_ring.finish()
    wu_flat = wu_all[...].reshape(WIDTH, WIDTH)

    def pair(held, low, rows=slice(0, ROWS)):
        value = held[pl.ds(2 * low, 2), rows]
        return value.reshape(-1, WIDTH)

    def set_pair(held, low, rows, value):
        held[pl.ds(2 * low, 2), rows] = value.reshape(2, -1, WIDTH)

    whole = slice(0, ROWS)

    def up_rows(low, rows):
        gl, slope = gelu_and_slope(dot(pair(c_all, low, rows), wu_flat, 1, 0))
        set_pair(gl_all, low, rows, gl.astype(BF))
        set_pair(slope_all, low, rows, slope)

    up_rows(here.low, whole)
    for part, rows in enumerate(HALVES):
        gather.rest(part)
        up_rows(1 - here.low, rows)
        if part == 0:
            for load in load_wd:
                load.wait()
            down_ring.finish()
            wd_flat = wd_all[...].reshape(WIDTH, WIDTH)
        sums[1].give(0, part, dot(pair(gl_all, 1 - here.low, rows), wd_flat, 1, 0))
        sums[1].cross(part)
    sums[1].give_all(1, dot(pair(gl_all, here.low), wd_flat, 1, 0))
    load_cot.wait()
    gather = GroupGather(here, post, dm_all)
    d_gain, d_bias = 0.0, 0.0
    for part, rows in enumerate(HALVES):
        m_normed, m_inv = norm_parts(sums[1].total(part))
        upstream = cot[rows].astype(F32)
        dm_all[here.member, rows] = norm_pull(m_normed, m_inv, vectors[6:7], upstream).astype(BF)
        gather.put(part)
        act[rows] = (res[2, rows] + m_normed * vectors[6:7] + vectors[7:8]).astype(BF)
        d_gain = d_gain + jnp.sum(upstream * m_normed, 0, keepdims=True)
        d_bias = d_bias + jnp.sum(upstream, 0, keepdims=True)
    writes = [local.copy(act, act_hbm)]
    d_vec[6:7] = d_gain
    d_vec[7:8] = d_bias
    gather.near()

    def du_rows(low, rows):
        d_gl = dot(pair(dm_all, low, rows), wd_flat, 1, 1)
        set_pair(du_all, low, rows, (d_gl * pair(slope_all, low, rows)).astype(BF))

    def put_down(axes):
        shard = here.across(axes)[0]
        gl = gl_all[:, :, pl.ds(pl.multiple_of(ROWS * shard, ROWS), ROWS)].reshape(512, ROWS)
        down_parts[shard] = dot(gl, dm_flat, 0, 0).astype(BF).reshape(2, 64, WIDTH)

    down_sum = CubeSum(here, post, down_parts, row_piece, down_in)
    du_rows(here.low, whole)
    sums[2].give_all(1, dot(pair(du_all, here.low), wu_flat, 1, 1))
    for part, rows in enumerate(HALVES):
        gather.rest(part)
        if part == 1:
            dm_flat = dm_all[...].reshape(512, WIDTH)
            for axes in ("xyz", "xy", "xz", "yz", "x", "y"):
                put_down(axes)
            down_sum.hop()
        du_rows(1 - here.low, rows)
        sums[2].give(0, part, dot(pair(du_all, 1 - here.low, rows), wu_flat, 1, 1))
        if part == 0:
            sums[2].cross(part)
    sums[2].cross(1)
    for axes in ("", "z"):
        put_down(axes)
    up_sum = CubeSum(here, post, up_parts, group_piece, up_in)
    out_sum = CubeSum(here, post, out_parts, row_piece, out_in)
    qkv_sums = [
        CubeSum(here, post, qkv_parts.at[part], group_piece, qkv_in.at[part]) for part in range(3)
    ]
    du_flat = du_all[...].reshape(512, WIDTH)
    c_flat = c_all[...].reshape(512, WIDTH)
    down_sum.hop()
    for block in range(SPOTS):
        term = dot(c_flat[:, ROWS * block : ROWS * (block + 1)], du_flat, 0, 0)
        up_parts[block // 2, block % 2] = term.astype(BF).reshape(2, 64, WIDTH)
    gather = GroupGather(here, post, dt_all)
    d_mi = [0.0, 0.0]
    d_ao = [0.0, 0.0]
    for part, rows in enumerate(HALVES):
        d_c = sums[2].total(part)
        h_normed, t_normed = res[1, rows], res[0, rows]
        d_h = cot[rows].astype(F32) + norm_pull(h_normed, h_inv[part], vectors[4:5], d_c)
        dt_all[here.member, rows] = norm_pull(t_normed, t_inv[part], vectors[2:3], d_h).astype(BF)
        gather.put(part)
        res[2, rows] = d_h
        d_mi[0] = d_mi[0] + jnp.sum(d_c * h_normed, 0, keepdims=True)
        d_mi[1] = d_mi[1] + jnp.sum(d_c, 0, keepdims=True)
        d_ao[0] = d_ao[0] + jnp.sum(d_h * t_normed, 0, keepdims=True)
        d_ao[1] = d_ao[1] + jnp.sum(d_h, 0, keepdims=True)
    d_vec[4:5], d_vec[5:6] = d_mi
    d_vec[2:3], d_vec[3:4] = d_ao
    gather.near()
    gather.rest(0)
    gather.rest(1)
    dt_flat = dt_all[...].reshape(512, WIDTH)
    d_o = dot(wo_flat, dt_flat, 1, 1)
    for head in range(4):
        do_send[head] = d_o[HD * head : HD * (head + 1)].astype(BF)
    swap = Swap(here, post, local, do_send, do_heads)
    down_sum.hop()
    o_flat = o_all[...].reshape(256, 512)
    out_parts[...] = dot(o_flat, dt_flat, 1, 0).astype(BF).reshape(SPOTS, 2, 16, WIDTH)
    up_sum.hop()
    out_sum.hop()
    swap.finish()
    for group in range(16):
        d_out[:, ROWS * group : ROWS * (group + 1)] = true_group(do_heads, group)
    grads[HD:] = jnp.zeros((2 * HD, 2048), F32)
    for query_at in range(0, 2048, 256):
        attend_back_block(qkv, start, o_true, lse, d_out, grads, query_at, 256)
        if query_at == 1024:
            up_sum.hop()
        if query_at == 1536:
            out_sum.hop()
    for at in range(16):
        put_stored(d_send.at[2], at, grads[2 * HD :])
    swaps = [Swap(here, post, local, d_send.at[2], d_in.at[2])]
    position = lax.broadcasted_iota(jnp.int32, (1, 2048), 1) - start[...]
    cos_t, sin_t = turn_tables(position.astype(F32))
    for part in (1, 0):
        first = grads[HD * part : HD * part + HD // 2]
        second = grads[HD * part + HD // 2 : HD * (part + 1)]
        turned = jnp.concatenate([first * cos_t + second * sin_t, second * cos_t - first * sin_t], 0)
        for at in range(16):
            put_stored(d_send.at[part], at, turned)
        swaps.append(Swap(here, post, local, d_send.at[part], d_in.at[part]))
    low_half, high_half = down_sum.total()
    g_down[0:64] = low_half
    g_down[64:128] = high_half
    writes.append(local.copy(g_down, g_down_hbm))
    for number, part in enumerate((2, 1, 0)):
        swaps[number].finish()
        if number == 2:
            up_sum.hop()
            out_sum.hop()
        d_all[256 * part : 256 * (part + 1)] = d_in[part].reshape(256, 512)
        for block in range(SPOTS):
            term = dot(
                a_t[ROWS * block : ROWS * (block + 1)], d_all[256 * part : 256 * (part + 1)], 1, 1
            )
            qkv_parts[part, block // 2, block % 2] = term.astype(BF).reshape(2, 64, 256)
        qkv_sums[part].hop()
        if number:
            qkv_sums[part + 1].hop()
    qkv_sums[2].hop()
    wqkv_flat = [wqkv[part].reshape(WIDTH, 256) for part in range(3)]

    def in_half(low):
        terms = [
            dot(d_all[256 * part : 256 * (part + 1), half_lanes(low)], wqkv_flat[part], 0, 1)
            for part in range(3)
        ]
        return terms[0] + terms[1] + terms[2]

    sums[3].give_all(0, in_half(1 - here.low))
    sums[3].give_all(1, in_half(here.low))
    sums[3].cross(0)
    sums[3].cross(1)
    qkv_sums[0].hop()
    qkv_sums[1].hop()
    d_gain, d_bias = 0.0, 0.0
    for part, rows in enumerate(HALVES):
        d_a = sums[3].total(part)
        normed, inv_std = norm_parts(tok[rows].astype(F32))
        in_grad[rows] = res[2, rows] + norm_pull(normed, inv_std, vectors[0:1], d_a)
        d_gain = d_gain + jnp.sum(d_a * normed, 0, keepdims=True)
        d_bias = d_bias + jnp.sum(d_a, 0, keepdims=True)
    writes.append(local.copy(in_grad, in_grad_hbm))
    d_vec[0:1] = d_gain
    d_vec[1:2] = d_bias
    for shard in range(SPOTS):
        at = 256 * (shard // 2) + 64 * (shard % 2)
        vec_send[shard] = jnp.concatenate(
            [d_vec[:, at : at + 64], d_vec[:, at + ROWS : at + ROWS + 64]], 1
        )
    vec_in[here.shard] = vec_send[here.shard]
    vec_sent = []
    for step in range(1, SPOTS):
        shard, place = here.plane(step)
        came = lax.rem(here.shard + SPOTS - step, SPOTS)
        vec_sent.append((post.send(vec_send.at[shard], vec_in.at[here.shard], place), vec_in.at[came]))
    qkv_sums[0].hop()
    for sent, landing in vec_sent:
        post.arrived(sent, landing)
    total = vec_in[0]
    for shard in range(1, SPOTS):
        total = total + vec_in[shard]
    vec_group[here.member] = total
    vec_sent = []
    for member, place in here.mates():
        mine = vec_group.at[here.member]
        vec_sent.append((post.send(mine, mine, place), vec_group.at[member]))
    low_half, high_half = up_sum.total()
    for member in range(GROUP):
        halved = low_half if member < 2 else high_half
        up_send[member] = halved[32 * (member % 2) : 32 * (member % 2) + 32].astype(BF)
    up_got[here.member] = up_send[here.member]
    ends = []
    for member, place in here.mates():
        ends.append((post.send(up_send.at[member], up_got.at[here.member], place), up_got.at[member]))
    low_half, high_half = out_sum.total()
    out_end[0:16] = low_half.astype(BF)
    out_end[16:32] = high_half.astype(BF)
    out_copy = pltpu.make_async_remote_copy(
        src_ref=out_end, dst_ref=out_got, send_sem=self_sems.at[3], recv_sem=self_sems.at[4],
        device_id=here.place(*out_from), device_id_type=MESH_ID,
    )
    pl.when(out_moves)(out_copy.start)

    @pl.when(out_stays)
    def _():
        out_got[...] = out_end[...]

    for part in (2, 1, 0):
        low_half, high_half = qkv_sums[part].total()
        for member in range(GROUP):
            halved = low_half if member < 2 else high_half
            qkv_end[part, member] = halved[32 * (member % 2) : 32 * (member % 2) + 32].astype(BF)
        qkv_got[part, here.member] = qkv_end[part, here.member]
        for member, place in here.mates():
            sent = post.send(qkv_end.at[part, member], qkv_got.at[part, here.member], place)
            ends.append((sent, qkv_got.at[part, member]))
    for sent, landing in vec_sent:
        post.arrived(sent, landing)
    total = vec_group[0] + vec_group[1] + vec_group[2] + vec_group[3]
    mine = total[:, 0:32]
    for member in range(1, GROUP):
        mine = jnp.where(here.member == member, total[:, 32 * member : 32 * (member + 1)], mine)
    g_vec[...] = mine

    @pl.when(out_moves)
    def _():
        out_copy.wait_recv()
        out_copy.wait_send()

    for sent, landing in ends:
        post.arrived(sent, landing)
    for write in writes:
        write.wait()
    post.finish()


def call_layer(*args):
    vmem = pl.BlockSpec(memory_space=pltpu.VMEM)
    anywhere = pl.BlockSpec(memory_space=pl.ANY)
    shape = jax.ShapeDtypeStruct
    dma = pltpu.SemaphoreType.DMA

    def held(*dims, kind=BF):
        return pltpu.VMEM(dims, kind)

    rows = (GROUP, ROWS, WIDTH)
    return pl.pallas_call(
        layer_kernel,
        out_shape=[
            shape((ROWS, WIDTH), BF),
            shape((ROWS, WIDTH), F32),
            shape((ROWS, WIDTH), F32),
            shape((GROUP, 32, WIDTH), BF),
            shape((3, GROUP, 32, 256), BF),
            shape((32, WIDTH), BF),
            shape((8, 32), F32),
        ],
        in_specs=[anywhere] * 17,
        out_specs=[anywhere] * 3 + [vmem] * 4,
        scratch_shapes=[
            held(ROWS, WIDTH, kind=F32), held(ROWS, WIDTH, kind=F32), held(ROWS, WIDTH),
            held(ROWS, WIDTH), held(ROWS, WIDTH), held(3, 32, WIDTH), held(32, 4 * WIDTH),
            held(1, ROWS, kind=jnp.int32), held(8, 1, 32),
            held(*rows), held(3, 4, 2, 2, 64, 256), held(3, GROUP, 32, 256), held(GROUP, 32, WIDTH),
            held(GROUP, 16, ROWS, kind=F32), held(SPOTS, 16, ROWS, kind=F32),
            held(32, WIDTH), held(SPOTS, 2, 16, WIDTH), held(4, 2, 2, 64, WIDTH), held(SPOTS, 2, 64, WIDTH),
            held(8, WIDTH, kind=F32), held(16, ROWS, kind=F32), held(1, 2048, kind=jnp.int32),
            held(WIDTH, 512), held(3, 4, HD, 512), held(3, 4, HD, 512), held(192, 2048),
            held(HD, 2048, kind=F32), held(1, 2048, kind=F32), held(4, HD, 512), held(4, HD, 512),
            held(*rows), held(*rows), held(*rows), held(*rows), held(*rows, kind=F32), held(*rows),
            held(3, ROWS, WIDTH, kind=F32),
            held(4, 2, 2, 64, WIDTH), held(4, 2, 2, 64, WIDTH), held(4, 2, 64, WIDTH), held(4, 2, 64, WIDTH),
            held(2, 2, ROWS, WIDTH, kind=F32),
            held(4, HD, 512), held(4, HD, 512), held(HD, 2048), held(192, 2048, kind=F32),
            held(3, 4, HD, 512), held(3, 4, HD, 512), held(768, 512),
            held(SPOTS, 2, 64, WIDTH), held(14, 64, WIDTH),
            held(4, 2, 2, 64, WIDTH), held(14, 64, WIDTH),
            held(SPOTS, 2, 16, WIDTH), held(14, 16, WIDTH),
            held(3, 4, 2, 2, 64, 256), held(3, 14, 64, 256),
            held(SPOTS, 8, ROWS, kind=F32), held(SPOTS, 8, ROWS, kind=F32), held(GROUP, 8, ROWS, kind=F32),
            held(8, WIDTH, kind=F32), held(GROUP, 32, WIDTH), held(3, GROUP, 32, 256), held(32, WIDTH),
            dma((300,)), dma((300,)), dma((40,)), dma((5,)),
        ],
        compiler_params=pltpu.CompilerParams(
            collective_id=0, has_side_effects=True, vmem_limit_bytes=VMEM_BYTES
        ),
        name="layer",
    )(*args)


def finish_kernel(
    act_in, grad_in, down_in, up_got, qkv_got, out_got, vec,
    act, in_grad, g_q, g_k, g_v, g_out, g_up, g_down, *rest
):
    g_norms, (held_grad, held_down, held_act), local = rest[:8], rest[8:11], Local(rest[11])
    stages = ((grad_in, held_grad, in_grad), (down_in, held_down, g_down), (act_in, held_act, act))
    loads = [local.copy(src, held) for src, held, _ in stages]
    stores = []
    for load, (_, held, dst) in zip(loads, stages):
        load.wait()
        stores.append(local.copy(held, dst))
    g_out[...] = out_got[...].astype(F32)
    for member in range(GROUP):
        for shard in range(SPOTS):
            at = ROWS * device_of(shard, member)
            g_up[:, at : at + 128] = up_got[member, :, 128 * shard : 128 * (shard + 1)].astype(F32)
        base = 256 * member
        for slot, out in enumerate((g_q, g_k, g_v)):
            out[:, base : base + 256] = qkv_got[slot, member].astype(F32)
    for row, out in enumerate(g_norms):
        out[...] = vec[row : row + 1]
    for store in stores:
        store.wait()


def call_finish(*args):
    vmem = pl.BlockSpec(memory_space=pltpu.VMEM)
    anywhere = pl.BlockSpec(memory_space=pl.ANY)
    shape = jax.ShapeDtypeStruct
    narrow = shape((32, WIDTH), F32)
    return pl.pallas_call(
        finish_kernel,
        out_shape=[
            shape((ROWS, WIDTH), BF), shape((ROWS, WIDTH), F32), narrow, narrow, narrow, narrow,
            shape((32, 4 * WIDTH), F32), shape((ROWS, WIDTH), F32),
        ] + [shape((1, 32), F32)] * 8,
        in_specs=[anywhere] * 3 + [vmem] * 4,
        out_specs=[anywhere] * 2 + [vmem] * 5 + [anywhere] + [vmem] * 8,
        scratch_shapes=[
            pltpu.VMEM((ROWS, WIDTH), F32), pltpu.VMEM((ROWS, WIDTH), F32), pltpu.VMEM((ROWS, WIDTH), BF),
            pltpu.SemaphoreType.DMA((6,)),
        ],
        compiler_params=pltpu.CompilerParams(vmem_limit_bytes=VMEM_BYTES),
        name="finish",
    )(*args)


def on_device_grouped(tokens, segments, cotangent, *params):
    weights, norms = params[:6], params[6:]
    results = call_layer(
        tokens[0], segments, cotangent[0], *weights, *[vector[None] for vector in norms]
    )
    outs = call_finish(*results)
    act, in_grad, *rest = outs
    return (act[None], in_grad[None], *rest[:6]) + tuple(vector[0] for vector in rest[6:])


def solution(mesh):
    in_specs = (
        P("dp", "ctx", None),
        P("dp", "ctx"),
        P("dp", "ctx", None),
        P(("dp", "ctx"), None),
        P(("dp", "ctx"), None),
        P(("dp", "ctx"), None),
        P(("dp", "ctx"), None),
        P(("dp", "ctx"), None),
        P(("dp", "ctx"), None),
        P(("dp", "ctx")),
        P(("dp", "ctx")),
        P(("dp", "ctx")),
        P(("dp", "ctx")),
        P(("dp", "ctx")),
        P(("dp", "ctx")),
        P(("dp", "ctx")),
        P(("dp", "ctx")),
    )
    out_specs = (
        P("dp", "ctx", None),
        P("dp", "ctx", None),
        P(("dp", "ctx"), None),
        P(("dp", "ctx"), None),
        P(("dp", "ctx"), None),
        P(("dp", "ctx"), None),
        P(("dp", "ctx"), None),
        P(("dp", "ctx"), None),
        P(("dp", "ctx")),
        P(("dp", "ctx")),
        P(("dp", "ctx")),
        P(("dp", "ctx")),
        P(("dp", "ctx")),
        P(("dp", "ctx")),
        P(("dp", "ctx")),
        P(("dp", "ctx")),
    )
    grouped = mesh.shape["dp"] == 2 and mesh.shape["ctx"] == 16
    return jax.shard_map(
        on_device_grouped if grouped else on_device, mesh=mesh, in_specs=in_specs, out_specs=out_specs, check_vma=False
    )
```
